32 devices in a mesh: seq: 4 (over z), batch: 8 (over y, x, core).
Axes of the slice: x: 2, y: 2, z: 4, core: 2. Of those that a mesh axis runs over, the one named last changes fastest.
Arguments:
- tokens: bfloat16 [8, 1024, 1024], P('batch', 'seq'), may hold values from -6 to 6
- cotangent: bfloat16 [8, 1024, 1024], P('batch', 'seq'), may hold values from -6 to 6
- group_ids: int32 [8], P('batch'), may hold values from 0 to 3
- loss_weight: float32 [4], replicated, may hold values from 0.5 to 2
- gain_attn: bfloat16 [1024], replicated, may hold values from 0.5 to 1.5
- w_query: bfloat16 [1024, 1024], P(('seq', 'batch')), may hold values from -0.1875 to 0.1875
- w_latent: bfloat16 [1024, 512], P(('seq', 'batch')), may hold values from -0.1875 to 0.1875
- w_key_up: bfloat16 [2, 256, 512], replicated, may hold values from -0.375 to 0.375
- w_value_up: bfloat16 [2, 256, 512], replicated, may hold values from -0.375 to 0.375
- w_out: bfloat16 [1024, 1024], P(None, ('seq', 'batch')), may hold values from -0.75 to 0.75
- gain_mlp: bfloat16 [1024], replicated, may hold values from 0.5 to 1.5
- w_gate: bfloat16 [1024, 2816], P(('seq', 'batch')), may hold values from -0.1875 to 0.1875
- w_up: bfloat16 [1024, 2816], P(('seq', 'batch')), may hold values from -0.1875 to 0.1875
- w_down: bfloat16 [2816, 1024], P(('seq', 'batch')), may hold values from -0.109375 to 0.109375
Outputs:
- output: bfloat16 [8, 1024, 1024], P('batch', 'seq')
- input_grad: bfloat16 [8, 1024, 1024], P('batch', 'seq')
- grad_gain_attn: float32 [1024], replicated
- grad_w_query: float32 [1024, 1024], P(('seq', 'batch'))
- grad_w_latent: float32 [1024, 512], P(('seq', 'batch'))
- grad_w_key_up: float32 [2, 256, 512], replicated
- grad_w_value_up: float32 [2, 256, 512], replicated
- grad_w_out: float32 [1024, 1024], P(None, ('seq', 'batch'))
- grad_gain_mlp: float32 [1024], replicated
- grad_w_gate: float32 [1024, 2816], P(('seq', 'batch'))
- grad_w_up: float32 [1024, 2816], P(('seq', 'batch'))
- grad_w_down: float32 [2816, 1024], P(('seq', 'batch'))
The draws below stay inside these ranges and needn't reach their ends.
All inputs are finite; a program needn't handle non-finite values.
Results may differ from the reference program's by a relative error of at most 0.02.
Values may be sent and summed in bfloat16 or wider, within the bound.
No kernel may reach another device: no remote copies, remote signals or barrier semaphores. Data moves between devices by JAX's collectives and lax.ppermute only.
A program may use at most 256 MiB of HBM per device.

```python
import math
import jax
import jax.numpy as jnp
from jax import lax

D = 1024
HEADS = 16
HEAD_DIM = 64
LATENT = 256
KV_GROUPS = 2
FF = 2816
GROUPS = 4
LEN = 1024
SEQS = 8


def place_ends(values, stream_key, smallest, largest):
    place = [jax.random.randint(jax.random.fold_in(stream_key, axis), (), 0, length) for axis, length in enumerate(values.shape)]
    widest = values.shape.index(max(values.shape))
    neighbour = place[:widest] + [(place[widest] + 1) % values.shape[widest]] + place[widest + 1:]
    return values.at[tuple(place)].set(smallest).at[tuple(neighbour)].set(largest)


def shard_levels(rng, dims, cuts, smallest, largest):
    factor_of = 1.0
    for position, shards_of in cuts:
        heights = jax.random.uniform(jax.random.fold_in(jax.random.fold_in(rng, 6), position), (shards_of,), jnp.float32, smallest / len(cuts), largest / len(cuts))
        factor_of = factor_of * jnp.repeat(jnp.exp(heights), dims[position] // shards_of).reshape((-1,) + (1,) * (len(dims) - 1 - position))
    return factor_of


def centred(key, extent, deviation, reach, shards=(), kind=jnp.bfloat16):
    array = deviation * jax.random.normal(key, extent, jnp.float32)
    if shards:
        array = array * shard_levels(key, extent, shards, -0.22, 0.18)
    return jnp.clip(array, -reach, reach).astype(kind)


def setup_inputs(seed: int = 0) -> dict:
    seeds = jax.random.split(jax.random.key(seed), 15)
    tokens = centred(seeds[0], (SEQS, LEN, D), 1.0, 6.0, ((0, 8), (1, 4)))
    cotangent = centred(seeds[1], (SEQS, LEN, D), 1.0, 6.0, ((0, 8), (1, 4)))
    group_ids = place_ends(jax.random.randint(seeds[2], (SEQS,), 0, GROUPS), jax.random.fold_in(seeds[2], 1), 0, GROUPS - 1).astype(jnp.int32)
    loss_weight = jnp.clip(jnp.exp(jax.random.uniform(seeds[3], (GROUPS,), jnp.float32, math.log(0.5), math.log(2.0))), 0.5, 2.0)
    gain_attn = jnp.clip(1.0 + 0.1 * jax.random.normal(seeds[4], (D,), jnp.float32), 0.5, 1.5).astype(jnp.bfloat16)
    w_query = centred(seeds[5], (D, HEADS * HEAD_DIM), D ** -0.5, 0.1875, ((0, 32),))
    w_latent = centred(seeds[6], (D, KV_GROUPS * LATENT), D ** -0.5, 0.1875, ((0, 32),))
    w_key_up = centred(seeds[7], (KV_GROUPS, LATENT, HEADS // KV_GROUPS * HEAD_DIM), LATENT ** -0.5, 0.375)
    w_value_up = centred(seeds[8], (KV_GROUPS, LATENT, HEADS // KV_GROUPS * HEAD_DIM), LATENT ** -0.5, 0.375)
    w_out = centred(seeds[9], (HEADS * HEAD_DIM, D), (HEADS * HEAD_DIM // 16) ** -0.5, 0.75, ((1, 32),))
    gain_mlp = jnp.clip(1.0 + 0.1 * jax.random.normal(seeds[10], (D,), jnp.float32), 0.5, 1.5).astype(jnp.bfloat16)
    w_gate = centred(seeds[11], (D, FF), D ** -0.5, 0.1875, ((0, 32),))
    w_up = centred(seeds[12], (D, FF), D ** -0.5, 0.1875, ((0, 32),))
    w_down = centred(seeds[13], (FF, D), FF ** -0.5, 0.109375, ((0, 32),))
    return {"tokens": tokens, "cotangent": cotangent, "group_ids": group_ids, "loss_weight": loss_weight, "gain_attn": gain_attn, "w_query": w_query, "w_latent": w_latent, "w_key_up": w_key_up, "w_value_up": w_value_up, "w_out": w_out, "gain_mlp": gain_mlp, "w_gate": w_gate, "w_up": w_up, "w_down": w_down}


@jax.custom_vjp
def low(v):
    return lax.optimization_barrier(v.astype(jnp.bfloat16)).astype(jnp.float32)

@jax.custom_vjp
def low_back(v):
    return v

def low_keep(v):
    return (low(v), None)

def low_pass(kept, grad):
    return (grad,)

def back_keep(v):
    return (v, None)

def back_low(kept, grad):
    return (low(grad),)
low.defvjp(low_keep, low_pass)
low_back.defvjp(back_keep, back_low)
EPSILON = 1e-06
HIGHEST = lax.Precision.HIGHEST

def layer(inputs, gain_one, query_w, latent_w, key_up, value_up, out_w, gain_two, gate_w, up_w, down_w):
    length = inputs.shape[0]
    scale = HEAD_DIM ** (-0.5)
    inv_one = lax.rsqrt(lax.optimization_barrier(jnp.mean(inputs * inputs, axis=-1, keepdims=True)) + EPSILON)
    normed_one = low(inputs * inv_one * gain_one)
    queries = low(low_back(jnp.dot(normed_one, query_w, precision=HIGHEST)))
    latent = low(low_back(jnp.dot(normed_one, latent_w, precision=HIGHEST)))
    latent_grouped = latent.reshape(length, KV_GROUPS, LATENT)
    key_all = low(jnp.einsum('lgr,grn->lgn', latent_grouped, key_up, precision=HIGHEST))
    value_all = low(jnp.einsum('lgr,grn->lgn', latent_grouped, value_up, precision=HIGHEST))
    query_heads = queries.reshape(length, HEADS, HEAD_DIM)
    key_heads = key_all.reshape(length, HEADS, HEAD_DIM)
    value_heads = value_all.reshape(length, HEADS, HEAD_DIM)
    positions = jnp.arange(length, dtype=jnp.int32)
    allowed = positions[None, :] <= positions[:, None]
    scores = low_back(jnp.einsum('ihd,jhd->hij', query_heads, key_heads, precision=HIGHEST)) * scale
    scores = jnp.where(allowed[None], scores, -1e+30)
    row_max = lax.optimization_barrier(jnp.max(scores, axis=-1, keepdims=True))
    exponent = jnp.exp(scores - row_max)
    probability = exponent / lax.optimization_barrier(jnp.sum(exponent, axis=-1, keepdims=True))
    attended = low(low_back(jnp.einsum('hij,jhd->ihd', low(probability), value_heads, precision=HIGHEST)))
    attended = attended.reshape(length, HEADS * HEAD_DIM)
    resid = inputs + low_back(jnp.dot(attended, out_w, precision=HIGHEST))
    inv_two = lax.rsqrt(lax.optimization_barrier(jnp.mean(resid * resid, axis=-1, keepdims=True)) + EPSILON)
    normed_two = low(resid * inv_two * gain_two)
    gate = low_back(jnp.dot(normed_two, gate_w, precision=HIGHEST))
    up_value = low_back(jnp.dot(normed_two, up_w, precision=HIGHEST))
    hidden = low(jax.nn.silu(gate) * up_value)
    return resid + low_back(jnp.dot(hidden, down_w, precision=HIGHEST))

def reference(tokens, cotangent, group_ids, loss_weight, gain_attn, w_query, w_latent, w_key_up, w_value_up, w_out, gain_mlp, w_gate, w_up, w_down):
    params = tuple((item.astype(jnp.float32) for item in (gain_attn, w_query, w_latent, w_key_up, w_value_up, w_out, gain_mlp, w_gate, w_up, w_down)))
    onehot = (group_ids[:, None] == jnp.arange(GROUPS, dtype=jnp.int32)[None, :]).astype(jnp.float32)
    counts = lax.optimization_barrier(jnp.sum(onehot, axis=0))
    own_count = lax.optimization_barrier(jnp.sum(onehot * counts[None, :], axis=1))
    own_weight = lax.optimization_barrier(jnp.sum(onehot * loss_weight[None, :], axis=1))
    seq_scale = own_weight * (SEQS / GROUPS) / own_count

    def one_sequence(carry, item):
        inputs, grad_in, factor = item
        result, pullback = jax.vjp(layer, inputs.astype(jnp.float32), *params)
        grads = pullback(grad_in.astype(jnp.float32) * factor)
        carry = tuple((total_item + grad_item for total_item, grad_item in zip(carry, grads[1:])))
        return (carry, (result.astype(jnp.bfloat16), grads[0].astype(jnp.bfloat16)))
    zeros = tuple((jnp.zeros_like(item) for item in params))
    totals, outs_pair = lax.scan(one_sequence, zeros, (tokens, cotangent, seq_scale))
    return (outs_pair[0], outs_pair[1], totals[0], totals[1], totals[2], totals[3], totals[4], totals[5], totals[6], totals[7], totals[8], totals[9])
```

```python
import math

import jax
import jax.numpy as jnp
from jax import lax
from jax.experimental import pallas as pl
from jax.experimental.pallas import tpu as pltpu
from jax.sharding import Mesh
from jax.sharding import PartitionSpec as P

HEADS = 16
HEAD_DIM = 64
LATENT = 256
KV_GROUPS = 2
GROUPS = 4
EPSILON = 1e-06
BF16 = jnp.bfloat16
F32 = jnp.float32
ROWS = (((0,), (0,)), ((), ()))
COLS = (((1,), (1,)), ((), ()))
PLAIN = (((1,), (0,)), ((), ()))


def dot(a, b, dims=PLAIN):
    return lax.dot_general(a, b, dims, preferred_element_type=F32)


def shift(values, axis, step):
    size = lax.axis_size(axis)
    return lax.ppermute(values, axis, [(i, (i + step) % size) for i in range(size)])


def swap(values):
    return shift(values, "core", 1)


def spread_z(shard):
    return [shard] + [shift(shard, "z", k) for k in range(1, lax.axis_size("z"))]


def spread_plane(stack, by_x):
    ny, nx = lax.axis_size("y"), lax.axis_size("x")
    blocks = [[None] * nx for _ in range(ny)]
    blocks[0][0] = stack
    for i in range(1, nx):
        blocks[0][i] = shift(stack, "x", i)
    for j in range(1, ny):
        blocks[j][0] = shift(stack, "y", j)
    for j in range(1, ny):
        for i in range(1, nx):
            blocks[j][i] = shift(blocks[j][0], "x", i) if by_x else shift(blocks[0][i], "y", j)
    return blocks


def collect(blocks, by_x):
    ny, nx, nz = lax.axis_size("y"), lax.axis_size("x"), lax.axis_size("z")
    if not by_x:
        blocks = [[blocks[j][i] for j in range(ny)] for i in range(nx)]
        first, second, n_first, n_second = "y", "x", ny, nx
    else:
        first, second, n_first, n_second = "x", "y", nx, ny
    totals = []
    for j in reversed(range(n_second)):
        total = blocks[j][0].astype(F32)
        for i in range(1, n_first):
            total = total + shift(blocks[j][i], first, i).astype(F32)
        totals.append(total)
    own = totals[-1]
    for j in range(1, n_second):
        own = own + shift(totals[n_second - 1 - j].astype(BF16), second, j).astype(F32)
    total = own[0]
    for k in range(1, nz):
        total = total + shift(own[k].astype(BF16), "z", k).astype(F32)
    return total


def place(sizes, offsets):
    return [lax.rem(lax.axis_index(name) + n + o, n) for (name, n), o in zip(sizes, offsets)]


def merge_blocks(blocks):
    ny, nx = len(blocks), len(blocks[0])
    nz, rows, columns = blocks[0][0].shape
    flat = [blocks[j][i] for j in range(ny) for i in range(nx)]
    sizes = (("z", nz), ("y", ny), ("x", nx))

    def kernel(*refs):
        out, sems = refs[-2], refs[-1]
        copies = []
        for j in range(ny):
            for i in range(nx):
                for k in range(nz):
                    z, y, x = place(sizes, (-k, -j, -i))
                    n = j * nx + i
                    copies.append(
                        pltpu.make_async_copy(refs[n].at[k], out.at[z, y, x], sems.at[n * nz + k])
                    )
        for copy in copies:
            copy.start()
        for copy in copies:
            copy.wait()

    out = pl.pallas_call(
        kernel,
        out_shape=jax.ShapeDtypeStruct((nz, ny, nx, rows, columns), flat[0].dtype),
        in_specs=[pl.BlockSpec(memory_space=pl.ANY)] * len(flat),
        out_specs=pl.BlockSpec(memory_space=pl.ANY),
        scratch_shapes=[pltpu.SemaphoreType.DMA((nz * ny * nx,))],
        name="merge",
    )(*flat)
    return out.reshape(nz * ny * nx * rows, columns)


def split_blocks(full):
    nz, ny, nx = lax.axis_size("z"), lax.axis_size("y"), lax.axis_size("x")
    rows = full.shape[0] // (nz * ny * nx)
    columns = full.shape[1]
    sizes = (("z", nz), ("y", ny), ("x", nx))

    def kernel(*refs):
        source, outs, sems = refs[0], refs[1:-1], refs[-1]
        copies = []
        for j in range(ny):
            for i in range(nx):
                for k in range(nz):
                    z, y, x = place(sizes, (k, j, i))
                    n = j * nx + i
                    copies.append(
                        pltpu.make_async_copy(source.at[z, y, x], outs[n].at[k], sems.at[n * nz + k])
                    )
        for copy in copies:
            copy.start()
        for copy in copies:
            copy.wait()

    outs = pl.pallas_call(
        kernel,
        out_shape=[jax.ShapeDtypeStruct((nz, rows, columns), full.dtype)] * (ny * nx),
        in_specs=[pl.BlockSpec(memory_space=pl.ANY)],
        out_specs=[pl.BlockSpec(memory_space=pl.ANY)] * (ny * nx),
        scratch_shapes=[pltpu.SemaphoreType.DMA((nz * ny * nx,))],
        name="split",
    )(full.reshape(nz, ny, nx, rows, columns))
    return [[outs[j * nx + i] for i in range(nx)] for j in range(ny)]


def all_sum(values, axes):
    for axis in axes:
        size = lax.axis_size(axis)
        total = values
        for k in range(1, size):
            total = total + shift(values, axis, k)
        values = total
    return values


def head_halves(pair):
    lane = lax.broadcasted_iota(jnp.int32, pair.shape, 1)
    zero = jnp.zeros_like(pair)
    return jnp.concatenate(
        [jnp.where(lane < HEAD_DIM, pair, zero), jnp.where(lane >= HEAD_DIM, pair, zero)], axis=0
    )


def join_halves(halves):
    rows = halves.shape[0] // 2
    lane = lax.broadcasted_iota(jnp.int32, (rows, halves.shape[1]), 1)
    return jnp.where(lane < HEAD_DIM, halves[:rows], halves[rows:])


def attend_kernel(nz, q_ref, *refs):
    lats, (wk_ref, wv_ref, att_ref, key_ref, value_ref, prob_ref) = refs[:nz], refs[nz:]
    local = q_ref.shape[1]
    z = lax.axis_index("z")
    q2 = head_halves(q_ref[0] * BF16(HEAD_DIM**-0.5))
    wk, wv = wk_ref[...], wv_ref[...]
    scores = []
    for k in range(nz):
        lat = lats[k][0]
        key = dot(lat, wk).astype(BF16)
        value = dot(lat, wv).astype(BF16)
        key_ref[0, k * local : (k + 1) * local] = key
        value_ref[0, k * local : (k + 1) * local] = value
        block = dot(q2, key, COLS)
        if k == 0:
            row = lax.rem(lax.broadcasted_iota(jnp.int32, block.shape, 0), local)
            column = lax.broadcasted_iota(jnp.int32, block.shape, 1)
            block = jnp.where(column <= row, block, -1e30)
        else:
            block = block + jnp.where(z >= k, 0.0, -1e30)
        scores.append(block)
    top = scores[0]
    for block in scores[1:]:
        top = jnp.maximum(top, block)
    top = jnp.max(top, axis=1, keepdims=True)
    exps = [jnp.exp(block - top) for block in scores]
    total = exps[0]
    for block in exps[1:]:
        total = total + block
    inverse = 1.0 / jnp.sum(total, axis=1, keepdims=True)
    mixed = jnp.zeros((2 * local, q_ref.shape[2]), F32)
    for k in range(nz):
        prob = (exps[k] * inverse).astype(BF16)
        prob_ref[0, 0, k] = prob
        mixed = mixed + dot(prob, value_ref[0, k * local : (k + 1) * local])
    att_ref[0] = join_halves(mixed).astype(BF16)


def attend(queries, lats, key_up, value_up):
    seqs, local, width = queries.shape
    nz = len(lats)
    pairs = width // 128
    query_spec = pl.BlockSpec((1, local, 128), lambda s, h: (s, 0, h))
    full_spec = pl.BlockSpec((1, nz * local, 128), lambda s, h: (s, 0, h))
    lat_spec = pl.BlockSpec((1, local, LATENT), lambda s, h: (s, 0, 0))
    up_spec = pl.BlockSpec((LATENT, 128), lambda s, h: (0, h))
    full = jax.ShapeDtypeStruct((seqs, nz * local, width), BF16)
    return pl.pallas_call(
        lambda *refs: attend_kernel(nz, *refs),
        grid=(seqs, pairs),
        in_specs=[query_spec] + [lat_spec] * nz + [up_spec] * 2,
        out_specs=[
            query_spec,
            full_spec,
            full_spec,
            pl.BlockSpec((1, 1, nz, 2 * local, local), lambda s, h: (s, h, 0, 0, 0)),
        ],
        out_shape=[
            jax.ShapeDtypeStruct(queries.shape, BF16),
            full,
            full,
            jax.ShapeDtypeStruct((seqs, pairs, nz, 2 * local, local), BF16),
        ],
        compiler_params=pltpu.CompilerParams(vmem_limit_bytes=48 * 2**20),
        cost_estimate=pl.CostEstimate(
            flops=12 * seqs * pairs * nz * local * local * 256,
            bytes_accessed=16 * 2**20,
            transcendentals=seqs * pairs * nz * 2 * local * local,
        ),
        name="attend",
    )(queries, *lats, key_up, value_up)


def attend_back_kernel(nz, pairs, q_ref, g_ref, att_ref, key_ref, value_ref, prob_ref, *refs):
    lats, (wk_ref, wv_ref), rest = refs[:nz], refs[nz : nz + 2], refs[nz + 2 :]
    dq_ref, dlats, (up_ref, lat_acc) = rest[0], rest[1 : nz + 1], rest[nz + 1 :]
    seq, pair = pl.program_id(0), pl.program_id(1)
    local = q_ref.shape[1]
    scale = HEAD_DIM**-0.5
    q2 = head_halves(q_ref[0] * BF16(scale))
    grad = g_ref[0]
    g2 = head_halves(grad)
    product = grad.astype(F32) * att_ref[0].astype(F32)
    inner = jnp.sum(head_halves(product), axis=1, keepdims=True)
    dq = jnp.zeros((2 * local, 128), F32)
    up_key = jnp.zeros((LATENT, 128), F32)
    up_value = jnp.zeros((LATENT, 128), F32)
    for k in range(nz):
        rows = slice(k * local, (k + 1) * local)
        prob = prob_ref[0, 0, k]
        key, value = key_ref[0, rows], value_ref[0, rows]
        grad_prob = dot(g2, value, COLS)
        grad_score = (prob.astype(F32) * (grad_prob - inner)).astype(BF16)
        dq = dq + dot(grad_score, key)
        grad_key = dot(grad_score, q2, ROWS).astype(BF16)
        grad_value = dot(prob, g2, ROWS).astype(BF16)
        term = dot(grad_key, wk_ref[...], COLS) + dot(grad_value, wv_ref[...], COLS)

        @pl.when(pair == 0)
        def _():
            lat_acc[rows] = term

        @pl.when(pair > 0)
        def _():
            lat_acc[rows] += term

        lat = lats[k][0]
        up_key = up_key + dot(lat, grad_key, ROWS)
        up_value = up_value + dot(lat, grad_value, ROWS)
    dq_ref[0] = (join_halves(dq) * scale).astype(BF16)

    @pl.when(seq == 0)
    def _():
        up_ref[0, pair] = up_key
        up_ref[1, pair] = up_value

    @pl.when(seq > 0)
    def _():
        up_ref[0, pair] += up_key
        up_ref[1, pair] += up_value

    @pl.when(pair == pairs - 1)
    def _():
        for k in range(nz):
            dlats[k][0] = lat_acc[k * local : (k + 1) * local].astype(BF16)


def attend_back(queries, grad_att, attended, keys, values, probs, lats, key_up, value_up):
    seqs, local, width = queries.shape
    nz = len(lats)
    pairs = width // 128
    query_spec = pl.BlockSpec((1, local, 128), lambda s, h: (s, 0, h))
    full_spec = pl.BlockSpec((1, nz * local, 128), lambda s, h: (s, 0, h))
    lat_spec = pl.BlockSpec((1, local, LATENT), lambda s, h: (s, 0, 0))
    up_spec = pl.BlockSpec((LATENT, 128), lambda s, h: (0, h))
    prob_spec = pl.BlockSpec((1, 1, nz, 2 * local, local), lambda s, h: (s, h, 0, 0, 0))
    outs = pl.pallas_call(
        lambda *refs: attend_back_kernel(nz, pairs, *refs),
        grid=(seqs, pairs),
        in_specs=[query_spec] * 3 + [full_spec] * 2 + [prob_spec] + [lat_spec] * nz + [up_spec] * 2,
        out_specs=[query_spec]
        + [lat_spec] * nz
        + [pl.BlockSpec((2, pairs, LATENT, 128), lambda s, h: (0, 0, 0, 0))],
        out_shape=[jax.ShapeDtypeStruct(queries.shape, BF16)]
        + [jax.ShapeDtypeStruct((seqs, local, LATENT), BF16)] * nz
        + [jax.ShapeDtypeStruct((2, pairs, LATENT, 128), F32)],
        scratch_shapes=[pltpu.VMEM((nz * local, LATENT), F32)],
        compiler_params=pltpu.CompilerParams(vmem_limit_bytes=48 * 2**20),
        cost_estimate=pl.CostEstimate(
            flops=24 * seqs * pairs * nz * local * local * 256,
            bytes_accessed=16 * 2**20,
            transcendentals=0,
        ),
        name="attend_back",
    )(queries, grad_att, attended, keys, values, probs, *lats, key_up, value_up)
    return outs[0], outs[1 : nz + 1], outs[nz + 1]


def half(values, which, axis=1):
    size = values.shape[axis] // 2
    return lax.dynamic_slice_in_dim(values, which * size, size, axis)


def in_order(core, own, other, axis):
    return jnp.where(
        core == 0,
        jnp.concatenate([own, other], axis=axis),
        jnp.concatenate([other, own], axis=axis),
    )


def rms_back(grad_normed, inputs, inv_rms, gain):
    weighted = grad_normed * gain
    return inv_rms * weighted - inputs * inv_rms**3 * jnp.mean(
        weighted * inputs, axis=-1, keepdims=True
    )


def inverse_rms(values):
    return lax.rsqrt(jnp.mean(values * values, axis=-1, keepdims=True) + EPSILON)


def on_device(
    tokens,
    cotangent,
    group_ids,
    loss_weight,
    gain_attn,
    w_query,
    w_latent,
    w_key_up,
    w_value_up,
    w_out,
    gain_mlp,
    w_gate,
    w_up,
    w_down,
):
    nz, ny, nx = lax.axis_size("z"), lax.axis_size("y"), lax.axis_size("x")
    core = lax.axis_index("core")
    other = 1 - core
    local, depth = tokens.shape[1:]
    latent_width = w_latent.shape[1] // 2
    hidden_width = w_gate.shape[1] // 2
    query_width = w_query.shape[1] // 2
    gain_one = gain_attn.astype(F32)
    gain_two = gain_mlp.astype(F32)

    out_t = w_out.T
    row_parts = [w_query, w_latent, out_t, w_gate, w_up]
    mine = [half(part, core) for part in row_parts]
    theirs = [half(part, other) for part in row_parts]
    attn_recv = swap(jnp.concatenate(theirs[:3], axis=1))
    attn_shard = in_order(core, jnp.concatenate(mine[:3], axis=1), attn_recv, 0)
    attn_z = jnp.stack(spread_z(attn_shard))
    q_blocks = spread_plane(attn_z[:, :, :query_width], True)
    lo_blocks = spread_plane(attn_z[:, :, query_width:], False)
    ff_recv = swap(jnp.concatenate(theirs[3:], axis=1))
    ff_shard = in_order(core, jnp.concatenate(mine[3:], axis=1), ff_recv, 0)
    down_recv = swap(half(w_down, other))
    down_shard = in_order(core, half(w_down, core), down_recv, 0)
    ff_z = jnp.stack(spread_z(ff_shard))
    gate_blocks = spread_plane(ff_z[:, :, :hidden_width], True)
    up_blocks = spread_plane(ff_z[:, :, hidden_width:], False)
    down_z = jnp.stack(spread_z(down_shard))
    down_blocks = spread_plane(down_z, True)

    both = swap(jnp.concatenate([tokens, cotangent], axis=0))
    inputs = jnp.concatenate([tokens[0], both[0]], axis=0).astype(F32)
    onehot = (group_ids[:, None] == jnp.arange(GROUPS, dtype=jnp.int32)[None, :]).astype(F32)
    onehot_other = swap(onehot)
    counts = all_sum(jnp.sum(onehot, axis=0) + jnp.sum(onehot_other, axis=0), ("x", "y"))
    total_seqs = ny * nx * 2 * group_ids.shape[0]

    def factor(row):
        return jnp.sum(row * loss_weight) * (total_seqs / GROUPS) / jnp.sum(row * counts)

    grad_out = jnp.concatenate(
        [
            cotangent[0].astype(F32) * factor(onehot[0]),
            both[1].astype(F32) * factor(onehot_other[0]),
        ],
        axis=0,
    )
    grad_out_low = grad_out.astype(BF16)

    inv_one = inverse_rms(inputs)
    normed_one = (inputs * inv_one * gain_one).astype(BF16)
    query_w = merge_blocks(q_blocks)
    lo_w = merge_blocks(lo_blocks)
    latent_w, out_w = lo_w[:, :latent_width], lo_w[:, latent_width:]
    latent = dot(normed_one, latent_w).astype(BF16).reshape(2, local, latent_width)
    lats = [latent] + [
        lax.ppermute(latent, "z", [(i, i + k) for i in range(nz - k)]) for k in range(1, nz)
    ]
    queries = dot(normed_one, query_w).astype(BF16).reshape(2, local, query_width)
    key_up = lax.dynamic_index_in_dim(w_key_up, core, 0, keepdims=False)
    value_up = lax.dynamic_index_in_dim(w_value_up, core, 0, keepdims=False)
    attended, keys, values, probs = attend(queries, lats, key_up, value_up)
    attended_flat = attended.reshape(2 * local, query_width)
    partial = dot(attended_flat, out_w, COLS)
    mixed = swap(jnp.concatenate([partial[local:], partial[:local]], axis=0).astype(BF16))
    resid = inputs + partial + mixed.astype(F32)

    inv_two = inverse_rms(resid)
    normed_two = (resid * inv_two * gain_two).astype(BF16)
    gate_w = merge_blocks(gate_blocks)
    up_w = merge_blocks(up_blocks)
    down_cols = merge_blocks(down_blocks)
    down_w = in_order(core, half(down_cols, core, 0), swap(half(down_cols, other, 0)), 1)
    gate = dot(normed_two, gate_w)
    up_value = dot(normed_two, up_w)
    sigma = jax.nn.sigmoid(gate)
    silu_gate = gate * sigma
    hidden = (silu_gate * up_value).astype(BF16)
    mlp_part = dot(hidden, down_w)
    result = (resid[:local] + mlp_part[:local] + swap(mlp_part[local:].astype(BF16)).astype(F32)).astype(
        BF16
    )[None]
    down_rows = dot(hidden, grad_out_low, ROWS).astype(BF16)
    grad_down = in_order(core, half(down_rows, core, 1), swap(half(down_rows, other, 1)), 0)
    down_total = collect(split_blocks(grad_down), True)
    grad_hidden = dot(grad_out_low, down_w, COLS)
    grad_gate = (grad_hidden * up_value * sigma * (1.0 + gate * (1.0 - sigma))).astype(BF16)
    grad_up = (grad_hidden * silu_gate).astype(BF16)
    gate_total = collect(split_blocks(dot(normed_two, grad_gate, ROWS).astype(BF16)), True)
    up_total = collect(split_blocks(dot(normed_two, grad_up, ROWS).astype(BF16)), False)
    normed_part = dot(grad_gate, gate_w, COLS) + dot(grad_up, up_w, COLS)
    gain_two_part = jnp.sum(normed_part * resid * inv_two, axis=0)
    grad_normed = normed_part + swap(
        jnp.concatenate([normed_part[local:], normed_part[:local]], axis=0).astype(BF16)
    ).astype(F32)
    grad_resid = grad_out + rms_back(grad_normed, resid, inv_two, gain_two)
    grad_resid_low = grad_resid.astype(BF16)

    grad_attended = dot(grad_resid_low, out_w).astype(BF16).reshape(2, local, query_width)
    out_rows = dot(grad_resid_low, attended_flat, ROWS).astype(BF16)
    out_total = collect(split_blocks(out_rows), False)
    grad_queries, grad_lats, up_grads = attend_back(
        queries, grad_attended, attended, keys, values, probs, lats, key_up, value_up
    )
    grad_latent = grad_lats[0].astype(F32)
    for k in range(1, nz):
        grad_latent = grad_latent + lax.ppermute(
            grad_lats[k], "z", [(i + k, i) for i in range(nz - k)]
        ).astype(F32)
    grad_latent = grad_latent.astype(BF16).reshape(2 * local, latent_width)
    grad_queries = grad_queries.reshape(2 * local, query_width)
    chips = nz * ny * nx
    up_flat = up_grads.reshape(chips * 16, -1).astype(BF16)
    up_sum = collect(split_blocks(up_flat), True).astype(BF16)
    up_all = merge_blocks(spread_plane(jnp.stack(spread_z(up_sum)), True))
    up_pair = in_order(core, up_all[None], swap(up_all)[None], 0).astype(F32)
    up_pair = up_pair.reshape((2,) + up_grads.shape).transpose(1, 0, 3, 2, 4)
    up_pair = up_pair.reshape(2, KV_GROUPS, LATENT, query_width)

    query_total = collect(split_blocks(dot(normed_one, grad_queries, ROWS).astype(BF16)), True)
    latent_total = collect(split_blocks(dot(normed_one, grad_latent, ROWS).astype(BF16)), False)
    normed_part = dot(grad_queries, query_w, COLS) + dot(grad_latent, latent_w, COLS)
    gain_one_part = jnp.sum(normed_part * inputs * inv_one, axis=0)
    grad_normed = normed_part[:local] + swap(normed_part[local:].astype(BF16)).astype(F32)
    input_grad = (
        grad_resid[:local] + rms_back(grad_normed, inputs[:local], inv_one[:local], gain_one)
    ).astype(BF16)[None]
    gains = all_sum(jnp.stack([gain_one_part, gain_two_part]), ("core", "x", "y", "z"))

    def owned(totals):
        joined = jnp.concatenate(totals, axis=1).astype(BF16)
        received = swap(half(joined, other, 0))
        mine = half(joined, core, 0)
        results, start = [], 0
        for total in totals:
            width = total.shape[1]
            results.append(
                in_order(core, mine[:, start : start + width], received[:, start : start + width], 1)
                .astype(F32)
            )
            start += width
        return results

    (owned_down,) = owned([down_total])
    owned_gate, owned_up = owned([gate_total, up_total])
    owned_out, owned_query, owned_latent = owned([out_total, query_total, latent_total])
    return (
        result,
        input_grad,
        gains[0],
        owned_query,
        owned_latent,
        up_pair[0],
        up_pair[1],
        owned_out.T,
        gains[1],
        owned_gate,
        owned_up,
        owned_down,
    )


def solution(mesh):
    nz = mesh.shape["seq"]
    chips = mesh.shape["batch"] // 2
    nx = math.isqrt(chips)
    while chips % nx:
        nx -= 1
    fine = Mesh(mesh.devices.reshape(nz, chips // nx, nx, 2), ("z", "y", "x", "core"))
    batch = ("y", "x", "core")
    every = ("z",) + batch
    by_rows = P(every, None)
    in_specs = (
        P(batch, "z", None),
        P(batch, "z", None),
        P(batch),
        P(),
        P(),
        by_rows,
        by_rows,
        P(),
        P(),
        P(None, every),
        P(),
        by_rows,
        by_rows,
        by_rows,
    )
    out_specs = (
        P(batch, "z", None),
        P(batch, "z", None),
        P(),
        by_rows,
        by_rows,
        P(),
        P(),
        P(None, every),
        P(),
        by_rows,
        by_rows,
        by_rows,
    )
    return jax.shard_map(
        on_device, mesh=fine, in_specs=in_specs, out_specs=out_specs, check_vma=False
    )
```

```python
import math

import jax
import jax.numpy as jnp
from jax import lax
from jax.experimental import pallas as pl
from jax.experimental.pallas import tpu as pltpu
from jax.sharding import Mesh
from jax.sharding import PartitionSpec as P

HEADS = 16
HEAD_DIM = 64
LATENT = 256
KV_GROUPS = 2
GROUPS = 4
EPSILON = 1e-06
BF16 = jnp.bfloat16
F32 = jnp.float32
ROWS = (((0,), (0,)), ((), ()))
OPT = {"attn_plane": 5, "attn_z": 13, "back_0": 112, "back_1": 92, "c_attend": 4, "c_back": 4, "c_fb": 4, "c_ff": 4, "c_merge": 4, "c_mix": 4, "c_rb": 4, "c_split": 4, "down_last": 2, "down_plane": 2, "down_z": 2, "ff_back_z": 1, "ff_plane": 4, "ff_z": 1, "gains": 2, "hidden": 1, "kv": 2, "kv_spread": 4, "kv_z": 3, "lat_back": 16, "normed_last": 1, "normed_part": 1, "query_back": 2}
COLS = (((1,), (1,)), ((), ()))
PLAIN = (((1,), (0,)), ((), ()))


def dot(a, b, dims=PLAIN):
    return lax.dot_general(a, b, dims, preferred_element_type=F32)


PLANE = ("y", "x", "core")


def shift(values, axis, step):
    size = lax.axis_size(axis)
    return lax.ppermute(values, axis, [(i, (i + step) % size) for i in range(size)])


def leg(values, first, step):
    size = lax.axis_size("x")
    pairs = []
    for y in range(size):
        for x in range(size):
            for core in range(2):
                if (core == 0) == first:
                    target = (y, (x + step) % size, core)
                else:
                    target = ((y + step) % size, x, core)
                pairs.append(
                    ((y * size + x) * 2 + core, (target[0] * size + target[1]) * 2 + target[2])
                )
    return lax.ppermute(values, PLANE, pairs)


def swap(values):
    return shift(values, "core", 1)


def spread_z(shard):
    return [shard] + [shift(shard, "z", k) for k in range(1, lax.axis_size("z"))]


def spread_ring(shard):
    nz = lax.axis_size("z")
    pairs = [(z * 2 + c, (z + 1 - 2 * c) % nz * 2 + c) for z in range(nz) for c in range(2)]
    blocks = [shard]
    for _ in range(nz - 1):
        blocks.append(lax.ppermute(blocks[-1], ("z", "core"), pairs))
    return blocks


def spread_own(stack):
    size = lax.axis_size("x")
    return (
        [leg(stack, True, a) for a in range(1, size)],
        [leg(stack, False, b) for b in range(1, size)],
    )


def spread_rest(stack, on_a, on_b):
    size = lax.axis_size("x")
    return [[stack] + on_a] + [
        [on_b[b - 1]] + [leg(block, False, b) for block in on_a] for b in range(1, size)
    ]


def after(value, *others):
    return lax.optimization_barrier((value,) + others)[0]


def tie(name, value, *others):
    mask = OPT.get(name, 0)
    chosen = [other for i, other in enumerate(others) if mask >> i & 1]
    return after(value, *chosen) if chosen else value


def cost(name, flops):
    return pl.CostEstimate(
        flops=int(flops * OPT.get(name, 0) / 4), bytes_accessed=4096, transcendentals=0
    )


def send_b(parts):
    return [leg(parts[b], False, b) for b in range(1, len(parts))]


def add_b(parts, received):
    row = parts[0]
    for part in received:
        row = add(row, part)
    return row


def send_a(row):
    return [leg(row[a], True, a) for a in range(1, row.shape[0])]


def add_a(row, received):
    own = row[0]
    for part in received:
        own = add(own, part)
    return own


def send_z(own):
    return [shift(own[k], "z", k) for k in range(1, own.shape[0])]


def add_z(own, received):
    total = own[0].astype(F32)
    for part in received:
        total = total + part.astype(F32)
    return total


def add(left, right):
    return (left.astype(F32) + right.astype(F32)).astype(BF16)


def to_half(values, step):
    nz = lax.axis_size("z")
    pairs = []
    for z in range(nz):
        keeper = z // (nz // 2)
        source = z * 2 + (keeper if step else 1 - keeper)
        pairs.append((source, (z + step) % nz * 2 + keeper))
    return lax.ppermute(values, ("z", "core"), pairs)


def spread_down_z(chip):
    nz, z, core = lax.axis_size("z"), lax.axis_index("z"), lax.axis_index("core")
    return [chip] + [to_half(chip, k) for k in range(1, nz)]


def down_stack(received):
    nz, z, core = lax.axis_size("z"), lax.axis_index("z"), lax.axis_index("core")
    received = jnp.stack(received)
    parts = []
    for j in range(nz // 2):
        step = lax.rem(z + nz - core * (nz // 2) - j, nz)
        parts.append(lax.dynamic_slice_in_dim(received, step, 1, 0))
    return jnp.concatenate(parts, axis=0)


def down_block(own, chip_z):
    count = own.shape[0]
    index = jnp.clip(chip_z - lax.axis_index("core") * count, 0, count - 1)
    return lax.dynamic_index_in_dim(own, index, 0, keepdims=False)


def send_down_z(own):
    nz, z, count = lax.axis_size("z"), lax.axis_index("z"), own.shape[0]
    received = []
    for k in range(1, nz):
        pairs = [((d + k) % nz * 2 + d // count, d * 2 + d // count) for d in range(nz)]
        part = down_block(own, lax.rem(z + nz - k, nz))
        received.append(lax.ppermute(part, ("z", "core"), pairs))
    return received


def own_down(own, received):
    nz, z, core = lax.axis_size("z"), lax.axis_index("z"), lax.axis_index("core")
    count = nz // 2
    total = down_block(own, z).astype(F32)
    for part in received:
        total = total + part.astype(F32)
    pairs = [(d * 2 + d // count, d * 2 + 1 - d // count) for d in range(nz)]
    sent = lax.ppermute(half(total, 1 - core, 0).astype(BF16), ("z", "core"), pairs)
    return jnp.where(core == z // count, half(total, core, 0), sent.astype(F32))


def place(size, nz, k, b, a):
    core = lax.axis_index("core")
    z = lax.rem(lax.axis_index("z") + nz + k, nz)
    y = lax.rem(lax.axis_index("y") + size + b + core * (a - b), size)
    x = lax.rem(lax.axis_index("x") + size + a + core * (b - a), size)
    return z, y, x


def merge_blocks(blocks, fixed=False, ring=False):
    size = len(blocks)
    nz, rows, columns = blocks[0][0].shape
    parts = [block for row in blocks for block in row]

    def kernel(*refs):
        out, sems = refs[-2], refs[-1]
        copies = []
        for b in range(size):
            for a in range(size):
                for k in range(nz):
                    away = k * (2 * lax.axis_index("core") - 1) if ring else -k
                    z, y, x = place(size, nz, away, -b, -a)
                    n = b * size + a
                    copies.append(
                        pltpu.make_async_copy(
                            refs[n].at[k], out.at[k if fixed else z, y, x], sems.at[n * nz + k]
                        )
                    )
        for copy in copies:
            copy.start()
        for copy in copies:
            copy.wait()

    out = pl.pallas_call(
        kernel,
        out_shape=jax.ShapeDtypeStruct((nz, size, size, rows, columns), parts[0].dtype),
        in_specs=[pl.BlockSpec(memory_space=pl.ANY)] * len(parts),
        out_specs=pl.BlockSpec(memory_space=pltpu.VMEM),
        scratch_shapes=[pltpu.SemaphoreType.DMA((nz * size * size,))],
        compiler_params=pltpu.CompilerParams(vmem_limit_bytes=48 * 2**20),
        cost_estimate=cost("c_merge", 3e9),
        name="merge",
    )(*parts)
    return out.reshape(nz * size * size * rows, columns)


def split_blocks(full, nz, fixed=False):
    size = lax.axis_size("x")
    rows = full.shape[0] // (nz * size * size)
    columns = full.shape[1]

    def kernel(*refs):
        source, outs, sems = refs[0], refs[1:-1], refs[-1]
        copies = []
        for b in range(size):
            for a in range(size):
                for k in range(nz):
                    z, y, x = place(size, nz, k, b, a)
                    copies.append(
                        pltpu.make_async_copy(
                            source.at[k if fixed else z, y, x],
                            outs[b].at[a, k],
                            sems.at[(b * size + a) * nz + k],
                        )
                    )
        for copy in copies:
            copy.start()
        for copy in copies:
            copy.wait()

    return pl.pallas_call(
        kernel,
        out_shape=[jax.ShapeDtypeStruct((size, nz, rows, columns), full.dtype)] * size,
        in_specs=[pl.BlockSpec(memory_space=pltpu.VMEM)],
        out_specs=[pl.BlockSpec(memory_space=pl.ANY)] * size,
        scratch_shapes=[pltpu.SemaphoreType.DMA((nz * size * size,))],
        compiler_params=pltpu.CompilerParams(vmem_limit_bytes=48 * 2**20),
        cost_estimate=cost("c_split", 3e9),
        name="split",
    )(full.reshape(nz, size, size, rows, columns))


def all_sum(values, axes):
    for axis in axes:
        size = lax.axis_size(axis)
        total = values
        for k in range(1, size):
            total = total + shift(values, axis, k)
        values = total
    return values


def head_halves(pair):
    lane = lax.broadcasted_iota(jnp.int32, pair.shape, 1)
    zero = jnp.zeros_like(pair)
    return jnp.concatenate(
        [jnp.where(lane < HEAD_DIM, pair, zero), jnp.where(lane >= HEAD_DIM, pair, zero)], axis=0
    )


def join_halves(halves):
    rows = halves.shape[0] // 2
    lane = lax.broadcasted_iota(jnp.int32, (rows, halves.shape[1]), 1)
    return jnp.where(lane < HEAD_DIM, halves[:rows], halves[rows:])


def attend_kernel(nz, q_ref, *refs):
    lats, (wk_ref, wv_ref, att_ref, key_ref, value_ref, prob_ref) = refs[:nz], refs[nz:]
    local = q_ref.shape[1]
    z = lax.axis_index("z")
    q2 = head_halves(q_ref[0] * BF16(HEAD_DIM**-0.5))
    wk, wv = wk_ref[...], wv_ref[...]
    scores = []
    for k in range(nz):
        lat = lats[k][0]
        key = dot(lat, wk).astype(BF16)
        value = dot(lat, wv).astype(BF16)
        key_ref[0, k * local : (k + 1) * local] = key
        value_ref[0, k * local : (k + 1) * local] = value
        block = dot(q2, key, COLS)
        if k == 0:
            row = lax.rem(lax.broadcasted_iota(jnp.int32, block.shape, 0), local)
            column = lax.broadcasted_iota(jnp.int32, block.shape, 1)
            block = jnp.where(column <= row, block, -1e30)
        else:
            block = block + jnp.where(z >= k, 0.0, -1e30)
        scores.append(block)
    top = scores[0]
    for block in scores[1:]:
        top = jnp.maximum(top, block)
    top = jnp.max(top, axis=1, keepdims=True)
    exps = [jnp.exp(block - top) for block in scores]
    total = exps[0]
    for block in exps[1:]:
        total = total + block
    inverse = 1.0 / jnp.sum(total, axis=1, keepdims=True)
    mixed = jnp.zeros((2 * local, q_ref.shape[2]), F32)
    for k in range(nz):
        prob = (exps[k] * inverse).astype(BF16)
        prob_ref[0, 0, k] = prob
        mixed = mixed + dot(prob, value_ref[0, k * local : (k + 1) * local])
    att_ref[0] = join_halves(mixed).astype(BF16)


def attend(queries, lats, key_up, value_up):
    seqs, local, width = queries.shape
    nz = len(lats)
    pairs = width // 128
    query_spec = pl.BlockSpec((1, local, 128), lambda s, h: (s, 0, h))
    full_spec = pl.BlockSpec((1, nz * local, 128), lambda s, h: (s, 0, h))
    lat_spec = pl.BlockSpec((1, local, LATENT), lambda s, h: (s, 0, 0))
    up_spec = pl.BlockSpec((LATENT, 128), lambda s, h: (0, h))
    full = jax.ShapeDtypeStruct((seqs, nz * local, width), BF16)
    return pl.pallas_call(
        lambda *refs: attend_kernel(nz, *refs),
        grid=(seqs, pairs),
        in_specs=[query_spec] + [lat_spec] * nz + [up_spec] * 2,
        out_specs=[
            query_spec,
            full_spec,
            full_spec,
            pl.BlockSpec((1, 1, nz, 2 * local, local), lambda s, h: (s, h, 0, 0, 0)),
        ],
        out_shape=[
            jax.ShapeDtypeStruct(queries.shape, BF16),
            full,
            full,
            jax.ShapeDtypeStruct((seqs, pairs, nz, 2 * local, local), BF16),
        ],
        compiler_params=pltpu.CompilerParams(vmem_limit_bytes=48 * 2**20),
        cost_estimate=cost("c_attend", 16e9),
        name="attend",
    )(queries, *lats, key_up, value_up)


def attend_back_kernel(nz, pairs, first, q_ref, g_ref, att_ref, key_ref, value_ref, prob_ref, *refs):
    lats, (wk_ref, wv_ref, old_ref), rest = refs[:nz], refs[nz : nz + 3], refs[nz + 3 :]
    dq_ref, dlats, (up_ref, lat_acc) = rest[0], rest[1 : nz + 1], rest[nz + 1 :]
    pair = pl.program_id(0)
    local = q_ref.shape[1]
    scale = HEAD_DIM**-0.5
    grad = g_ref[0].astype(F32)
    query = head_halves(q_ref[0].astype(F32) * scale)
    g2 = head_halves(grad)
    inner = jnp.sum(head_halves(grad * att_ref[0].astype(F32)), axis=1, keepdims=True)
    query_t, g2_t = query.T.astype(BF16), g2.T.astype(BF16)
    g2 = g2.astype(BF16)
    dq = jnp.zeros((2 * local, 128), F32)
    up_key = jnp.zeros((128, LATENT), F32)
    up_value = jnp.zeros((128, LATENT), F32)
    for k in range(nz):
        rows = slice(k * local, (k + 1) * local)
        prob = prob_ref[0, 0, k]
        key, value = key_ref[0, rows], value_ref[0, rows]
        grad_prob = dot(g2, value, COLS)
        grad_score = (prob.astype(F32) * (grad_prob - inner)).astype(BF16)
        dq = dq + dot(grad_score, key)
        grad_key = dot(query_t, grad_score).astype(BF16)
        grad_value = dot(g2_t, prob).astype(BF16)
        term = dot(wk_ref[...], grad_key) + dot(wv_ref[...], grad_value)

        @pl.when(pair == 0)
        def _():
            lat_acc[:, rows] = term

        @pl.when(pair > 0)
        def _():
            lat_acc[:, rows] += term

        lat = lats[k][0]
        up_key = up_key + dot(grad_key, lat)
        up_value = up_value + dot(grad_value, lat)
    dq_ref[0] = (join_halves(dq) * scale).astype(BF16)
    up_ref[0, 0] = up_key.T if first else up_key.T + old_ref[0, 0]
    up_ref[1, 0] = up_value.T if first else up_value.T + old_ref[1, 0]

    @pl.when(pair == pairs - 1)
    def _():
        for k in range(nz):
            dlats[k][0] = lat_acc[:, k * local : (k + 1) * local].T.astype(BF16)


def attend_back(seq, queries, grad_att, attended, keys, values, probs, lats, key_up, value_up, old):
    _, local, width = queries.shape
    nz = len(lats)
    pairs = width // 128
    query_spec = pl.BlockSpec((1, local, 128), lambda h: (seq, 0, h))
    full_spec = pl.BlockSpec((1, nz * local, 128), lambda h: (seq, 0, h))
    lat_spec = pl.BlockSpec((1, local, LATENT), lambda h: (seq, 0, 0))
    up_spec = pl.BlockSpec((LATENT, 128), lambda h: (0, h))
    prob_spec = pl.BlockSpec((1, 1, nz, 2 * local, local), lambda h: (seq, h, 0, 0, 0))
    grad_spec = pl.BlockSpec((2, 1, LATENT, 128), lambda h: (0, h, 0, 0))
    outs = pl.pallas_call(
        lambda *refs: attend_back_kernel(nz, pairs, old is None, *refs),
        grid=(pairs,),
        in_specs=[query_spec] * 3
        + [full_spec] * 2
        + [prob_spec]
        + [lat_spec] * nz
        + [up_spec] * 2
        + [pl.BlockSpec(memory_space=pl.ANY) if old is None else grad_spec],
        out_specs=[pl.BlockSpec((1, local, 128), lambda h: (0, 0, h))]
        + [pl.BlockSpec((1, local, LATENT), lambda h: (0, 0, 0))] * nz
        + [grad_spec],
        out_shape=[jax.ShapeDtypeStruct((1, local, width), BF16)]
        + [jax.ShapeDtypeStruct((1, local, LATENT), BF16)] * nz
        + [jax.ShapeDtypeStruct((2, pairs, LATENT, 128), F32)],
        scratch_shapes=[pltpu.VMEM((LATENT, nz * local), F32)],
        compiler_params=pltpu.CompilerParams(vmem_limit_bytes=48 * 2**20),
        cost_estimate=cost("c_back", 17e9),
        name="attend_back",
    )(queries, grad_att, attended, keys, values, probs, *lats, key_up, value_up,
      key_up if old is None else old)
    return outs[0], outs[1 : nz + 1], outs[nz + 1]


VMEM = pl.BlockSpec(memory_space=pltpu.VMEM)
ANY = pl.BlockSpec(memory_space=pl.ANY)
PARAMS = pltpu.CompilerParams(vmem_limit_bytes=56 * 2**20)


def chunks(width):
    return [slice(start, min(start + 256, width)) for start in range(0, width, 256)]


def row_blocks(count, body):
    @pl.loop(0, count, step=64)
    def _(start):
        body(pl.ds(pl.multiple_of(start, 64), 64))


def block_copies(size, nz, sems, make):
    copies = []
    for b in range(size):
        for a in range(size):
            for k in range(nz):
                copies.append(make(b, a, k, sems.at[(b * size + a) * nz + k]))
    for copy in copies:
        copy.start()
    return copies


def mix_heads(attended, attn_w, first):
    rows, width = attended.shape
    depth = attn_w.shape[0]
    step = rows // 4

    def kernel(att_ref, w_ref, part_ref, sent_ref):
        part = dot(att_ref[...], w_ref[:, first : first + width], COLS)
        part_ref[...] = part
        sent_ref[...] = part.astype(BF16)

    return pl.pallas_call(
        kernel,
        grid=(4,),
        in_specs=[
            pl.BlockSpec((step, width), lambda i: (i, 0)),
            pl.BlockSpec(attn_w.shape, lambda i: (0, 0)),
        ],
        out_specs=[
            pl.BlockSpec((step, depth), lambda i: (i, 0)),
            pl.BlockSpec((step, depth), lambda i: ((i + 2) % 4, 0)),
        ],
        out_shape=[
            jax.ShapeDtypeStruct((rows, depth), F32),
            jax.ShapeDtypeStruct((rows, depth), BF16),
        ],
        compiler_params=PARAMS,
        cost_estimate=cost("c_mix", 2e9),
        name="mix_heads",
    )(attended, attn_w)


def feed_forward(tokens, partial, mixed, gain, grad_low, blocks, ring):
    size = len(blocks)
    nz, block_rows, wide = blocks[0][0].shape
    rows, depth = partial.shape
    width = wide // 2
    half_z = nz // 2
    down_rows = width // (half_z * size * size)
    direct = block_rows % 16 == 0 and down_rows % 16 == 0
    flat = [block for row in blocks for block in row]
    if not direct:
        flat = [merge_blocks(blocks, ring=ring)]

    def kernel(x_ref, part_ref, mix_ref, gain_ref, go_ref, *refs):
        sources, refs = refs[: len(flat)], refs[len(flat) :]
        resid_ref, norm_ref, w_ref, gate_ref, up_ref, hid_ref = refs[:6]
        outs, (grad_ref, in_sems, out_sems) = refs[6:-3], refs[-3:]

        def fetch(b, a, k, sem):
            away = k * (2 * lax.axis_index("core") - 1) if ring else -k
            z, y, x = place(size, nz, away, -b, -a)
            start = ((z * size + y) * size + x) * block_rows
            target = w_ref.at[pl.ds(pl.multiple_of(start, 16), block_rows)]
            return pltpu.make_async_copy(sources[b * size + a].at[k], target, sem)

        if direct:
            copies = block_copies(size, nz, in_sems, fetch)
        else:
            copies = [pltpu.make_async_copy(sources[0], w_ref, in_sems.at[0])]
            copies[0].start()

        def norm(at):
            resid = x_ref[at].astype(F32) + part_ref[at] + mix_ref[at].astype(F32)
            resid_ref[at] = resid
            norm_ref[at] = (resid * inverse_rms(resid) * gain_ref[...]).astype(BF16)

        row_blocks(rows, norm)
        for copy in copies:
            copy.wait()
        normed = norm_ref[...]
        low = go_ref[...]
        for at in chunks(width):
            gate = dot(normed, w_ref[:, at])
            up = dot(normed, w_ref[:, width + at.start : width + at.stop])
            gate_ref[:, at] = gate
            up_ref[:, at] = up
            hidden = (gate * jax.nn.sigmoid(gate) * up).astype(BF16)
            hid_ref[:, at] = hidden
            grad_ref[at] = dot(hidden, low, ROWS).astype(BF16)

        def leave(b, a, k, sem):
            _, y, x = place(size, nz, 0, b, a)
            start = ((k * size + y) * size + x) * down_rows
            source = grad_ref.at[pl.ds(pl.multiple_of(start, 16), down_rows)]
            return pltpu.make_async_copy(source, outs[b].at[a, k], sem)

        if direct:
            copies = block_copies(size, half_z, out_sems, leave)
        else:
            copies = [pltpu.make_async_copy(grad_ref, outs[0], out_sems.at[0])]
            copies[0].start()
        for copy in copies:
            copy.wait()

    outs = pl.pallas_call(
        kernel,
        in_specs=[VMEM] * 5 + [ANY] * len(flat),
        out_specs=[VMEM] * 6 + [ANY] * (size if direct else 1),
        out_shape=[
            jax.ShapeDtypeStruct((rows, depth), F32),
            jax.ShapeDtypeStruct((rows, depth), BF16),
            jax.ShapeDtypeStruct((depth, wide), BF16),
            jax.ShapeDtypeStruct((rows, width), F32),
            jax.ShapeDtypeStruct((rows, width), F32),
            jax.ShapeDtypeStruct((rows, width), BF16),
        ]
        + (
            [jax.ShapeDtypeStruct((size, half_z, down_rows, depth), BF16)] * size
            if direct
            else [jax.ShapeDtypeStruct((width, depth), BF16)]
        ),
        scratch_shapes=[
            pltpu.VMEM((width, depth), BF16),
            pltpu.SemaphoreType.DMA((nz * size * size,)),
            pltpu.SemaphoreType.DMA((half_z * size * size,)),
        ],
        compiler_params=PARAMS,
        cost_estimate=cost("c_ff", 14e9),
        name="feed_forward",
    )(tokens, partial, mixed, gain, grad_low, *flat)
    parts = list(outs[6:]) if direct else split_blocks(outs[6], half_z, True)
    return (*outs[:6], list(parts))


def feed_back(gate, up, hidden, normed, grad_low, blocks):
    size = len(blocks)
    half_z, block_rows, depth = blocks[0][0].shape
    nz = half_z * 2
    rows, width = gate.shape
    wide = 2 * width
    local = rows // 2
    grad_rows = depth // (nz * size * size)
    direct = block_rows % 16 == 0 and grad_rows % 16 == 0
    flat = [block for row in blocks for block in row]
    if not direct:
        flat = [merge_blocks(blocks, True)]

    def kernel(gate_ref, up_ref, hid_ref, norm_ref, go_ref, *refs):
        sources, refs = refs[: len(flat)], refs[len(flat) :]
        grad_ref, own_ref, sent_ref = refs[:3]
        outs, (w_ref, dw_ref, norm_t, acc_ref, in_sems, out_sems) = refs[3:-6], refs[-6:]

        def fetch(b, a, k, sem):
            _, y, x = place(size, nz, 0, -b, -a)
            start = ((k * size + y) * size + x) * block_rows
            target = w_ref.at[pl.ds(pl.multiple_of(start, 16), block_rows)]
            return pltpu.make_async_copy(sources[b * size + a].at[k], target, sem)

        if direct:
            copies = block_copies(size, half_z, in_sems, fetch)
        else:
            copies = [pltpu.make_async_copy(sources[0], w_ref, in_sems.at[0])]
            copies[0].start()
        norm_t[...] = norm_ref[...].T
        for copy in copies:
            copy.wait()
        low = go_ref[...]
        for at in chunks(width):
            weights = w_ref[at]
            grad_hidden = dot(low, weights, COLS)
            gate = gate_ref[:, at]
            sigma = jax.nn.sigmoid(gate)
            grad_gate = grad_hidden * up_ref[:, at] * sigma * (1.0 + gate * (1.0 - sigma))
            grad_up = grad_hidden * (gate * sigma)
            other = slice(width + at.start, width + at.stop)
            grad_ref[:, at] = grad_gate.astype(BF16)
            grad_ref[:, other] = grad_up.astype(BF16)
            dw_ref[:, at] = dot(norm_t[...], grad_ref[:, at]).astype(BF16)
            dw_ref[:, other] = dot(norm_t[...], grad_ref[:, other]).astype(BF16)
            term = dot(hid_ref[:, at], weights)
            if at.start == 0:
                acc_ref[...] = term
            else:
                acc_ref[...] += term

        def leave(b, a, k, sem):
            z, y, x = place(size, nz, k, b, a)
            start = ((z * size + y) * size + x) * grad_rows
            source = dw_ref.at[pl.ds(pl.multiple_of(start, 16), grad_rows)]
            return pltpu.make_async_copy(source, outs[b].at[a, k], sem)

        if direct:
            copies = block_copies(size, nz, out_sems, leave)
        else:
            copies = [pltpu.make_async_copy(dw_ref, outs[0], out_sems.at[0])]
            copies[0].start()
        own_ref[...] = acc_ref[:local]
        sent_ref[...] = acc_ref[local:].astype(BF16)
        for copy in copies:
            copy.wait()

    outs = pl.pallas_call(
        kernel,
        in_specs=[VMEM] * 5 + [ANY] * len(flat),
        out_specs=[VMEM] * 3 + [ANY] * (size if direct else 1),
        out_shape=[
            jax.ShapeDtypeStruct((rows, wide), BF16),
            jax.ShapeDtypeStruct((local, depth), F32),
            jax.ShapeDtypeStruct((local, depth), BF16),
        ]
        + (
            [jax.ShapeDtypeStruct((size, nz, grad_rows, wide), BF16)] * size
            if direct
            else [jax.ShapeDtypeStruct((depth, wide), BF16)]
        ),
        scratch_shapes=[
            pltpu.VMEM((width, depth), BF16),
            pltpu.VMEM((depth, wide), BF16),
            pltpu.VMEM((depth, rows), BF16),
            pltpu.VMEM((rows, depth), F32),
            pltpu.SemaphoreType.DMA((half_z * size * size,)),
            pltpu.SemaphoreType.DMA((nz * size * size,)),
        ],
        compiler_params=PARAMS,
        cost_estimate=cost("c_fb", 18e9),
        name="feed_back",
    )(gate, up, hidden, normed, grad_low, *flat)
    parts = outs[3:] if direct else split_blocks(outs[3], nz)
    return outs[0], outs[1], outs[2], list(parts)


def resid_back(normed_part, received, resid, grad_out, gain, attended, attn_w, first):
    rows, depth = resid.shape
    width = attended.shape[1]

    def kernel(part_ref, recv_ref, resid_ref, go_ref, gain_ref, att_ref, w_ref, grad_ref, datt_ref, dw_ref, dg_ref, low_ref):
        dg_ref[...] = jnp.zeros_like(dg_ref)

        def norm(at):
            resid = resid_ref[at]
            part = part_ref[at]
            inverse = inverse_rms(resid)
            scaled = resid * inverse
            dg_ref[...] += jnp.sum(part * scaled, axis=0, keepdims=True)
            weighted = (part + recv_ref[at].astype(F32)) * gain_ref[...]
            mean = jnp.mean(weighted * scaled, axis=-1, keepdims=True)
            grad = go_ref[at] + inverse * (weighted - scaled * mean)
            grad_ref[at] = grad
            low_ref[at] = grad.astype(BF16)

        row_blocks(rows, norm)
        low = low_ref[...]
        datt_ref[...] = dot(low, w_ref[:, first : first + width]).astype(BF16)
        dw_ref[...] = dot(low, att_ref[...], ROWS).astype(BF16)

    return pl.pallas_call(
        kernel,
        in_specs=[VMEM] * 7,
        out_specs=[VMEM] * 4,
        out_shape=[
            jax.ShapeDtypeStruct((rows, depth), F32),
            jax.ShapeDtypeStruct((rows, width), BF16),
            jax.ShapeDtypeStruct((depth, width), BF16),
            jax.ShapeDtypeStruct((1, depth), F32),
        ],
        scratch_shapes=[pltpu.VMEM((rows, depth), BF16)],
        compiler_params=PARAMS,
        cost_estimate=cost("c_rb", 4e9),
        name="resid_back",
    )(normed_part, received, resid, grad_out, gain, attended, attn_w)


def half(values, which, axis=1):
    size = values.shape[axis] // 2
    return lax.dynamic_slice_in_dim(values, which * size, size, axis)


def in_order(core, own, other, axis):
    return jnp.where(
        core == 0,
        jnp.concatenate([own, other], axis=axis),
        jnp.concatenate([other, own], axis=axis),
    )


def rms_back(grad_normed, inputs, inv_rms, gain):
    weighted = grad_normed * gain
    return inv_rms * weighted - inputs * inv_rms**3 * jnp.mean(
        weighted * inputs, axis=-1, keepdims=True
    )


def inverse_rms(values):
    return lax.rsqrt(jnp.mean(values * values, axis=-1, keepdims=True) + EPSILON)


def on_device(
    tokens,
    cotangent,
    group_ids,
    loss_weight,
    gain_attn,
    w_query,
    w_latent,
    w_key_up,
    w_value_up,
    w_out,
    gain_mlp,
    w_gate,
    w_up,
    w_down,
):
    nz, ny, nx = lax.axis_size("z"), lax.axis_size("y"), lax.axis_size("x")
    core = lax.axis_index("core")
    other = 1 - core
    local, depth = tokens.shape[1:]
    latent_width = w_latent.shape[1] // 2
    hidden_width = w_gate.shape[1] // 2
    query_width = w_query.shape[1] // 2
    gain_one = gain_attn.astype(F32)
    gain_two = gain_mlp.astype(F32)

    out_t = w_out.T
    row_parts = [w_query, w_latent, out_t, w_gate, w_up]
    mine = [half(part, core) for part in row_parts]
    theirs = [half(part, other) for part in row_parts]
    attn_recv = swap(jnp.concatenate(theirs[:3], axis=1))
    ff_recv = swap(jnp.concatenate(theirs[3:], axis=1))
    down_recv = to_half(w_down, 0)
    both = swap(jnp.concatenate([tokens, cotangent], axis=0))
    onehot = (group_ids[:, None] == jnp.arange(GROUPS, dtype=jnp.int32)[None, :]).astype(F32)
    onehot_other = swap(onehot)
    attn_shard = in_order(core, jnp.concatenate(mine[:3], axis=1), attn_recv, 0)
    ff_shard = in_order(core, jnp.concatenate(mine[3:], axis=1), ff_recv, 0)
    down_chip = in_order(core, w_down, down_recv, 0)

    counts = jnp.sum(onehot, axis=0) + jnp.sum(onehot_other, axis=0)
    counts = all_sum(counts, ("x", "y"))
    attn_shard = tie("attn_z", attn_shard, both, ff_shard, down_chip, onehot_other)
    attn_z = spread_z(attn_shard)
    attn_stack = tie("attn_plane", jnp.stack(attn_z), counts, ff_shard, down_chip)
    attn_a, attn_b = spread_own(attn_stack)
    attn_blocks = spread_rest(attn_stack, attn_a, attn_b)
    ff_shard = tie("ff_z", ff_shard, attn_z, counts)
    ff_z = spread_ring(ff_shard) if OPT.get("ring", 0) else spread_z(ff_shard)
    ff_stack = tie("ff_plane", jnp.stack(ff_z), attn_a, attn_b, attn_blocks[-1][-1])
    ff_a, ff_b = spread_own(ff_stack)

    tokens_both = jnp.concatenate([tokens[0], both[0]], axis=0)
    inputs = tokens_both.astype(F32)
    inv_one = inverse_rms(inputs)
    normed_one = (inputs * inv_one * gain_one).astype(BF16)
    total_seqs = ny * nx * 2 * group_ids.shape[0]

    def factor(row):
        return jnp.sum(row * loss_weight) * (total_seqs / GROUPS) / jnp.sum(row * counts)

    grad_out = jnp.concatenate(
        [
            cotangent[0].astype(F32) * factor(onehot[0]),
            both[1].astype(F32) * factor(onehot_other[0]),
        ],
        axis=0,
    )
    grad_out_low = grad_out.astype(BF16)

    attn_w = merge_blocks(attn_blocks)
    query_w = attn_w[:, :query_width]
    latent_w = attn_w[:, query_width : query_width + latent_width]
    latent = dot(normed_one, latent_w).astype(BF16).reshape(2, local, latent_width)
    latent = tie("lat", latent, ff_z, ff_a, ff_b)
    key_up = lax.dynamic_index_in_dim(w_key_up, core, 0, keepdims=False)
    value_up = lax.dynamic_index_in_dim(w_value_up, core, 0, keepdims=False)
    lats = [latent] + [
        lax.ppermute(latent, "z", [(i, i + k) for i in range(nz - k)]) for k in range(1, nz)
    ]
    ff_blocks = spread_rest(
        ff_stack, [tie("ff_rest", part, lats, attn_blocks[-1][-1]) for part in ff_a], ff_b
    )
    ff_last = ff_blocks[-1][-1]
    down_z = spread_down_z(tie("down_z", down_chip, ff_z, lats, (ff_a, ff_b), ff_last))
    down_own = tie("down_plane", down_stack(down_z), (ff_a, ff_b), ff_last)
    down_a, down_b = spread_own(down_own)
    down_blocks = spread_rest(down_own, down_a, down_b)
    down_last = down_blocks[-1][-1]
    queries = dot(normed_one, query_w).astype(BF16).reshape(2, local, query_width)
    queries = tie("attend", queries, (ff_a, ff_b), down_z, ff_last)
    attended, keys, values, probs = attend(queries, lats, key_up, value_up)
    attended_flat = tie("post", attended, (ff_a, ff_b), ff_last, down_z, (down_a, down_b))
    attended_flat = attended_flat.reshape(2 * local, query_width)
    first = query_width + latent_width
    partial, sent = mix_heads(attended_flat, attn_w, first)
    mixed = swap(sent)

    mixed = tie("gate", mixed, down_z, (down_a, down_b), down_last)
    resid, normed_two, ff_w, gate, up_value, hidden, down_parts = feed_forward(
        tokens_both, partial, mixed, gain_two[None], grad_out_low, ff_blocks, bool(OPT.get("ring", 0))
    )
    hidden = tie("hidden", hidden, (down_a, down_b), down_last)
    down_recv = send_b(down_parts)
    gate = tie("down_w", gate, down_parts, down_last)
    grad_ff, mlp_own, mlp_sent, ff_parts = feed_back(
        gate, up_value, hidden, normed_two, grad_out_low, down_blocks
    )
    ff_recv = send_b(ff_parts)
    down_row = add_b(down_parts, down_recv)
    down_recv_a = send_a(down_row)
    normed_part = dot(tie("normed_part", grad_ff, ff_parts, down_recv), ff_w, COLS)
    received = swap(
        jnp.concatenate([normed_part[local:], normed_part[:local]], axis=0).astype(BF16)
    )
    grad_resid, grad_attended, out_rows, gain_two_part = resid_back(
        normed_part, received, resid, grad_out, gain_two[None], attended_flat, attn_w, first
    )
    gain_two_part = gain_two_part[0]

    grad_attended = grad_attended.reshape(2, local, query_width)
    down_own = add_a(down_row, down_recv_a)
    down_recv_z = send_down_z(tie("down_back_z", down_own, grad_attended))
    grad_attended = tie(
        "back_0", grad_attended, down_recv, ff_parts, down_recv_a, out_rows, down_row, down_own, ff_recv
    )
    query_0, lat_0, up_0 = attend_back(
        0, queries, grad_attended, attended, keys, values, probs, lats, key_up, value_up, None
    )
    ff_row = add_b(ff_parts, ff_recv)
    ff_recv_a = send_a(ff_row)
    ff_own = add_a(ff_row, ff_recv_a)
    grad_attended = tie(
        "back_1",
        grad_attended,
        query_0,
        down_recv_a,
        ff_recv,
        down_recv_z,
        ff_row,
        down_own,
        ff_own,
    )
    query_1, lat_1, kv_grads = attend_back(
        1, queries, grad_attended, attended, keys, values, probs, lats, key_up, value_up, up_0
    )
    gate_own, up_own = ff_own[:, :, :hidden_width], ff_own[:, :, hidden_width:]
    gate_recv_z = send_z(gate_own)
    lat_1 = tie("lat_back", list(lat_1), ff_recv, ff_row, ff_recv_a, down_recv_z, gate_recv_z)
    lat_sum = jnp.concatenate([lat_0[0], lat_1[0]], axis=0).astype(F32)
    lat_recv = []
    for k in range(1, nz):
        sent = jnp.concatenate([lat_0[k], lat_1[k]], axis=0)
        lat_recv.append(lax.ppermute(sent, "z", [(i, i - k) for i in range(k, nz)]))
    kv_flat = kv_grads.reshape(depth, -1).astype(BF16)
    kv_parts = split_blocks(tie("kv", kv_flat, ff_recv, lat_1), nz, True)
    kv_row = add_b(kv_parts, send_b(kv_parts))
    kv_own = add_a(kv_row, send_a(kv_row))
    grad_queries = jnp.concatenate([query_0[0], query_1[0]], axis=0)
    grad_queries = tie("query_back", grad_queries, ff_recv_a, lat_1, ff_own)
    query_rows = dot(normed_one, grad_queries, ROWS).astype(BF16)
    attn_parts = split_blocks(jnp.concatenate([query_rows, out_rows], axis=1), nz)
    attn_parts = tie("attn_back", list(attn_parts), ff_recv_a, kv_own, down_recv_z)
    attn_recv = send_b(attn_parts)
    attn_row = add_b(attn_parts, attn_recv)
    attn_recv_a = send_a(attn_row)
    attn_own = add_a(attn_row, attn_recv_a)
    up_recv_z = send_z(tie("ff_back_z", up_own, lat_recv, down_recv_z, kv_row, attn_recv))
    kv_z = tie("kv_z", kv_own, lat_recv, attn_recv, up_recv_z)
    kv_recv = [shift(kv_z, "z", k) for k in range(1, nz)]
    attn_recv_z = send_z(tie("attn_back_z", attn_own, up_recv_z, kv_recv, lat_recv))
    for part in lat_recv:
        lat_sum = lat_sum + part.astype(F32)
    grad_latent = lat_sum.astype(BF16)
    grad_latent = tie(
        "grad_latent", grad_latent, attn_recv, ff_recv_a, ff_own, down_recv_z, kv_row, kv_own
    ).reshape(2 * local, latent_width)
    normed_query = dot(tie("normed_query", grad_queries, attn_parts, lat_1), query_w, COLS)
    last_parts = split_blocks(dot(normed_one, grad_latent, ROWS).astype(BF16), nz)
    last_parts = tie("last_back", list(last_parts), attn_recv, attn_recv_a, up_recv_z, normed_query)
    last_recv = send_b(last_parts)
    last_row = add_b(last_parts, last_recv)
    last_recv_a = send_a(last_row)
    last_own = add_a(last_row, last_recv_a)
    last_recv_z = send_z(tie("last_back_z", last_own, up_recv_z, kv_recv, attn_recv_z))
    normed_part = normed_query + dot(
        tie("normed_last", grad_latent, last_parts, up_recv_z), latent_w, COLS
    )
    gain_one_part = jnp.sum(normed_part * inputs * inv_one, axis=0)
    gains = jnp.stack([gain_one_part, gain_two_part])
    gains = tie("gains", gains, last_parts, last_recv, attn_recv_a, up_recv_z, kv_recv)
    gains = all_sum(gains, ("core", "x", "y", "z"))
    grad_normed = normed_part[:local] + swap(normed_part[local:].astype(BF16)).astype(F32)
    input_grad = (
        grad_resid[:local] + rms_back(grad_normed, inputs[:local], inv_one[:local], gain_one)
    ).astype(BF16)[None]
    mlp_sent = tie("mlp", mlp_sent, ff_parts, grad_attended, attn_parts)
    result = (resid[:local] + mlp_own + swap(mlp_sent).astype(F32)).astype(BF16)[None]
    kv_sum = kv_z.astype(F32)
    for part in kv_recv:
        kv_sum = kv_sum + part.astype(F32)
    kv_sum = tie("kv_spread", kv_sum.astype(BF16), last_parts, attn_recv, attn_recv_a)
    kv_a, kv_b = spread_own(kv_sum)
    kv_all = merge_blocks(spread_rest(kv_sum, kv_a, kv_b), fixed=True)
    kv_pair = in_order(core, kv_all[None], swap(kv_all)[None], 0).astype(F32)
    kv_pair = kv_pair.reshape((2,) + kv_grads.shape).transpose(1, 0, 3, 2, 4)
    kv_pair = kv_pair.reshape(2, KV_GROUPS, LATENT, query_width)

    def owned(totals):
        joined = jnp.concatenate(totals, axis=1).astype(BF16)
        received = swap(half(joined, other, 0))
        mine = half(joined, core, 0)
        results, start = [], 0
        for total in totals:
            width = total.shape[1]
            results.append(
                in_order(core, mine[:, start : start + width], received[:, start : start + width], 1)
                .astype(F32)
            )
            start += width
        return results

    owned_gate, owned_up = owned([add_z(gate_own, gate_recv_z), add_z(up_own, up_recv_z)])
    owned_down = own_down(down_own, tie("down_last", down_recv_z, attn_recv, lat_recv))
    attn_total = add_z(attn_own, attn_recv_z)
    owned_query, owned_out = owned([attn_total[:, :query_width], attn_total[:, query_width:]])
    (owned_latent,) = owned([add_z(last_own, last_recv_z)])
    return (
        result,
        input_grad,
        gains[0],
        owned_query,
        owned_latent,
        kv_pair[0],
        kv_pair[1],
        owned_out.T,
        gains[1],
        owned_gate,
        owned_up,
        owned_down,
    )


def solution(mesh):
    nz = mesh.shape["seq"]
    chips = mesh.shape["batch"] // 2
    nx = math.isqrt(chips)
    while chips % nx:
        nx -= 1
    fine = Mesh(mesh.devices.reshape(nz, chips // nx, nx, 2), ("z", "y", "x", "core"))
    batch = ("y", "x", "core")
    every = ("z",) + batch
    by_rows = P(every, None)
    in_specs = (
        P(batch, "z", None),
        P(batch, "z", None),
        P(batch),
        P(),
        P(),
        by_rows,
        by_rows,
        P(),
        P(),
        P(None, every),
        P(),
        by_rows,
        by_rows,
        by_rows,
    )
    out_specs = (
        P(batch, "z", None),
        P(batch, "z", None),
        P(),
        by_rows,
        by_rows,
        P(),
        P(),
        P(None, every),
        P(),
        by_rows,
        by_rows,
        by_rows,
    )
    return jax.shard_map(
        on_device, mesh=fine, in_specs=in_specs, out_specs=out_specs, check_vma=False
    )
```

```python
import math

import jax
import jax.numpy as jnp
from jax import lax
from jax.experimental import pallas as pl
from jax.experimental.pallas import tpu as pltpu
from jax.sharding import Mesh
from jax.sharding import PartitionSpec as P

HEADS = 16
HEAD_DIM = 64
LATENT = 256
KV_GROUPS = 2
GROUPS = 4
EPSILON = 1e-06
BF16 = jnp.bfloat16
F32 = jnp.float32
ROWS = (((0,), (0,)), ((), ()))
OPT = {"attn_z": 13, "back_0": 16, "back_1": 80, "c_attend": 4, "c_back": 3, "c_fb": 3, "c_ff": 3, "c_merge": 4, "c_mix": 2, "c_nb": 2, "c_rb": 4, "c_split": 4, "down_last": 2, "down_plane": 3, "down_z": 2, "ff_back_z": 8, "ff_plane": 8, "ff_z": 2, "gains": 4, "gate_row": 1, "kv": 2, "kv_spread": 5, "kv_sum": 3, "kv_z": 3, "lat_back": 28, "normed_last": 1, "normed_part": 1, "query_back": 2, "up_b": 1, "up_last": 1}
COLS = (((1,), (1,)), ((), ()))
PLAIN = (((1,), (0,)), ((), ()))


def dot(a, b, dims=PLAIN):
    return lax.dot_general(a, b, dims, preferred_element_type=F32)


PLANE = ("y", "x", "core")


def shift(values, axis, step):
    size = lax.axis_size(axis)
    return lax.ppermute(values, axis, [(i, (i + step) % size) for i in range(size)])


def leg(values, first, step):
    size = lax.axis_size("x")
    pairs = []
    for y in range(size):
        for x in range(size):
            for core in range(2):
                if (core == 0) == first:
                    target = (y, (x + step) % size, core)
                else:
                    target = ((y + step) % size, x, core)
                pairs.append(
                    ((y * size + x) * 2 + core, (target[0] * size + target[1]) * 2 + target[2])
                )
    return lax.ppermute(values, PLANE, pairs)


def swap(values):
    return shift(values, "core", 1)


def spread_z(shard):
    return [shard] + [shift(shard, "z", k) for k in range(1, lax.axis_size("z"))]


def spread_ring(shard):
    nz = lax.axis_size("z")
    pairs = [(z * 2 + c, (z + 1 - 2 * c) % nz * 2 + c) for z in range(nz) for c in range(2)]
    blocks = [shard]
    for _ in range(nz - 1):
        blocks.append(lax.ppermute(blocks[-1], ("z", "core"), pairs))
    return blocks


def spread_own(stack, late=None):
    size = lax.axis_size("x")
    late = stack if late is None else late
    return (
        [leg(stack, True, a) for a in range(1, size)],
        [leg(late, False, b) for b in range(1, size)],
    )


def spread_rest(stack, on_a, on_b):
    size = lax.axis_size("x")
    return [[stack] + on_a] + [
        [on_b[b - 1]] + [leg(block, False, b) for block in on_a] for b in range(1, size)
    ]


def after(value, *others):
    return lax.optimization_barrier((value,) + others)[0]


def tie(name, value, *others):
    mask = OPT.get(name, 0)
    chosen = [other for i, other in enumerate(others) if mask >> i & 1]
    return after(value, *chosen) if chosen else value


def cost(name, flops):
    return pl.CostEstimate(
        flops=int(flops * OPT.get(name, 0) / 4), bytes_accessed=4096, transcendentals=0
    )


def send_b(parts):
    return [leg(parts[b], False, b) for b in range(1, len(parts))]


def add_b(parts, received):
    row = parts[0]
    for part in received:
        row = add(row, part)
    return row


def send_a(row):
    return [leg(row[a], True, a) for a in range(1, row.shape[0])]


def add_a(row, received):
    own = row[0]
    for part in received:
        own = add(own, part)
    return own


RING = bool(OPT.get("ring_back", 0))


def ring(values):
    nz = lax.axis_size("z")
    pairs = [(z * 2 + c, (z + 1 - 2 * c) % nz * 2 + c) for z in range(nz) for c in range(2)]
    return lax.ppermute(values, ("z", "core"), pairs)


def back_away(k):
    return k * (2 * lax.axis_index("core") - 1) if RING else k


def send_z(own):
    if not RING:
        return [shift(own[k], "z", k) for k in range(1, own.shape[0])]
    part = own[1]
    for k in range(2, own.shape[0]):
        part = add(own[k], ring(part))
    return [ring(part)]


def add_z(own, received):
    total = own[0].astype(F32)
    for part in received:
        total = total + part.astype(F32)
    return total


def add(left, right):
    return (left.astype(F32) + right.astype(F32)).astype(BF16)


def to_half(values, step):
    nz = lax.axis_size("z")
    pairs = []
    for z in range(nz):
        keeper = z // (nz // 2)
        source = z * 2 + (keeper if step else 1 - keeper)
        pairs.append((source, (z + step) % nz * 2 + keeper))
    return lax.ppermute(values, ("z", "core"), pairs)


def spread_down_z(chip):
    nz, z, core = lax.axis_size("z"), lax.axis_index("z"), lax.axis_index("core")
    return [chip] + [to_half(chip, k) for k in range(1, nz)]


def down_stack(received):
    nz, z, core = lax.axis_size("z"), lax.axis_index("z"), lax.axis_index("core")
    received = jnp.stack(received)
    parts = []
    for j in range(nz // 2):
        step = lax.rem(z + nz - core * (nz // 2) - j, nz)
        parts.append(lax.dynamic_slice_in_dim(received, step, 1, 0))
    return jnp.concatenate(parts, axis=0)


def down_block(own, chip_z):
    count = own.shape[0]
    index = jnp.clip(chip_z - lax.axis_index("core") * count, 0, count - 1)
    return lax.dynamic_index_in_dim(own, index, 0, keepdims=False)


def send_down_z(own):
    nz, z, count = lax.axis_size("z"), lax.axis_index("z"), own.shape[0]
    received = []
    for k in range(1, nz):
        pairs = [((d + k) % nz * 2 + d // count, d * 2 + d // count) for d in range(nz)]
        part = down_block(own, lax.rem(z + nz - k, nz))
        received.append(lax.ppermute(part, ("z", "core"), pairs))
    return received


def own_down(own, received):
    nz, z, core = lax.axis_size("z"), lax.axis_index("z"), lax.axis_index("core")
    count = nz // 2
    total = down_block(own, z).astype(F32)
    for part in received:
        total = total + part.astype(F32)
    pairs = [(d * 2 + d // count, d * 2 + 1 - d // count) for d in range(nz)]
    sent = lax.ppermute(half(total, 1 - core, 0).astype(BF16), ("z", "core"), pairs)
    return jnp.where(core == z // count, half(total, core, 0), sent.astype(F32))


def place(size, nz, k, b, a):
    core = lax.axis_index("core")
    z = lax.rem(lax.axis_index("z") + nz + k, nz)
    y = lax.rem(lax.axis_index("y") + size + b + core * (a - b), size)
    x = lax.rem(lax.axis_index("x") + size + a + core * (b - a), size)
    return z, y, x


def merge_blocks(blocks, fixed=False, ring=False):
    size = len(blocks)
    nz, rows, columns = blocks[0][0].shape
    parts = [block for row in blocks for block in row]

    def kernel(*refs):
        out, sems = refs[-2], refs[-1]
        copies = []
        for b in range(size):
            for a in range(size):
                for k in range(nz):
                    away = k * (2 * lax.axis_index("core") - 1) if ring else -k
                    z, y, x = place(size, nz, away, -b, -a)
                    n = b * size + a
                    copies.append(
                        pltpu.make_async_copy(
                            refs[n].at[k], out.at[k if fixed else z, y, x], sems.at[n * nz + k]
                        )
                    )
        for copy in copies:
            copy.start()
        for copy in copies:
            copy.wait()

    out = pl.pallas_call(
        kernel,
        out_shape=jax.ShapeDtypeStruct((nz, size, size, rows, columns), parts[0].dtype),
        in_specs=[pl.BlockSpec(memory_space=pl.ANY)] * len(parts),
        out_specs=pl.BlockSpec(memory_space=pltpu.VMEM),
        scratch_shapes=[pltpu.SemaphoreType.DMA((nz * size * size,))],
        compiler_params=pltpu.CompilerParams(vmem_limit_bytes=48 * 2**20),
        cost_estimate=cost("c_merge", 3e9),
        name="merge",
    )(*parts)
    return out.reshape(nz * size * size * rows, columns)


def split_blocks(full, nz, fixed=False):
    size = lax.axis_size("x")
    rows = full.shape[0] // (nz * size * size)
    columns = full.shape[1]

    def kernel(*refs):
        source, outs, sems = refs[0], refs[1:-1], refs[-1]
        copies = []
        for b in range(size):
            for a in range(size):
                for k in range(nz):
                    z, y, x = place(size, nz, back_away(k), b, a)
                    copies.append(
                        pltpu.make_async_copy(
                            source.at[k if fixed else z, y, x],
                            outs[b].at[a, k],
                            sems.at[(b * size + a) * nz + k],
                        )
                    )
        for copy in copies:
            copy.start()
        for copy in copies:
            copy.wait()

    return pl.pallas_call(
        kernel,
        out_shape=[jax.ShapeDtypeStruct((size, nz, rows, columns), full.dtype)] * size,
        in_specs=[pl.BlockSpec(memory_space=pltpu.VMEM)],
        out_specs=[pl.BlockSpec(memory_space=pl.ANY)] * size,
        scratch_shapes=[pltpu.SemaphoreType.DMA((nz * size * size,))],
        compiler_params=pltpu.CompilerParams(vmem_limit_bytes=48 * 2**20),
        cost_estimate=cost("c_split", 3e9),
        name="split",
    )(full.reshape(nz, size, size, rows, columns))


def all_sum(values, axes):
    for axis in axes:
        size = lax.axis_size(axis)
        total = values
        for k in range(1, size):
            total = total + shift(values, axis, k)
        values = total
    return values


def head_halves(pair):
    lane = lax.broadcasted_iota(jnp.int32, pair.shape, 1)
    zero = jnp.zeros_like(pair)
    return jnp.concatenate(
        [jnp.where(lane < HEAD_DIM, pair, zero), jnp.where(lane >= HEAD_DIM, pair, zero)], axis=0
    )


def join_halves(halves):
    rows = halves.shape[0] // 2
    lane = lax.broadcasted_iota(jnp.int32, (rows, halves.shape[1]), 1)
    return jnp.where(lane < HEAD_DIM, halves[:rows], halves[rows:])


def attend_kernel(nz, q_ref, *refs):
    lats, (wk_ref, wv_ref, att_ref, key_ref, value_ref, prob_ref) = refs[:nz], refs[nz:]
    local = q_ref.shape[1]
    z = lax.axis_index("z")
    q2 = head_halves(q_ref[0] * BF16(HEAD_DIM**-0.5))
    wk, wv = wk_ref[...], wv_ref[...]
    scores = []
    for k in range(nz):
        lat = lats[k][0]
        key = dot(lat, wk).astype(BF16)
        value = dot(lat, wv).astype(BF16)
        key_ref[0, k * local : (k + 1) * local] = key
        value_ref[0, k * local : (k + 1) * local] = value
        block = dot(q2, key, COLS)
        if k == 0:
            row = lax.rem(lax.broadcasted_iota(jnp.int32, block.shape, 0), local)
            column = lax.broadcasted_iota(jnp.int32, block.shape, 1)
            block = jnp.where(column <= row, block, -1e30)
        else:
            block = block + jnp.where(z >= k, 0.0, -1e30)
        scores.append(block)
    top = scores[0]
    for block in scores[1:]:
        top = jnp.maximum(top, block)
    top = jnp.max(top, axis=1, keepdims=True)
    exps = [jnp.exp(block - top) for block in scores]
    total = exps[0]
    for block in exps[1:]:
        total = total + block
    inverse = 1.0 / jnp.sum(total, axis=1, keepdims=True)
    mixed = jnp.zeros((2 * local, q_ref.shape[2]), F32)
    for k in range(nz):
        prob = (exps[k] * inverse).astype(BF16)
        prob_ref[0, 0, k] = prob
        mixed = mixed + dot(prob, value_ref[0, k * local : (k + 1) * local])
    att_ref[0] = join_halves(mixed).astype(BF16)


def attend(queries, lats, key_up, value_up):
    seqs, local, width = queries.shape
    nz = len(lats)
    pairs = width // 128
    query_spec = pl.BlockSpec((1, local, 128), lambda s, h: (s, 0, h))
    full_spec = pl.BlockSpec((1, nz * local, 128), lambda s, h: (s, 0, h))
    lat_spec = pl.BlockSpec((1, local, LATENT), lambda s, h: (s, 0, 0))
    up_spec = pl.BlockSpec((LATENT, 128), lambda s, h: (0, h))
    full = jax.ShapeDtypeStruct((seqs, nz * local, width), BF16)
    return pl.pallas_call(
        lambda *refs: attend_kernel(nz, *refs),
        grid=(seqs, pairs),
        in_specs=[query_spec] + [lat_spec] * nz + [up_spec] * 2,
        out_specs=[
            query_spec,
            full_spec,
            full_spec,
            pl.BlockSpec((1, 1, nz, 2 * local, local), lambda s, h: (s, h, 0, 0, 0)),
        ],
        out_shape=[
            jax.ShapeDtypeStruct(queries.shape, BF16),
            full,
            full,
            jax.ShapeDtypeStruct((seqs, pairs, nz, 2 * local, local), BF16),
        ],
        compiler_params=pltpu.CompilerParams(vmem_limit_bytes=48 * 2**20),
        cost_estimate=cost("c_attend", 16e9),
        name="attend",
    )(queries, *lats, key_up, value_up)


def attend_back_kernel(nz, pairs, first, q_ref, g_ref, att_ref, key_ref, value_ref, prob_ref, *refs):
    lats, (wk_ref, wv_ref, old_ref), rest = refs[:nz], refs[nz : nz + 3], refs[nz + 3 :]
    dq_ref, dlats, (up_ref, lat_acc) = rest[0], rest[1 : nz + 1], rest[nz + 1 :]
    pair = pl.program_id(0)
    local = q_ref.shape[1]
    scale = HEAD_DIM**-0.5
    grad = g_ref[0].astype(F32)
    query = head_halves(q_ref[0].astype(F32) * scale)
    g2 = head_halves(grad)
    inner = jnp.sum(head_halves(grad * att_ref[0].astype(F32)), axis=1, keepdims=True)
    query_t, g2_t = query.T.astype(BF16), g2.T.astype(BF16)
    g2 = g2.astype(BF16)
    @pl.when(pair == 0)
    def _():
        lat_acc[...] = jnp.zeros_like(lat_acc)

    dq = jnp.zeros((2 * local, 128), F32)
    up_key = jnp.zeros((128, LATENT), F32)
    up_value = jnp.zeros((128, LATENT), F32)
    for k in range(nz):
        rows = slice(k * local, (k + 1) * local)
        prob = prob_ref[0, 0, k]
        key, value = key_ref[0, rows], value_ref[0, rows]
        grad_prob = dot(g2, value, COLS)
        grad_score = (prob.astype(F32) * (grad_prob - inner)).astype(BF16)
        dq = dq + dot(grad_score, key)
        grad_key = dot(query_t, grad_score).astype(BF16)
        grad_value = dot(g2_t, prob).astype(BF16)
        term = dot(wk_ref[...], grad_key) + dot(wv_ref[...], grad_value)

        lat_acc[:, rows] += term
        lat = lats[k][0]
        up_key = up_key + dot(grad_key, lat)
        up_value = up_value + dot(grad_value, lat)
    dq_ref[0] = (join_halves(dq) * scale).astype(BF16)
    up_ref[0, 0] = up_key.T if first else up_key.T + old_ref[0, 0]
    up_ref[1, 0] = up_value.T if first else up_value.T + old_ref[1, 0]

    @pl.when(pair == pairs - 1)
    def _():
        for k in range(nz):
            dlats[k][0] = lat_acc[:, k * local : (k + 1) * local].T.astype(BF16)


def attend_back(seq, queries, grad_att, attended, keys, values, probs, lats, key_up, value_up, old):
    _, local, width = queries.shape
    nz = len(lats)
    pairs = width // 128
    query_spec = pl.BlockSpec((1, local, 128), lambda h: (seq, 0, h))
    full_spec = pl.BlockSpec((1, nz * local, 128), lambda h: (seq, 0, h))
    lat_spec = pl.BlockSpec((1, local, LATENT), lambda h: (seq, 0, 0))
    up_spec = pl.BlockSpec((LATENT, 128), lambda h: (0, h))
    prob_spec = pl.BlockSpec((1, 1, nz, 2 * local, local), lambda h: (seq, h, 0, 0, 0))
    grad_spec = pl.BlockSpec((2, 1, LATENT, 128), lambda h: (0, h, 0, 0))
    outs = pl.pallas_call(
        lambda *refs: attend_back_kernel(nz, pairs, old is None, *refs),
        grid=(pairs,),
        in_specs=[query_spec] * 3
        + [full_spec] * 2
        + [prob_spec]
        + [lat_spec] * nz
        + [up_spec] * 2
        + [pl.BlockSpec(memory_space=pl.ANY) if old is None else grad_spec],
        out_specs=[pl.BlockSpec((1, local, 128), lambda h: (0, 0, h))]
        + [pl.BlockSpec((1, local, LATENT), lambda h: (0, 0, 0))] * nz
        + [grad_spec],
        out_shape=[jax.ShapeDtypeStruct((1, local, width), BF16)]
        + [jax.ShapeDtypeStruct((1, local, LATENT), BF16)] * nz
        + [jax.ShapeDtypeStruct((2, pairs, LATENT, 128), F32)],
        scratch_shapes=[pltpu.VMEM((LATENT, nz * local), F32)],
        compiler_params=pltpu.CompilerParams(vmem_limit_bytes=48 * 2**20),
        cost_estimate=cost("c_back", 17e9),
        name="attend_back",
    )(queries, grad_att, attended, keys, values, probs, *lats, key_up, value_up,
      key_up if old is None else old)
    return outs[0], outs[1 : nz + 1], outs[nz + 1]


VMEM = pl.BlockSpec(memory_space=pltpu.VMEM)
ANY = pl.BlockSpec(memory_space=pl.ANY)
PARAMS = pltpu.CompilerParams(vmem_limit_bytes=56 * 2**20)


def chunks(width):
    return [slice(start, min(start + 256, width)) for start in range(0, width, 256)]


def row_blocks(count, body):
    @pl.loop(0, count, step=64)
    def _(start):
        body(pl.ds(pl.multiple_of(start, 64), 64))


def block_copies(size, nz, sems, make):
    copies = []
    for b in range(size):
        for a in range(size):
            for k in range(nz):
                copies.append(make(b, a, k, sems.at[(b * size + a) * nz + k]))
    for copy in copies:
        copy.start()
    return copies


def mix_heads(attended, attn_w, first):
    rows, width = attended.shape
    depth = attn_w.shape[0]
    local = rows // 2

    def kernel(att_ref, w_ref, sent_ref, out_w, sem):
        copy = pltpu.make_async_copy(w_ref.at[:, pl.ds(first, width)], out_w, sem)
        copy.start()
        copy.wait()
        sent_ref[:local] = dot(att_ref[local:], out_w[...], COLS).astype(BF16)
        sent_ref[local:] = dot(att_ref[:local], out_w[...], COLS).astype(BF16)

    return pl.pallas_call(
        kernel,
        in_specs=[VMEM, ANY],
        out_specs=VMEM,
        out_shape=jax.ShapeDtypeStruct((rows, depth), BF16),
        scratch_shapes=[pltpu.VMEM((depth, width), BF16), pltpu.SemaphoreType.DMA],
        compiler_params=pltpu.CompilerParams(vmem_limit_bytes=16 * 2**20),
        cost_estimate=cost("c_mix", 2e9),
        name="mix_heads",
    )(attended, attn_w)


def feed_forward(tokens, attended, attn_w, first, mixed, gain, grad_low, blocks):
    size = len(blocks)
    nz, block_rows, wide = blocks[0][0].shape
    rows, heads_width = attended.shape
    depth = tokens.shape[1]
    width = wide // 2
    half_z = nz // 2
    down_rows = width // (half_z * size * size)
    direct = block_rows % 16 == 0 and down_rows % 16 == 0
    flat = [block for row in blocks for block in row]
    if not direct:
        flat = [merge_blocks(blocks)]
    shapes = [
        ((rows, depth), F32),
        ((rows, depth), BF16),
        ((depth, wide), BF16),
        ((rows, width), BF16),
        ((rows, width), BF16),
        ((rows, width), BF16),
    ]

    def kernel(x_ref, att_ref, mix_ref, gain_ref, go_ref, attn_ref, *refs):
        sources, refs = refs[: len(flat)], refs[len(flat) :]
        leaving, outs = refs[:6], refs[6 : 6 + (size if direct else 1)]
        held, (out_w, grad_ref, sem, held_sems, in_sems, out_sems) = refs[-12:-6], refs[-6:]
        resid_ref, norm_ref, w_ref, gate_ref, up_ref, hid_ref = held

        def fetch(b, a, k, sem):
            z, y, x = place(size, nz, -k, -b, -a)
            start = ((z * size + y) * size + x) * block_rows
            target = w_ref.at[pl.ds(pl.multiple_of(start, 16), block_rows)]
            return pltpu.make_async_copy(sources[b * size + a].at[k], target, sem)

        first_copy = pltpu.make_async_copy(attn_ref.at[:, pl.ds(first, heads_width)], out_w, sem)
        first_copy.start()
        if direct:
            copies = block_copies(size, nz, in_sems, fetch)
        else:
            copies = [pltpu.make_async_copy(sources[0], w_ref, in_sems.at[0])]
            copies[0].start()
        out_copies = [
            pltpu.make_async_copy(held[i], leaving[i], held_sems.at[i]) for i in range(6)
        ]
        first_copy.wait()
        resid_ref[...] = dot(att_ref[...], out_w[...], COLS)

        def norm(at):
            resid = x_ref[at].astype(F32) + resid_ref[at] + mix_ref[at].astype(F32)
            resid_ref[at] = resid
            norm_ref[at] = (resid * inverse_rms(resid) * gain_ref[...]).astype(BF16)

        row_blocks(rows, norm)
        out_copies[0].start()
        out_copies[1].start()
        for copy in copies:
            copy.wait()
        out_copies[2].start()
        normed = norm_ref[...]
        low = go_ref[...]
        for at in chunks(width):
            gate = dot(normed, w_ref[:, at])
            up = dot(normed, w_ref[:, width + at.start : width + at.stop])
            gate_ref[:, at] = gate.astype(BF16)
            up_ref[:, at] = up.astype(BF16)
            hid_ref[:, at] = (gate * jax.nn.sigmoid(gate) * up).astype(BF16)
        for copy in out_copies[3:]:
            copy.start()
        for at in chunks(width):
            grad_ref[at] = dot(hid_ref[:, at], low, ROWS).astype(BF16)

        def leave(b, a, k, sem):
            _, y, x = place(size, nz, 0, b, a)
            start = ((k * size + y) * size + x) * down_rows
            source = grad_ref.at[pl.ds(pl.multiple_of(start, 16), down_rows)]
            return pltpu.make_async_copy(source, outs[b].at[a, k], sem)

        if direct:
            copies = block_copies(size, half_z, out_sems, leave)
        else:
            copies = [pltpu.make_async_copy(grad_ref, outs[0], out_sems.at[0])]
            copies[0].start()
        for copy in copies + out_copies:
            copy.wait()

    outs = pl.pallas_call(
        kernel,
        in_specs=[VMEM] * 5 + [ANY] * (1 + len(flat)),
        out_specs=[ANY] * (6 + (size if direct else 1)),
        out_shape=[jax.ShapeDtypeStruct(*shape) for shape in shapes]
        + (
            [jax.ShapeDtypeStruct((size, half_z, down_rows, depth), BF16)] * size
            if direct
            else [jax.ShapeDtypeStruct((width, depth), BF16)]
        ),
        scratch_shapes=[pltpu.VMEM(*shape) for shape in shapes]
        + [
            pltpu.VMEM((depth, heads_width), BF16),
            pltpu.VMEM((width, depth), BF16),
            pltpu.SemaphoreType.DMA,
            pltpu.SemaphoreType.DMA((6,)),
            pltpu.SemaphoreType.DMA((nz * size * size,)),
            pltpu.SemaphoreType.DMA((half_z * size * size,)),
        ],
        compiler_params=PARAMS,
        cost_estimate=cost("c_ff", 14e9),
        name="feed_forward",
    )(tokens, attended, mixed, gain, grad_low, attn_w, *flat)
    parts = list(outs[6:]) if direct else split_blocks(outs[6], half_z, True)
    return (*outs[:6], list(parts))


def feed_back(gate, up, hidden, normed, grad_low, blocks):
    size = len(blocks)
    half_z, block_rows, depth = blocks[0][0].shape
    nz = half_z * 2
    rows, width = gate.shape
    wide = 2 * width
    local = rows // 2
    grad_rows = depth // (nz * size * size)
    direct = block_rows % 16 == 0 and grad_rows % 16 == 0
    flat = [block for row in blocks for block in row]
    if not direct:
        flat = [merge_blocks(blocks, True)]
    parts = chunks(width)

    def kernel(norm_ref, go_ref, gate_in, up_in, hid_in, *refs):
        sources, refs = refs[: len(flat)], refs[len(flat) :]
        grad_out, own_ref, sent_ref = refs[:3]
        outs, refs = refs[3:-9], refs[-9:]
        w_ref, dw_ref, gate_ref, up_ref, hid_ref, grad_ref, sems, in_sems, out_sems = refs

        def fetch(b, a, k, sem):
            _, y, x = place(size, nz, 0, -b, -a)
            start = ((k * size + y) * size + x) * block_rows
            target = w_ref.at[pl.ds(pl.multiple_of(start, 16), block_rows)]
            return pltpu.make_async_copy(sources[b * size + a].at[k], target, sem)

        if direct:
            copies = block_copies(size, half_z, in_sems, fetch)
        else:
            copies = [pltpu.make_async_copy(sources[0], w_ref, in_sems.at[0])]
            copies[0].start()
        arriving = []
        for i, at in enumerate(parts):
            span = pl.ds(at.start, at.stop - at.start)
            arriving.append(
                [
                    pltpu.make_async_copy(source.at[:, span], target.at[:, span], sems.at[3 * i + j])
                    for j, (source, target) in enumerate(
                        ((gate_in, gate_ref), (up_in, up_ref), (hid_in, hid_ref))
                    )
                ]
            )
            for copy in arriving[-1]:
                copy.start()
        normed = norm_ref[...]
        for copy in copies:
            copy.wait()
        low = go_ref[...]
        for i, at in enumerate(parts):
            for copy in arriving[i]:
                copy.wait()
            grad_hidden = dot(low, w_ref[at], COLS)
            gate = gate_ref[:, at].astype(F32)
            sigma = jax.nn.sigmoid(gate)
            grad_gate = grad_hidden * up_ref[:, at].astype(F32) * sigma * (1.0 + gate * (1.0 - sigma))
            grad_up = grad_hidden * (gate * sigma)
            other = slice(width + at.start, width + at.stop)
            grad_ref[:, at] = grad_gate.astype(BF16)
            grad_ref[:, other] = grad_up.astype(BF16)
            dw_ref[:, at] = dot(normed, grad_ref[:, at], ROWS).astype(BF16)
            dw_ref[:, other] = dot(normed, grad_ref[:, other], ROWS).astype(BF16)

        def leave(part):
            def make(b, a, k, sem):
                z, y, x = place(size, nz, back_away(k), b, a)
                start = ((z * size + y) * size + x) * grad_rows
                rows_at = pl.ds(pl.multiple_of(start, 16), grad_rows)
                source = dw_ref.at[rows_at, pl.ds(part * width, width)]
                return pltpu.make_async_copy(source, outs[part * size + b].at[a, k], sem)

            return make

        if direct:
            copies = []
            for part in range(2):
                copies += block_copies(size, nz, out_sems.at[part], leave(part))
        else:
            copies = []
            for part in range(2):
                source = dw_ref.at[:, pl.ds(part * width, width)]
                copies.append(pltpu.make_async_copy(source, outs[part], out_sems.at[part, 0]))
                copies[-1].start()
        last = pltpu.make_async_copy(grad_ref, grad_out, sems.at[3 * len(parts)])
        last.start()
        own_ref[...] = dot(hid_ref[:local], w_ref[...])
        sent_ref[...] = dot(hid_ref[local:], w_ref[...]).astype(BF16)
        for copy in copies + [last]:
            copy.wait()

    outs = pl.pallas_call(
        kernel,
        in_specs=[VMEM] * 2 + [ANY] * (3 + len(flat)),
        out_specs=[ANY] + [VMEM] * 2 + [ANY] * (2 * size if direct else 2),
        out_shape=[
            jax.ShapeDtypeStruct((rows, wide), BF16),
            jax.ShapeDtypeStruct((local, depth), F32),
            jax.ShapeDtypeStruct((local, depth), BF16),
        ]
        + (
            [jax.ShapeDtypeStruct((size, nz, grad_rows, width), BF16)] * (2 * size)
            if direct
            else [jax.ShapeDtypeStruct((depth, width), BF16)] * 2
        ),
        scratch_shapes=[
            pltpu.VMEM((width, depth), BF16),
            pltpu.VMEM((depth, wide), BF16),
            pltpu.VMEM((rows, width), BF16),
            pltpu.VMEM((rows, width), BF16),
            pltpu.VMEM((rows, width), BF16),
            pltpu.VMEM((rows, wide), BF16),
            pltpu.SemaphoreType.DMA((3 * len(parts) + 1,)),
            pltpu.SemaphoreType.DMA((half_z * size * size,)),
            pltpu.SemaphoreType.DMA((2, nz * size * size)),
        ],
        compiler_params=PARAMS,
        cost_estimate=cost("c_fb", 18e9),
        name="feed_back",
    )(normed, grad_low, gate, up, hidden, *flat)
    if direct:
        parts = [list(outs[3 : 3 + size]), list(outs[3 + size :])]
    else:
        parts = [list(split_blocks(part, nz)) for part in outs[3:]]
    return outs[0], outs[1], outs[2], *parts


def norm_back(grad_ff, ff_w):
    rows, wide = grad_ff.shape
    depth = ff_w.shape[0]
    local = rows // 2

    def kernel(grad_ref, w_ref, part_ref, sent_ref):
        for at in chunks(depth):
            part = dot(grad_ref[...], w_ref[at], COLS)
            part_ref[:, at] = part
            sent_ref[:local, at] = part[local:].astype(BF16)
            sent_ref[local:, at] = part[:local].astype(BF16)

    return pl.pallas_call(
        kernel,
        in_specs=[VMEM] * 2,
        out_specs=[VMEM] * 2,
        out_shape=[
            jax.ShapeDtypeStruct((rows, depth), F32),
            jax.ShapeDtypeStruct((rows, depth), BF16),
        ],
        compiler_params=pltpu.CompilerParams(vmem_limit_bytes=32 * 2**20),
        cost_estimate=cost("c_nb", 6e9),
        name="norm_back",
    )(grad_ff, ff_w)


def resid_back(normed_part, received, resid, cotangents, factors, gain, attended, attn_w, first):
    rows, depth = resid.shape
    width = attended.shape[1]
    local = rows // 2

    def kernel(part_ref, recv_ref, resid_ref, cot_ref, gain_ref, att_ref, fac_ref, w_ref, *refs):
        grad_ref, datt_ref, dw_ref, dg_ref, low_ref, sum_ref, out_w, sem = refs
        copy = pltpu.make_async_copy(w_ref.at[:, pl.ds(first, width)], out_w, sem)
        copy.start()
        sum_ref[...] = jnp.zeros_like(sum_ref)

        def norm(at):
            resid = resid_ref[at]
            part = part_ref[at]
            inverse = inverse_rms(resid)
            scaled = resid * inverse
            gains = part * scaled
            total = gains[:8]
            for row in range(8, 64, 8):
                total = total + gains[row : row + 8]
            sum_ref[...] += total
            weighted = (part + recv_ref[at].astype(F32)) * gain_ref[...]
            mean = jnp.mean(weighted * scaled, axis=-1, keepdims=True)
            factor = jnp.where(at.start < local, fac_ref[0], fac_ref[1])
            grad = cot_ref[at].astype(F32) * factor + inverse * (weighted - scaled * mean)
            low_ref[at] = grad.astype(BF16)

            @pl.when(at.start < local)
            def _():
                grad_ref[at] = grad

        row_blocks(rows, norm)
        dg_ref[...] = jnp.sum(sum_ref[...], axis=0, keepdims=True)
        copy.wait()
        low = low_ref[...]
        datt_ref[...] = dot(low, out_w[...]).astype(BF16)
        dw_ref[...] = dot(low, att_ref[...], ROWS).astype(BF16)

    return pl.pallas_call(
        kernel,
        in_specs=[VMEM] * 6 + [pl.BlockSpec(memory_space=pltpu.SMEM), ANY],
        out_specs=[VMEM] * 4,
        out_shape=[
            jax.ShapeDtypeStruct((local, depth), F32),
            jax.ShapeDtypeStruct((rows, width), BF16),
            jax.ShapeDtypeStruct((depth, width), BF16),
            jax.ShapeDtypeStruct((1, depth), F32),
        ],
        scratch_shapes=[
            pltpu.VMEM((rows, depth), BF16),
            pltpu.VMEM((8, depth), F32),
            pltpu.VMEM((depth, width), BF16),
            pltpu.SemaphoreType.DMA,
        ],
        compiler_params=pltpu.CompilerParams(vmem_limit_bytes=32 * 2**20),
        cost_estimate=cost("c_rb", 4e9),
        name="resid_back",
    )(normed_part, received, resid, cotangents, gain, attended, factors, attn_w)


def half(values, which, axis=1):
    size = values.shape[axis] // 2
    return lax.dynamic_slice_in_dim(values, which * size, size, axis)


def in_order(core, own, other, axis):
    return jnp.where(
        core == 0,
        jnp.concatenate([own, other], axis=axis),
        jnp.concatenate([other, own], axis=axis),
    )


def rms_back(grad_normed, inputs, inv_rms, gain):
    weighted = grad_normed * gain
    return inv_rms * weighted - inputs * inv_rms**3 * jnp.mean(
        weighted * inputs, axis=-1, keepdims=True
    )


def inverse_rms(values):
    return lax.rsqrt(jnp.mean(values * values, axis=-1, keepdims=True) + EPSILON)


def on_device(
    tokens,
    cotangent,
    group_ids,
    loss_weight,
    gain_attn,
    w_query,
    w_latent,
    w_key_up,
    w_value_up,
    w_out,
    gain_mlp,
    w_gate,
    w_up,
    w_down,
):
    nz, ny, nx = lax.axis_size("z"), lax.axis_size("y"), lax.axis_size("x")
    core = lax.axis_index("core")
    other = 1 - core
    local, depth = tokens.shape[1:]
    latent_width = w_latent.shape[1] // 2
    hidden_width = w_gate.shape[1] // 2
    query_width = w_query.shape[1] // 2
    gain_one = gain_attn.astype(F32)
    gain_two = gain_mlp.astype(F32)

    out_t = w_out.T
    row_parts = [w_query, w_latent, out_t, w_gate, w_up]
    mine = [half(part, core) for part in row_parts]
    theirs = [half(part, other) for part in row_parts]
    attn_recv = swap(jnp.concatenate(theirs[:3], axis=1))
    ff_recv = swap(jnp.concatenate(theirs[3:], axis=1))
    down_recv = to_half(w_down, 0)
    both = swap(jnp.concatenate([tokens, cotangent], axis=0))
    onehot = (group_ids[:, None] == jnp.arange(GROUPS, dtype=jnp.int32)[None, :]).astype(F32)
    onehot_other = swap(onehot)
    attn_shard = in_order(core, jnp.concatenate(mine[:3], axis=1), attn_recv, 0)
    ff_shard = in_order(core, jnp.concatenate(mine[3:], axis=1), ff_recv, 0)
    down_chip = in_order(core, w_down, down_recv, 0)

    counts = jnp.sum(onehot, axis=0) + jnp.sum(onehot_other, axis=0)
    counts = all_sum(counts, ("x", "y"))
    attn_shard = tie("attn_z", attn_shard, both, ff_shard, down_chip, onehot_other)
    attn_z = spread_z(attn_shard)
    attn_stack = tie("attn_plane", jnp.stack(attn_z), counts, ff_shard, down_chip)
    attn_a, attn_b = spread_own(attn_stack)
    attn_blocks = spread_rest(attn_stack, attn_a, attn_b)
    ff_shard = tie("ff_z", ff_shard, attn_z, counts)
    ff_z = spread_z(ff_shard)

    tokens_both = jnp.concatenate([tokens[0], both[0]], axis=0)
    inputs = tokens_both.astype(F32)
    inv_one = inverse_rms(inputs)
    normed_one = (inputs * inv_one * gain_one).astype(BF16)
    total_seqs = ny * nx * 2 * group_ids.shape[0]

    def factor(row):
        return jnp.sum(row * loss_weight) * (total_seqs / GROUPS) / jnp.sum(row * counts)

    factors = jnp.stack([factor(onehot[0]), factor(onehot_other[0])])
    cotangents = jnp.concatenate([cotangent[0], both[1]], axis=0)
    grad_out_low = (
        cotangents.astype(F32) * jnp.repeat(factors, local)[:, None]
    ).astype(BF16)

    attn_w = merge_blocks(attn_blocks)
    query_w = attn_w[:, :query_width]
    latent_w = attn_w[:, query_width : query_width + latent_width]
    latent = dot(normed_one, latent_w).astype(BF16).reshape(2, local, latent_width)
    latent = tie("lat", latent, ff_z)
    key_up = lax.dynamic_index_in_dim(w_key_up, core, 0, keepdims=False)
    value_up = lax.dynamic_index_in_dim(w_value_up, core, 0, keepdims=False)
    lats = [latent]
    for _ in range(1, nz):
        lats.append(lax.ppermute(lats[-1], "z", [(i, i + 1) for i in range(nz - 1)]))
    ff_z = tie("ff_plane", ff_z, attn_a, attn_b, attn_blocks[-1][-1], latent, lats[1:])
    ff_stack = jnp.stack(ff_z)
    ff_a, ff_b = spread_own(ff_stack, tie("ff_late", ff_stack, lats[1:], attn_blocks[-1][-1]))
    ff_blocks = spread_rest(
        ff_stack, [tie("ff_rest", part, lats, attn_blocks[-1][-1]) for part in ff_a], ff_b
    )
    ff_last = ff_blocks[-1][-1]
    down_z = spread_down_z(tie("down_z", down_chip, ff_z, lats, (ff_a, ff_b), ff_last))
    down_own = tie("down_plane", down_stack(down_z), (ff_a, ff_b), ff_last)
    down_a, down_b = spread_own(down_own)
    queries = dot(normed_one, query_w).astype(BF16).reshape(2, local, query_width)
    queries = tie("attend", queries, (ff_a, ff_b), down_z, ff_last, ff_a)
    attended, keys, values, probs = attend(queries, lats, key_up, value_up)
    attended_flat = tie("post", attended, (ff_a, ff_b), ff_last, down_z, (down_a, down_b), ff_a)
    attended_flat = attended_flat.reshape(2 * local, query_width)
    first = query_width + latent_width
    mixed = swap(mix_heads(attended_flat, attn_w, first))

    mixed = tie("gate", mixed, down_z, (down_a, down_b), (ff_a, ff_b), ff_last)
    resid, normed_two, ff_w, gate, up_value, hidden, down_parts = feed_forward(
        tokens_both, attended_flat, attn_w, first, mixed, gain_two[None], grad_out_low, ff_blocks
    )
    down_blocks = spread_rest(down_own, tie("down_rest", down_a, hidden), down_b)
    down_last = down_blocks[-1][-1]
    hidden = tie("hidden", hidden, (down_a, down_b), down_last)
    down_recv = send_b(down_parts)
    gate = tie("down_w", gate, down_parts, down_last)
    grad_ff, mlp_own, mlp_sent, gate_parts, up_parts = feed_back(
        gate, up_value, hidden, normed_two, grad_out_low, down_blocks
    )
    gate_recv = send_b(tie("gate_b", gate_parts, down_recv))
    up_parts = tie("up_b", up_parts, gate_recv, down_recv)
    up_recv = send_b(up_parts)
    down_row = add_b(down_parts, down_recv)
    down_recv_a = send_a(down_row)
    normed_part, sent = norm_back(tie("normed_part", grad_ff, gate_parts, down_recv), ff_w)
    received = swap(sent)
    grad_resid, grad_attended, out_rows, gain_two_part = resid_back(
        normed_part,
        received,
        resid,
        cotangents,
        factors,
        gain_two[None],
        attended_flat,
        attn_w,
        first,
    )
    gain_two_part = gain_two_part[0]

    grad_attended = grad_attended.reshape(2, local, query_width)
    down_own = add_a(tie("down_a", down_row, grad_attended), down_recv_a)
    down_recv_z = send_down_z(tie("down_back_z", down_own, grad_attended))
    gate_row = add_b(tie("gate_row", gate_parts, grad_attended), gate_recv)
    gate_recv_a = send_a(gate_row)
    gate_own = add_a(gate_row, gate_recv_a)
    grad_attended = tie(
        "back_0",
        grad_attended,
        down_recv,
        gate_recv,
        down_recv_a,
        out_rows,
        down_row,
        down_own,
        up_recv,
        gate_row,
        gate_own,
    )
    query_0, lat_0, up_0 = attend_back(
        0, queries, grad_attended, attended, keys, values, probs, lats, key_up, value_up, None
    )
    up_row = add_b(up_parts, up_recv)
    up_recv_a = send_a(up_row)
    up_own = add_a(up_row, up_recv_a)
    grad_attended = tie(
        "back_1",
        grad_attended,
        query_0,
        down_recv_a,
        up_recv,
        down_recv_z,
        up_row,
        down_own,
        gate_own,
        up_own,
    )
    query_1, lat_1, kv_grads = attend_back(
        1, queries, grad_attended, attended, keys, values, probs, lats, key_up, value_up, up_0
    )
    gate_recv_z = send_z(tie("gate_z", gate_own, grad_attended))
    lat_1 = tie("lat_back", list(lat_1), gate_own, up_row, up_recv_a, down_recv_z, gate_recv_z)
    lat_sum = jnp.concatenate([lat_0[0], lat_1[0]], axis=0).astype(F32)
    lat_recv = []
    for k in range(1, nz):
        sent = jnp.concatenate([lat_0[k], lat_1[k]], axis=0)
        lat_recv.append(lax.ppermute(sent, "z", [(i, i - k) for i in range(k, nz)]))
    kv_flat = kv_grads.reshape(depth, -1).astype(BF16)
    kv_parts = split_blocks(tie("kv", kv_flat, up_recv, lat_1), nz, True)
    kv_row = add_b(kv_parts, send_b(kv_parts))
    kv_row = tie("kv_a", kv_row, lat_recv)
    kv_own = add_a(kv_row, send_a(kv_row))
    grad_queries = jnp.concatenate([query_0[0], query_1[0]], axis=0)
    kv_z = tie("kv_z", kv_own, lat_recv, gate_recv_z)
    kv_recv = spread_ring(kv_z)[1:] if OPT.get("ring_kv", 0) else spread_z(kv_z)[1:]
    query_rows = dot(normed_one, tie("query_back", grad_queries, up_recv_a, lat_1, up_own), ROWS)
    normed_query = dot(tie("normed_query", grad_queries, lat_1), query_w, COLS)
    for part in lat_recv:
        lat_sum = lat_sum + part.astype(F32)
    grad_latent = tie("grad_latent", lat_sum.astype(BF16), query_rows, normed_query, kv_row, kv_own)
    grad_latent = grad_latent.reshape(2 * local, latent_width)
    last_rows = dot(normed_one, grad_latent, ROWS)
    attn_rows = [query_rows.astype(BF16), last_rows.astype(BF16), out_rows]
    attn_parts = list(split_blocks(jnp.concatenate(attn_rows, axis=1), nz))
    attn_recv = send_b(tie("attn_back", attn_parts, kv_row, kv_own))
    attn_row = add_b(attn_parts, attn_recv)
    attn_recv_a = send_a(attn_row)
    attn_own = add_a(attn_row, attn_recv_a)
    up_recv_z = send_z(
        tie("ff_back_z", up_own, lat_recv, gate_recv_z, kv_row, attn_recv, attn_recv_a, kv_recv)
    )
    attn_recv_z = send_z(tie("attn_back_z", attn_own, up_recv_z, kv_recv))
    normed_part = normed_query + dot(tie("normed_last", grad_latent, attn_parts), latent_w, COLS)
    gain_one_part = jnp.sum(normed_part * inputs * inv_one, axis=0)
    gains = jnp.stack([gain_one_part, gain_two_part])
    gains = tie("gains", gains, attn_parts, attn_recv, attn_recv_a, up_recv_z, kv_recv)
    gains = all_sum(gains, ("core", "x", "y", "z"))
    grad_normed = normed_part[:local] + swap(normed_part[local:].astype(BF16)).astype(F32)
    input_grad = (
        grad_resid + rms_back(grad_normed, inputs[:local], inv_one[:local], gain_one)
    ).astype(BF16)[None]
    mlp_sent = tie("mlp", mlp_sent, gate_parts, grad_attended, attn_parts)
    result = (resid[:local] + mlp_own + swap(mlp_sent).astype(F32)).astype(BF16)[None]
    kv_sum = kv_z.astype(F32)
    for part in tie("kv_sum", kv_recv, attn_parts, attn_recv, attn_recv_a):
        kv_sum = kv_sum + part.astype(F32)
    kv_sum = tie("kv_spread", kv_sum.astype(BF16), attn_parts, attn_recv, attn_recv_a)
    kv_a, kv_b = spread_own(kv_sum)
    kv_all = merge_blocks(spread_rest(kv_sum, kv_a, kv_b), fixed=True)
    kv_pair = in_order(core, kv_all[None], swap(kv_all)[None], 0).astype(F32)
    kv_pair = kv_pair.reshape((2,) + kv_grads.shape).transpose(1, 0, 3, 2, 4)
    kv_pair = kv_pair.reshape(2, KV_GROUPS, LATENT, query_width)

    def owned(totals):
        joined = jnp.concatenate(totals, axis=1).astype(BF16)
        received = swap(half(joined, other, 0))
        mine = half(joined, core, 0)
        results, start = [], 0
        for total in totals:
            width = total.shape[1]
            results.append(
                in_order(core, mine[:, start : start + width], received[:, start : start + width], 1)
                .astype(F32)
            )
            start += width
        return results

    gate_recv_z = tie("gate_last", gate_recv_z, attn_recv, attn_recv_a)
    up_recv_z = tie("up_last", up_recv_z, attn_recv, attn_recv_a)
    owned_gate, owned_up = owned([add_z(gate_own, gate_recv_z), add_z(up_own, up_recv_z)])
    owned_down = own_down(down_own, tie("down_last", down_recv_z, attn_recv, lat_recv, attn_recv_a))
    attn_total = add_z(attn_own, attn_recv_z)
    first = query_width + latent_width
    owned_query, owned_latent, owned_out = owned(
        [attn_total[:, :query_width], attn_total[:, query_width:first], attn_total[:, first:]]
    )
    return (
        result,
        input_grad,
        gains[0],
        owned_query,
        owned_latent,
        kv_pair[0],
        kv_pair[1],
        owned_out.T,
        gains[1],
        owned_gate,
        owned_up,
        owned_down,
    )


def solution(mesh):
    nz = mesh.shape["seq"]
    chips = mesh.shape["batch"] // 2
    nx = math.isqrt(chips)
    while chips % nx:
        nx -= 1
    fine = Mesh(mesh.devices.reshape(nz, chips // nx, nx, 2), ("z", "y", "x", "core"))
    batch = ("y", "x", "core")
    every = ("z",) + batch
    by_rows = P(every, None)
    in_specs = (
        P(batch, "z", None),
        P(batch, "z", None),
        P(batch),
        P(),
        P(),
        by_rows,
        by_rows,
        P(),
        P(),
        P(None, every),
        P(),
        by_rows,
        by_rows,
        by_rows,
    )
    out_specs = (
        P(batch, "z", None),
        P(batch, "z", None),
        P(),
        by_rows,
        by_rows,
        P(),
        P(),
        P(None, every),
        P(),
        by_rows,
        by_rows,
        by_rows,
    )
    return jax.shard_map(
        on_device, mesh=fine, in_specs=in_specs, out_specs=out_specs, check_vma=False
    )
```

```python
import math

import jax
import jax.numpy as jnp
from jax import lax
from jax.experimental import pallas as pl
from jax.experimental.pallas import tpu as pltpu
from jax.sharding import Mesh
from jax.sharding import PartitionSpec as P

HEADS = 16
HEAD_DIM = 64
LATENT = 256
KV_GROUPS = 2
GROUPS = 4
EPSILON = 1e-06
BF16 = jnp.bfloat16
F32 = jnp.float32
ROWS = (((0,), (0,)), ((), ()))
OPT = {"attn_z": 13, "back_0": 16, "back_1": 80, "c_attend": 4, "c_back": 3, "c_fb": 3, "c_ff": 3, "c_merge": 4, "c_mix": 4, "c_nb": 2, "c_rb": 4, "c_split": 4, "down_last": 2, "down_plane": 3, "down_z": 2, "ff_back_z": 8, "ff_late": 2, "ff_plane": 8, "ff_z": 2, "gains": 4, "gate_row": 1, "kv": 3, "kv_spread": 5, "kv_sum": 3, "kv_z": 3, "lat_back": 28, "normed_last": 1, "normed_part": 1, "normed_query": 1, "query_back": 6, "up_b": 1, "up_last": 1}
COLS = (((1,), (1,)), ((), ()))
PLAIN = (((1,), (0,)), ((), ()))


def dot(a, b, dims=PLAIN):
    return lax.dot_general(a, b, dims, preferred_element_type=F32)


PLANE = ("y", "x", "core")


def shift(values, axis, step):
    size = lax.axis_size(axis)
    return lax.ppermute(values, axis, [(i, (i + step) % size) for i in range(size)])


def leg(values, first, step):
    size = lax.axis_size("x")
    pairs = []
    for y in range(size):
        for x in range(size):
            for core in range(2):
                if (core == 0) == first:
                    target = (y, (x + step) % size, core)
                else:
                    target = ((y + step) % size, x, core)
                pairs.append(
                    ((y * size + x) * 2 + core, (target[0] * size + target[1]) * 2 + target[2])
                )
    return lax.ppermute(values, PLANE, pairs)


def swap(values):
    return shift(values, "core", 1)


def spread_z(shard):
    return [shard] + [shift(shard, "z", k) for k in range(1, lax.axis_size("z"))]


def spread_ring(shard):
    nz = lax.axis_size("z")
    pairs = [(z * 2 + c, (z + 1 - 2 * c) % nz * 2 + c) for z in range(nz) for c in range(2)]
    blocks = [shard]
    for _ in range(nz - 1):
        blocks.append(lax.ppermute(blocks[-1], ("z", "core"), pairs))
    return blocks


def spread_own(stack, late=None):
    size = lax.axis_size("x")
    late = stack if late is None else late
    return (
        [leg(stack, True, a) for a in range(1, size)],
        [leg(late, False, b) for b in range(1, size)],
    )


def spread_rest(stack, on_a, on_b):
    size = lax.axis_size("x")
    return [[stack] + on_a] + [
        [on_b[b - 1]] + [leg(block, False, b) for block in on_a] for b in range(1, size)
    ]


def after(value, *others):
    return lax.optimization_barrier((value,) + others)[0]


def tie(name, value, *others):
    mask = OPT.get(name, 0)
    chosen = [other for i, other in enumerate(others) if mask >> i & 1]
    return after(value, *chosen) if chosen else value


def cost(name, flops):
    return pl.CostEstimate(
        flops=int(flops * OPT.get(name, 0) / 4), bytes_accessed=4096, transcendentals=0
    )


def send_b(parts):
    return [leg(parts[b], False, b) for b in range(1, len(parts))]


def add_b(parts, received):
    row = parts[0]
    for part in received:
        row = add(row, part)
    return row


def send_a(row):
    return [leg(row[a], True, a) for a in range(1, row.shape[0])]


def add_a(row, received):
    own = row[0]
    for part in received:
        own = add(own, part)
    return own


RING = bool(OPT.get("ring_back", 0))


def ring(values):
    nz = lax.axis_size("z")
    pairs = [(z * 2 + c, (z + 1 - 2 * c) % nz * 2 + c) for z in range(nz) for c in range(2)]
    return lax.ppermute(values, ("z", "core"), pairs)


def back_away(k):
    return k * (2 * lax.axis_index("core") - 1) if RING else k


def send_z(own):
    if not RING:
        return [shift(own[k], "z", k) for k in range(1, own.shape[0])]
    part = own[1]
    for k in range(2, own.shape[0]):
        part = add(own[k], ring(part))
    return [ring(part)]


def add_z(own, received):
    total = own[0].astype(F32)
    for part in received:
        total = total + part.astype(F32)
    return total


def add(left, right):
    return (left.astype(F32) + right.astype(F32)).astype(BF16)


def to_half(values, step):
    nz = lax.axis_size("z")
    pairs = []
    for z in range(nz):
        keeper = z // (nz // 2)
        source = z * 2 + (keeper if step else 1 - keeper)
        pairs.append((source, (z + step) % nz * 2 + keeper))
    return lax.ppermute(values, ("z", "core"), pairs)


def spread_down_z(chip):
    nz, z, core = lax.axis_size("z"), lax.axis_index("z"), lax.axis_index("core")
    return [chip] + [to_half(chip, k) for k in range(1, nz)]


def down_stack(received):
    nz, z, core = lax.axis_size("z"), lax.axis_index("z"), lax.axis_index("core")
    received = jnp.stack(received)
    parts = []
    for j in range(nz // 2):
        step = lax.rem(z + nz - core * (nz // 2) - j, nz)
        parts.append(lax.dynamic_slice_in_dim(received, step, 1, 0))
    return jnp.concatenate(parts, axis=0)


def down_block(own, chip_z):
    count = own.shape[0]
    index = jnp.clip(chip_z - lax.axis_index("core") * count, 0, count - 1)
    return lax.dynamic_index_in_dim(own, index, 0, keepdims=False)


def send_down_z(own):
    nz, z, count = lax.axis_size("z"), lax.axis_index("z"), own.shape[0]
    received = []
    for k in range(1, nz):
        pairs = [((d + k) % nz * 2 + d // count, d * 2 + d // count) for d in range(nz)]
        part = down_block(own, lax.rem(z + nz - k, nz))
        received.append(lax.ppermute(part, ("z", "core"), pairs))
    return received


def own_down(own, received):
    nz, z, core = lax.axis_size("z"), lax.axis_index("z"), lax.axis_index("core")
    count = nz // 2
    total = down_block(own, z).astype(F32)
    for part in received:
        total = total + part.astype(F32)
    pairs = [(d * 2 + d // count, d * 2 + 1 - d // count) for d in range(nz)]
    sent = lax.ppermute(half(total, 1 - core, 0).astype(BF16), ("z", "core"), pairs)
    return jnp.where(core == z // count, half(total, core, 0), sent.astype(F32))


def place(size, nz, k, b, a):
    core = lax.axis_index("core")
    z = lax.rem(lax.axis_index("z") + nz + k, nz)
    y = lax.rem(lax.axis_index("y") + size + b + core * (a - b), size)
    x = lax.rem(lax.axis_index("x") + size + a + core * (b - a), size)
    return z, y, x


def merge_blocks(blocks, fixed=False, ring=False):
    size = len(blocks)
    nz, rows, columns = blocks[0][0].shape
    parts = [block for row in blocks for block in row]

    def kernel(*refs):
        out, sems = refs[-2], refs[-1]
        copies = []
        for b in range(size):
            for a in range(size):
                for k in range(nz):
                    away = k * (2 * lax.axis_index("core") - 1) if ring else -k
                    z, y, x = place(size, nz, away, -b, -a)
                    n = b * size + a
                    copies.append(
                        pltpu.make_async_copy(
                            refs[n].at[k], out.at[k if fixed else z, y, x], sems.at[n * nz + k]
                        )
                    )
        for copy in copies:
            copy.start()
        for copy in copies:
            copy.wait()

    out = pl.pallas_call(
        kernel,
        out_shape=jax.ShapeDtypeStruct((nz, size, size, rows, columns), parts[0].dtype),
        in_specs=[pl.BlockSpec(memory_space=pl.ANY)] * len(parts),
        out_specs=pl.BlockSpec(memory_space=pltpu.VMEM),
        scratch_shapes=[pltpu.SemaphoreType.DMA((nz * size * size,))],
        compiler_params=pltpu.CompilerParams(vmem_limit_bytes=48 * 2**20),
        cost_estimate=cost("c_merge", 3e9),
        name="merge",
    )(*parts)
    return out.reshape(nz * size * size * rows, columns)


def split_blocks(full, nz, fixed=False):
    size = lax.axis_size("x")
    rows = full.shape[0] // (nz * size * size)
    columns = full.shape[1]

    def kernel(*refs):
        source, outs, sems = refs[0], refs[1:-1], refs[-1]
        copies = []
        for b in range(size):
            for a in range(size):
                for k in range(nz):
                    z, y, x = place(size, nz, back_away(k), b, a)
                    copies.append(
                        pltpu.make_async_copy(
                            source.at[k if fixed else z, y, x],
                            outs[b].at[a, k],
                            sems.at[(b * size + a) * nz + k],
                        )
                    )
        for copy in copies:
            copy.start()
        for copy in copies:
            copy.wait()

    return pl.pallas_call(
        kernel,
        out_shape=[jax.ShapeDtypeStruct((size, nz, rows, columns), full.dtype)] * size,
        in_specs=[pl.BlockSpec(memory_space=pltpu.VMEM)],
        out_specs=[pl.BlockSpec(memory_space=pl.ANY)] * size,
        scratch_shapes=[pltpu.SemaphoreType.DMA((nz * size * size,))],
        compiler_params=pltpu.CompilerParams(vmem_limit_bytes=48 * 2**20),
        cost_estimate=cost("c_split", 3e9),
        name="split",
    )(full.reshape(nz, size, size, rows, columns))


def all_sum(values, axes):
    for axis in axes:
        size = lax.axis_size(axis)
        total = values
        for k in range(1, size):
            total = total + shift(values, axis, k)
        values = total
    return values


def head_halves(pair):
    lane = lax.broadcasted_iota(jnp.int32, pair.shape, 1)
    zero = jnp.zeros_like(pair)
    return jnp.concatenate(
        [jnp.where(lane < HEAD_DIM, pair, zero), jnp.where(lane >= HEAD_DIM, pair, zero)], axis=0
    )


def join_halves(halves):
    rows = halves.shape[0] // 2
    lane = lax.broadcasted_iota(jnp.int32, (rows, halves.shape[1]), 1)
    return jnp.where(lane < HEAD_DIM, halves[:rows], halves[rows:])


def attend_kernel(nz, q_ref, *refs):
    lats, (wk_ref, wv_ref, att_ref, key_ref, value_ref, prob_ref) = refs[:nz], refs[nz:]
    local = q_ref.shape[1]
    z = lax.axis_index("z")
    q2 = head_halves(q_ref[0] * BF16(HEAD_DIM**-0.5))
    wk, wv = wk_ref[...], wv_ref[...]
    scores = []
    for k in range(nz):
        lat = lats[k][0]
        key = dot(lat, wk).astype(BF16)
        value = dot(lat, wv).astype(BF16)
        key_ref[0, k * local : (k + 1) * local] = key
        value_ref[0, k * local : (k + 1) * local] = value
        block = dot(q2, key, COLS)
        if k == 0:
            row = lax.rem(lax.broadcasted_iota(jnp.int32, block.shape, 0), local)
            column = lax.broadcasted_iota(jnp.int32, block.shape, 1)
            block = jnp.where(column <= row, block, -1e30)
        else:
            block = block + jnp.where(z >= k, 0.0, -1e30)
        scores.append(block)
    top = scores[0]
    for block in scores[1:]:
        top = jnp.maximum(top, block)
    top = jnp.max(top, axis=1, keepdims=True)
    exps = [jnp.exp(block - top) for block in scores]
    total = exps[0]
    for block in exps[1:]:
        total = total + block
    inverse = 1.0 / jnp.sum(total, axis=1, keepdims=True)
    mixed = jnp.zeros((2 * local, q_ref.shape[2]), F32)
    for k in range(nz):
        prob = (exps[k] * inverse).astype(BF16)
        prob_ref[0, 0, k] = prob
        mixed = mixed + dot(prob, value_ref[0, k * local : (k + 1) * local])
    att_ref[0] = join_halves(mixed).astype(BF16)


def attend(queries, lats, key_up, value_up):
    seqs, local, width = queries.shape
    nz = len(lats)
    pairs = width // 128
    query_spec = pl.BlockSpec((1, local, 128), lambda s, h: (s, 0, h))
    full_spec = pl.BlockSpec((1, nz * local, 128), lambda s, h: (s, 0, h))
    lat_spec = pl.BlockSpec((1, local, LATENT), lambda s, h: (s, 0, 0))
    up_spec = pl.BlockSpec((LATENT, 128), lambda s, h: (0, h))
    full = jax.ShapeDtypeStruct((seqs, nz * local, width), BF16)
    return pl.pallas_call(
        lambda *refs: attend_kernel(nz, *refs),
        grid=(seqs, pairs),
        in_specs=[query_spec] + [lat_spec] * nz + [up_spec] * 2,
        out_specs=[
            query_spec,
            full_spec,
            full_spec,
            pl.BlockSpec((1, 1, nz, 2 * local, local), lambda s, h: (s, h, 0, 0, 0)),
        ],
        out_shape=[
            jax.ShapeDtypeStruct(queries.shape, BF16),
            full,
            full,
            jax.ShapeDtypeStruct((seqs, pairs, nz, 2 * local, local), BF16),
        ],
        compiler_params=pltpu.CompilerParams(vmem_limit_bytes=48 * 2**20),
        cost_estimate=cost("c_attend", 16e9),
        name="attend",
    )(queries, *lats, key_up, value_up)


def attend_back_kernel(nz, pairs, first, q_ref, g_ref, att_ref, key_ref, value_ref, prob_ref, *refs):
    lats, (wk_ref, wv_ref, old_ref), rest = refs[:nz], refs[nz : nz + 3], refs[nz + 3 :]
    dq_ref, dlats, (up_ref, lat_acc) = rest[0], rest[1 : nz + 1], rest[nz + 1 :]
    pair = pl.program_id(0)
    local = q_ref.shape[1]
    scale = HEAD_DIM**-0.5
    grad = g_ref[0].astype(F32)
    query = head_halves(q_ref[0].astype(F32) * scale)
    g2 = head_halves(grad)
    inner = jnp.sum(head_halves(grad * att_ref[0].astype(F32)), axis=1, keepdims=True)
    query_t, g2_t = query.T.astype(BF16), g2.T.astype(BF16)
    g2 = g2.astype(BF16)
    @pl.when(pair == 0)
    def _():
        lat_acc[...] = jnp.zeros_like(lat_acc)

    dq = jnp.zeros((2 * local, 128), F32)
    up_key = jnp.zeros((128, LATENT), F32)
    up_value = jnp.zeros((128, LATENT), F32)
    for k in range(nz):
        rows = slice(k * local, (k + 1) * local)
        prob = prob_ref[0, 0, k]
        key, value = key_ref[0, rows], value_ref[0, rows]
        grad_prob = dot(g2, value, COLS)
        grad_score = (prob.astype(F32) * (grad_prob - inner)).astype(BF16)
        dq = dq + dot(grad_score, key)
        grad_key = dot(query_t, grad_score).astype(BF16)
        grad_value = dot(g2_t, prob).astype(BF16)
        term = dot(wk_ref[...], grad_key) + dot(wv_ref[...], grad_value)

        lat_acc[:, rows] += term
        lat = lats[k][0]
        up_key = up_key + dot(grad_key, lat)
        up_value = up_value + dot(grad_value, lat)
    dq_ref[0] = (join_halves(dq) * scale).astype(BF16)
    up_ref[0, 0] = up_key.T if first else up_key.T + old_ref[0, 0]
    up_ref[1, 0] = up_value.T if first else up_value.T + old_ref[1, 0]

    @pl.when(pair == pairs - 1)
    def _():
        for k in range(nz):
            dlats[k][0] = lat_acc[:, k * local : (k + 1) * local].T.astype(BF16)


def attend_back(seq, queries, grad_att, attended, keys, values, probs, lats, key_up, value_up, old):
    _, local, width = queries.shape
    nz = len(lats)
    pairs = width // 128
    query_spec = pl.BlockSpec((1, local, 128), lambda h: (seq, 0, h))
    full_spec = pl.BlockSpec((1, nz * local, 128), lambda h: (seq, 0, h))
    lat_spec = pl.BlockSpec((1, local, LATENT), lambda h: (seq, 0, 0))
    up_spec = pl.BlockSpec((LATENT, 128), lambda h: (0, h))
    prob_spec = pl.BlockSpec((1, 1, nz, 2 * local, local), lambda h: (seq, h, 0, 0, 0))
    grad_spec = pl.BlockSpec((2, 1, LATENT, 128), lambda h: (0, h, 0, 0))
    outs = pl.pallas_call(
        lambda *refs: attend_back_kernel(nz, pairs, old is None, *refs),
        grid=(pairs,),
        in_specs=[query_spec] * 3
        + [full_spec] * 2
        + [prob_spec]
        + [lat_spec] * nz
        + [up_spec] * 2
        + [pl.BlockSpec(memory_space=pl.ANY) if old is None else grad_spec],
        out_specs=[pl.BlockSpec((1, local, 128), lambda h: (0, 0, h))]
        + [pl.BlockSpec((1, local, LATENT), lambda h: (0, 0, 0))] * nz
        + [grad_spec],
        out_shape=[jax.ShapeDtypeStruct((1, local, width), BF16)]
        + [jax.ShapeDtypeStruct((1, local, LATENT), BF16)] * nz
        + [jax.ShapeDtypeStruct((2, pairs, LATENT, 128), F32)],
        scratch_shapes=[pltpu.VMEM((LATENT, nz * local), F32)],
        compiler_params=pltpu.CompilerParams(vmem_limit_bytes=48 * 2**20),
        cost_estimate=cost("c_back", 17e9),
        name="attend_back",
    )(queries, grad_att, attended, keys, values, probs, *lats, key_up, value_up,
      key_up if old is None else old)
    return outs[0], outs[1 : nz + 1], outs[nz + 1]


VMEM = pl.BlockSpec(memory_space=pltpu.VMEM)
ANY = pl.BlockSpec(memory_space=pl.ANY)
PARAMS = pltpu.CompilerParams(vmem_limit_bytes=56 * 2**20)


def chunks(width):
    return [slice(start, min(start + 256, width)) for start in range(0, width, 256)]


def row_blocks(count, body):
    @pl.loop(0, count, step=64)
    def _(start):
        body(pl.ds(pl.multiple_of(start, 64), 64))


def block_copies(size, nz, sems, make):
    copies = []
    for b in range(size):
        for a in range(size):
            for k in range(nz):
                copies.append(make(b, a, k, sems.at[(b * size + a) * nz + k]))
    for copy in copies:
        copy.start()
    return copies


def mix_heads(attended, attn_w, first):
    rows, width = attended.shape
    depth = attn_w.shape[0]
    local = rows // 2

    def kernel(att_ref, w_ref, sent_ref, out_w, sem):
        copy = pltpu.make_async_copy(w_ref.at[:, pl.ds(first, width)], out_w, sem)
        copy.start()
        copy.wait()
        sent_ref[:local] = dot(att_ref[local:], out_w[...], COLS).astype(BF16)
        sent_ref[local:] = dot(att_ref[:local], out_w[...], COLS).astype(BF16)

    return pl.pallas_call(
        kernel,
        in_specs=[VMEM, ANY],
        out_specs=VMEM,
        out_shape=jax.ShapeDtypeStruct((rows, depth), BF16),
        scratch_shapes=[pltpu.VMEM((depth, width), BF16), pltpu.SemaphoreType.DMA],
        compiler_params=pltpu.CompilerParams(vmem_limit_bytes=16 * 2**20),
        cost_estimate=cost("c_mix", 2e9),
        name="mix_heads",
    )(attended, attn_w)


def feed_forward(tokens, attended, attn_w, first, mixed, gain, grad_low, blocks):
    size = len(blocks)
    nz, block_rows, wide = blocks[0][0].shape
    rows, heads_width = attended.shape
    depth = tokens.shape[1]
    width = wide // 2
    half_z = nz // 2
    down_rows = width // (half_z * size * size)
    direct = block_rows % 16 == 0 and down_rows % 16 == 0
    flat = [block for row in blocks for block in row]
    if not direct:
        flat = [merge_blocks(blocks)]
    shapes = [
        ((rows, depth), F32),
        ((rows, depth), BF16),
        ((depth, wide), BF16),
        ((rows, width), BF16),
        ((rows, width), BF16),
        ((rows, width), BF16),
    ]

    def kernel(x_ref, att_ref, mix_ref, gain_ref, go_ref, attn_ref, *refs):
        sources, refs = refs[: len(flat)], refs[len(flat) :]
        leaving, outs = refs[:6], refs[6 : 6 + (size if direct else 1)]
        held, (out_w, grad_ref, sem, held_sems, in_sems, out_sems) = refs[-12:-6], refs[-6:]
        resid_ref, norm_ref, w_ref, gate_ref, up_ref, hid_ref = held

        def fetch(b, a, k, sem):
            z, y, x = place(size, nz, -k, -b, -a)
            start = ((z * size + y) * size + x) * block_rows
            target = w_ref.at[pl.ds(pl.multiple_of(start, 16), block_rows)]
            return pltpu.make_async_copy(sources[b * size + a].at[k], target, sem)

        first_copy = pltpu.make_async_copy(attn_ref.at[:, pl.ds(first, heads_width)], out_w, sem)
        first_copy.start()
        if direct:
            copies = block_copies(size, nz, in_sems, fetch)
        else:
            copies = [pltpu.make_async_copy(sources[0], w_ref, in_sems.at[0])]
            copies[0].start()
        out_copies = [
            pltpu.make_async_copy(held[i], leaving[i], held_sems.at[i]) for i in range(6)
        ]
        first_copy.wait()
        resid_ref[...] = dot(att_ref[...], out_w[...], COLS)

        def norm(at):
            resid = x_ref[at].astype(F32) + resid_ref[at] + mix_ref[at].astype(F32)
            resid_ref[at] = resid
            norm_ref[at] = (resid * inverse_rms(resid) * gain_ref[...]).astype(BF16)

        row_blocks(rows, norm)
        out_copies[0].start()
        out_copies[1].start()
        for copy in copies:
            copy.wait()
        out_copies[2].start()
        normed = norm_ref[...]
        low = go_ref[...]
        for at in chunks(width):
            gate = dot(normed, w_ref[:, at])
            up = dot(normed, w_ref[:, width + at.start : width + at.stop])
            gate_ref[:, at] = gate.astype(BF16)
            up_ref[:, at] = up.astype(BF16)
            hid_ref[:, at] = (gate * jax.nn.sigmoid(gate) * up).astype(BF16)
        for copy in out_copies[3:]:
            copy.start()
        for at in chunks(width):
            grad_ref[at] = dot(hid_ref[:, at], low, ROWS).astype(BF16)

        def leave(b, a, k, sem):
            _, y, x = place(size, nz, 0, b, a)
            start = ((k * size + y) * size + x) * down_rows
            source = grad_ref.at[pl.ds(pl.multiple_of(start, 16), down_rows)]
            return pltpu.make_async_copy(source, outs[b].at[a, k], sem)

        if direct:
            copies = block_copies(size, half_z, out_sems, leave)
        else:
            copies = [pltpu.make_async_copy(grad_ref, outs[0], out_sems.at[0])]
            copies[0].start()
        for copy in copies + out_copies:
            copy.wait()

    outs = pl.pallas_call(
        kernel,
        in_specs=[VMEM] * 5 + [ANY] * (1 + len(flat)),
        out_specs=[ANY] * (6 + (size if direct else 1)),
        out_shape=[jax.ShapeDtypeStruct(*shape) for shape in shapes]
        + (
            [jax.ShapeDtypeStruct((size, half_z, down_rows, depth), BF16)] * size
            if direct
            else [jax.ShapeDtypeStruct((width, depth), BF16)]
        ),
        scratch_shapes=[pltpu.VMEM(*shape) for shape in shapes]
        + [
            pltpu.VMEM((depth, heads_width), BF16),
            pltpu.VMEM((width, depth), BF16),
            pltpu.SemaphoreType.DMA,
            pltpu.SemaphoreType.DMA((6,)),
            pltpu.SemaphoreType.DMA((nz * size * size,)),
            pltpu.SemaphoreType.DMA((half_z * size * size,)),
        ],
        compiler_params=PARAMS,
        cost_estimate=cost("c_ff", 14e9),
        name="feed_forward",
    )(tokens, attended, mixed, gain, grad_low, attn_w, *flat)
    parts = list(outs[6:]) if direct else split_blocks(outs[6], half_z, True)
    return (*outs[:6], list(parts))


def feed_back(gate, up, hidden, normed, grad_low, blocks):
    size = len(blocks)
    half_z, block_rows, depth = blocks[0][0].shape
    nz = half_z * 2
    rows, width = gate.shape
    wide = 2 * width
    local = rows // 2
    grad_rows = depth // (nz * size * size)
    direct = block_rows % 16 == 0 and grad_rows % 16 == 0
    flat = [block for row in blocks for block in row]
    if not direct:
        flat = [merge_blocks(blocks, True)]
    parts = chunks(width)

    def kernel(norm_ref, go_ref, gate_in, up_in, hid_in, *refs):
        sources, refs = refs[: len(flat)], refs[len(flat) :]
        grad_out, own_ref, sent_ref = refs[:3]
        outs, refs = refs[3:-9], refs[-9:]
        w_ref, dw_ref, gate_ref, up_ref, hid_ref, grad_ref, sems, in_sems, out_sems = refs

        def fetch(b, a, k, sem):
            _, y, x = place(size, nz, 0, -b, -a)
            start = ((k * size + y) * size + x) * block_rows
            target = w_ref.at[pl.ds(pl.multiple_of(start, 16), block_rows)]
            return pltpu.make_async_copy(sources[b * size + a].at[k], target, sem)

        if direct:
            copies = block_copies(size, half_z, in_sems, fetch)
        else:
            copies = [pltpu.make_async_copy(sources[0], w_ref, in_sems.at[0])]
            copies[0].start()
        arriving = []
        for i, at in enumerate(parts):
            span = pl.ds(at.start, at.stop - at.start)
            arriving.append(
                [
                    pltpu.make_async_copy(source.at[:, span], target.at[:, span], sems.at[3 * i + j])
                    for j, (source, target) in enumerate(
                        ((gate_in, gate_ref), (up_in, up_ref), (hid_in, hid_ref))
                    )
                ]
            )
            for copy in arriving[-1]:
                copy.start()
        normed = norm_ref[...]
        for copy in copies:
            copy.wait()
        low = go_ref[...]
        for i, at in enumerate(parts):
            for copy in arriving[i]:
                copy.wait()
            grad_hidden = dot(low, w_ref[at], COLS)
            gate = gate_ref[:, at].astype(F32)
            sigma = jax.nn.sigmoid(gate)
            grad_gate = grad_hidden * up_ref[:, at].astype(F32) * sigma * (1.0 + gate * (1.0 - sigma))
            grad_up = grad_hidden * (gate * sigma)
            other = slice(width + at.start, width + at.stop)
            grad_ref[:, at] = grad_gate.astype(BF16)
            grad_ref[:, other] = grad_up.astype(BF16)
            dw_ref[:, at] = dot(normed, grad_ref[:, at], ROWS).astype(BF16)
            dw_ref[:, other] = dot(normed, grad_ref[:, other], ROWS).astype(BF16)

        def leave(part):
            def make(b, a, k, sem):
                z, y, x = place(size, nz, back_away(k), b, a)
                start = ((z * size + y) * size + x) * grad_rows
                rows_at = pl.ds(pl.multiple_of(start, 16), grad_rows)
                source = dw_ref.at[rows_at, pl.ds(part * width, width)]
                return pltpu.make_async_copy(source, outs[part * size + b].at[a, k], sem)

            return make

        if direct:
            copies = []
            for part in range(2):
                copies += block_copies(size, nz, out_sems.at[part], leave(part))
        else:
            copies = []
            for part in range(2):
                source = dw_ref.at[:, pl.ds(part * width, width)]
                copies.append(pltpu.make_async_copy(source, outs[part], out_sems.at[part, 0]))
                copies[-1].start()
        last = pltpu.make_async_copy(grad_ref, grad_out, sems.at[3 * len(parts)])
        last.start()
        own_ref[...] = dot(hid_ref[:local], w_ref[...])
        sent_ref[...] = dot(hid_ref[local:], w_ref[...]).astype(BF16)
        for copy in copies + [last]:
            copy.wait()

    outs = pl.pallas_call(
        kernel,
        in_specs=[VMEM] * 2 + [ANY] * (3 + len(flat)),
        out_specs=[ANY] + [VMEM] * 2 + [ANY] * (2 * size if direct else 2),
        out_shape=[
            jax.ShapeDtypeStruct((rows, wide), BF16),
            jax.ShapeDtypeStruct((local, depth), F32),
            jax.ShapeDtypeStruct((local, depth), BF16),
        ]
        + (
            [jax.ShapeDtypeStruct((size, nz, grad_rows, width), BF16)] * (2 * size)
            if direct
            else [jax.ShapeDtypeStruct((depth, width), BF16)] * 2
        ),
        scratch_shapes=[
            pltpu.VMEM((width, depth), BF16),
            pltpu.VMEM((depth, wide), BF16),
            pltpu.VMEM((rows, width), BF16),
            pltpu.VMEM((rows, width), BF16),
            pltpu.VMEM((rows, width), BF16),
            pltpu.VMEM((rows, wide), BF16),
            pltpu.SemaphoreType.DMA((3 * len(parts) + 1,)),
            pltpu.SemaphoreType.DMA((half_z * size * size,)),
            pltpu.SemaphoreType.DMA((2, nz * size * size)),
        ],
        compiler_params=PARAMS,
        cost_estimate=cost("c_fb", 18e9),
        name="feed_back",
    )(normed, grad_low, gate, up, hidden, *flat)
    if direct:
        parts = [list(outs[3 : 3 + size]), list(outs[3 + size :])]
    else:
        parts = [list(split_blocks(part, nz)) for part in outs[3:]]
    return outs[0], outs[1], outs[2], *parts


def norm_back(grad_ff, ff_w):
    rows, wide = grad_ff.shape
    depth = ff_w.shape[0]
    local = rows // 2

    def kernel(grad_ref, w_ref, part_ref, sent_ref):
        for at in chunks(depth):
            part = dot(grad_ref[...], w_ref[at], COLS)
            part_ref[:, at] = part
            sent_ref[:local, at] = part[local:].astype(BF16)
            sent_ref[local:, at] = part[:local].astype(BF16)

    return pl.pallas_call(
        kernel,
        in_specs=[VMEM] * 2,
        out_specs=[VMEM] * 2,
        out_shape=[
            jax.ShapeDtypeStruct((rows, depth), F32),
            jax.ShapeDtypeStruct((rows, depth), BF16),
        ],
        compiler_params=pltpu.CompilerParams(vmem_limit_bytes=32 * 2**20),
        cost_estimate=cost("c_nb", 6e9),
        name="norm_back",
    )(grad_ff, ff_w)


def resid_back(normed_part, received, resid, cotangents, factors, gain, attended, attn_w, first):
    rows, depth = resid.shape
    width = attended.shape[1]
    local = rows // 2

    def kernel(part_ref, recv_ref, resid_ref, cot_ref, gain_ref, att_ref, fac_ref, w_ref, *refs):
        grad_ref, datt_ref, dw_ref, dg_ref, low_ref, sum_ref, out_w, sem = refs
        copy = pltpu.make_async_copy(w_ref.at[:, pl.ds(first, width)], out_w, sem)
        copy.start()
        sum_ref[...] = jnp.zeros_like(sum_ref)

        def norm(at):
            resid = resid_ref[at]
            part = part_ref[at]
            inverse = inverse_rms(resid)
            scaled = resid * inverse
            gains = part * scaled
            total = gains[:8]
            for row in range(8, 64, 8):
                total = total + gains[row : row + 8]
            sum_ref[...] += total
            weighted = (part + recv_ref[at].astype(F32)) * gain_ref[...]
            mean = jnp.mean(weighted * scaled, axis=-1, keepdims=True)
            factor = jnp.where(at.start < local, fac_ref[0], fac_ref[1])
            grad = cot_ref[at].astype(F32) * factor + inverse * (weighted - scaled * mean)
            low_ref[at] = grad.astype(BF16)

            @pl.when(at.start < local)
            def _():
                grad_ref[at] = grad

        row_blocks(rows, norm)
        dg_ref[...] = jnp.sum(sum_ref[...], axis=0, keepdims=True)
        copy.wait()
        low = low_ref[...]
        datt_ref[...] = dot(low, out_w[...]).astype(BF16)
        dw_ref[...] = dot(low, att_ref[...], ROWS).astype(BF16)

    return pl.pallas_call(
        kernel,
        in_specs=[VMEM] * 6 + [pl.BlockSpec(memory_space=pltpu.SMEM), ANY],
        out_specs=[VMEM] * 4,
        out_shape=[
            jax.ShapeDtypeStruct((local, depth), F32),
            jax.ShapeDtypeStruct((rows, width), BF16),
            jax.ShapeDtypeStruct((depth, width), BF16),
            jax.ShapeDtypeStruct((1, depth), F32),
        ],
        scratch_shapes=[
            pltpu.VMEM((rows, depth), BF16),
            pltpu.VMEM((8, depth), F32),
            pltpu.VMEM((depth, width), BF16),
            pltpu.SemaphoreType.DMA,
        ],
        compiler_params=pltpu.CompilerParams(vmem_limit_bytes=32 * 2**20),
        cost_estimate=cost("c_rb", 4e9),
        name="resid_back",
    )(normed_part, received, resid, cotangents, gain, attended, factors, attn_w)


def half(values, which, axis=1):
    size = values.shape[axis] // 2
    return lax.dynamic_slice_in_dim(values, which * size, size, axis)


def in_order(core, own, other, axis):
    return jnp.where(
        core == 0,
        jnp.concatenate([own, other], axis=axis),
        jnp.concatenate([other, own], axis=axis),
    )


def rms_back(grad_normed, inputs, inv_rms, gain):
    weighted = grad_normed * gain
    return inv_rms * weighted - inputs * inv_rms**3 * jnp.mean(
        weighted * inputs, axis=-1, keepdims=True
    )


def inverse_rms(values):
    return lax.rsqrt(jnp.mean(values * values, axis=-1, keepdims=True) + EPSILON)


def on_device(
    tokens,
    cotangent,
    group_ids,
    loss_weight,
    gain_attn,
    w_query,
    w_latent,
    w_key_up,
    w_value_up,
    w_out,
    gain_mlp,
    w_gate,
    w_up,
    w_down,
):
    nz, ny, nx = lax.axis_size("z"), lax.axis_size("y"), lax.axis_size("x")
    core = lax.axis_index("core")
    other = 1 - core
    local, depth = tokens.shape[1:]
    latent_width = w_latent.shape[1] // 2
    hidden_width = w_gate.shape[1] // 2
    query_width = w_query.shape[1] // 2
    gain_one = gain_attn.astype(F32)
    gain_two = gain_mlp.astype(F32)

    out_t = w_out.T
    row_parts = [w_query, w_latent, out_t, w_gate, w_up]
    mine = [half(part, core) for part in row_parts]
    theirs = [half(part, other) for part in row_parts]
    attn_recv = swap(jnp.concatenate(theirs[:3], axis=1))
    ff_recv = swap(jnp.concatenate(theirs[3:], axis=1))
    down_recv = to_half(w_down, 0)
    both = swap(jnp.concatenate([tokens, cotangent], axis=0))
    onehot = (group_ids[:, None] == jnp.arange(GROUPS, dtype=jnp.int32)[None, :]).astype(F32)
    onehot_other = swap(onehot)
    attn_shard = in_order(core, jnp.concatenate(mine[:3], axis=1), attn_recv, 0)
    ff_shard = in_order(core, jnp.concatenate(mine[3:], axis=1), ff_recv, 0)
    down_chip = in_order(core, w_down, down_recv, 0)

    counts = jnp.sum(onehot, axis=0) + jnp.sum(onehot_other, axis=0)
    counts = all_sum(counts, ("x", "y"))
    attn_shard = tie("attn_z", attn_shard, both, ff_shard, down_chip, onehot_other)
    attn_z = spread_z(attn_shard)
    attn_stack = tie("attn_plane", jnp.stack(attn_z), counts, ff_shard, down_chip)
    attn_a, attn_b = spread_own(attn_stack)
    attn_blocks = spread_rest(attn_stack, attn_a, attn_b)
    ff_shard = tie("ff_z", ff_shard, attn_z, counts)
    ff_z = spread_z(ff_shard)

    tokens_both = jnp.concatenate([tokens[0], both[0]], axis=0)
    inputs = tokens_both.astype(F32)
    inv_one = inverse_rms(inputs)
    normed_one = (inputs * inv_one * gain_one).astype(BF16)
    total_seqs = ny * nx * 2 * group_ids.shape[0]

    def factor(row):
        return jnp.sum(row * loss_weight) * (total_seqs / GROUPS) / jnp.sum(row * counts)

    factors = jnp.stack([factor(onehot[0]), factor(onehot_other[0])])
    cotangents = jnp.concatenate([cotangent[0], both[1]], axis=0)
    grad_out_low = (
        cotangents.astype(F32) * jnp.repeat(factors, local)[:, None]
    ).astype(BF16)

    attn_w = merge_blocks(attn_blocks)
    query_w = attn_w[:, :query_width]
    latent_w = attn_w[:, query_width : query_width + latent_width]
    latent = dot(normed_one, latent_w).astype(BF16).reshape(2, local, latent_width)
    latent = tie("lat", latent, ff_z)
    key_up = lax.dynamic_index_in_dim(w_key_up, core, 0, keepdims=False)
    value_up = lax.dynamic_index_in_dim(w_value_up, core, 0, keepdims=False)
    lats = [latent]
    for _ in range(1, nz):
        lats.append(lax.ppermute(lats[-1], "z", [(i, i + 1) for i in range(nz - 1)]))
    ff_z = tie("ff_plane", ff_z, attn_a, attn_b, attn_blocks[-1][-1], latent, lats[1:])
    ff_stack = jnp.stack(ff_z)
    ff_a, ff_b = spread_own(ff_stack, tie("ff_late", ff_stack, lats[1:], attn_blocks[-1][-1]))
    ff_blocks = spread_rest(
        ff_stack, [tie("ff_rest", part, lats, attn_blocks[-1][-1]) for part in ff_a], ff_b
    )
    ff_last = ff_blocks[-1][-1]
    down_z = spread_down_z(tie("down_z", down_chip, ff_z, lats, (ff_a, ff_b), ff_last))
    down_own = tie("down_plane", down_stack(down_z), (ff_a, ff_b), ff_last)
    down_a, down_b = spread_own(down_own)
    queries = dot(normed_one, query_w).astype(BF16).reshape(2, local, query_width)
    queries = tie("attend", queries, (ff_a, ff_b), down_z, ff_last, ff_a)
    attended, keys, values, probs = attend(queries, lats, key_up, value_up)
    attended_flat = tie("post", attended, (ff_a, ff_b), ff_last, down_z, (down_a, down_b), ff_a)
    attended_flat = attended_flat.reshape(2 * local, query_width)
    first = query_width + latent_width
    mixed = swap(mix_heads(attended_flat, attn_w, first))

    mixed = tie("gate", mixed, down_z, (down_a, down_b), (ff_a, ff_b), ff_last)
    resid, normed_two, ff_w, gate, up_value, hidden, down_parts = feed_forward(
        tokens_both, attended_flat, attn_w, first, mixed, gain_two[None], grad_out_low, ff_blocks
    )
    down_blocks = spread_rest(down_own, tie("down_rest", down_a, hidden), down_b)
    down_last = down_blocks[-1][-1]
    hidden = tie("hidden", hidden, (down_a, down_b), down_last)
    down_recv = send_b(down_parts)
    gate = tie("down_w", gate, down_parts, down_last)
    grad_ff, mlp_own, mlp_sent, gate_parts, up_parts = feed_back(
        gate, up_value, hidden, normed_two, grad_out_low, down_blocks
    )
    gate_recv = send_b(tie("gate_b", gate_parts, down_recv))
    up_parts = tie("up_b", up_parts, gate_recv, down_recv)
    up_recv = send_b(up_parts)
    down_row = add_b(down_parts, down_recv)
    down_recv_a = send_a(down_row)
    normed_part, sent = norm_back(tie("normed_part", grad_ff, gate_parts, down_recv), ff_w)
    received = swap(sent)
    grad_resid, grad_attended, out_rows, gain_two_part = resid_back(
        normed_part,
        received,
        resid,
        cotangents,
        factors,
        gain_two[None],
        attended_flat,
        attn_w,
        first,
    )
    gain_two_part = gain_two_part[0]

    grad_attended = grad_attended.reshape(2, local, query_width)
    down_own = add_a(tie("down_a", down_row, grad_attended), down_recv_a)
    down_recv_z = send_down_z(tie("down_back_z", down_own, grad_attended))
    gate_row = add_b(tie("gate_row", gate_parts, grad_attended), gate_recv)
    gate_recv_a = send_a(gate_row)
    gate_own = add_a(gate_row, gate_recv_a)
    grad_attended = tie(
        "back_0",
        grad_attended,
        down_recv,
        gate_recv,
        down_recv_a,
        out_rows,
        down_row,
        down_own,
        up_recv,
        gate_row,
        gate_own,
    )
    query_0, lat_0, up_0 = attend_back(
        0, queries, grad_attended, attended, keys, values, probs, lats, key_up, value_up, None
    )
    up_row = add_b(up_parts, up_recv)
    up_recv_a = send_a(up_row)
    up_own = add_a(up_row, up_recv_a)
    grad_attended = tie(
        "back_1",
        grad_attended,
        query_0,
        down_recv_a,
        up_recv,
        down_recv_z,
        up_row,
        down_own,
        gate_own,
        up_own,
    )
    query_1, lat_1, kv_grads = attend_back(
        1, queries, grad_attended, attended, keys, values, probs, lats, key_up, value_up, up_0
    )
    gate_recv_z = send_z(tie("gate_z", gate_own, grad_attended))
    lat_1 = tie("lat_back", list(lat_1), gate_own, up_row, up_recv_a, down_recv_z, gate_recv_z)
    lat_sum = jnp.concatenate([lat_0[0], lat_1[0]], axis=0).astype(F32)
    lat_recv = []
    for k in range(1, nz):
        sent = jnp.concatenate([lat_0[k], lat_1[k]], axis=0)
        lat_recv.append(lax.ppermute(sent, "z", [(i, i - k) for i in range(k, nz)]))
    kv_flat = kv_grads.reshape(depth, -1).astype(BF16)
    kv_parts = split_blocks(tie("kv", kv_flat, up_recv, lat_1), nz, True)
    kv_row = add_b(kv_parts, send_b(kv_parts))
    kv_row = tie("kv_a", kv_row, lat_recv)
    kv_own = add_a(kv_row, send_a(kv_row))
    grad_queries = jnp.concatenate([query_0[0], query_1[0]], axis=0)
    kv_z = tie("kv_z", kv_own, lat_recv, gate_recv_z)
    kv_recv = spread_ring(kv_z)[1:] if OPT.get("ring_kv", 0) else spread_z(kv_z)[1:]
    query_rows = dot(normed_one, tie("query_back", grad_queries, up_recv_a, lat_1, up_own), ROWS)
    normed_query = dot(tie("normed_query", grad_queries, lat_1), query_w, COLS)
    for part in lat_recv:
        lat_sum = lat_sum + part.astype(F32)
    grad_latent = tie("grad_latent", lat_sum.astype(BF16), query_rows, normed_query, kv_row, kv_own)
    grad_latent = grad_latent.reshape(2 * local, latent_width)
    last_rows = dot(normed_one, grad_latent, ROWS)
    attn_rows = [query_rows.astype(BF16), last_rows.astype(BF16), out_rows]
    attn_parts = list(split_blocks(jnp.concatenate(attn_rows, axis=1), nz))
    attn_recv = send_b(tie("attn_back", attn_parts, kv_row, kv_own))
    attn_row = add_b(attn_parts, attn_recv)
    attn_recv_a = send_a(attn_row)
    attn_own = add_a(attn_row, attn_recv_a)
    up_recv_z = send_z(
        tie("ff_back_z", up_own, lat_recv, gate_recv_z, kv_row, attn_recv, attn_recv_a, kv_recv)
    )
    attn_recv_z = send_z(tie("attn_back_z", attn_own, up_recv_z, kv_recv))
    normed_part = normed_query + dot(tie("normed_last", grad_latent, attn_parts), latent_w, COLS)
    gain_one_part = jnp.sum(normed_part * inputs * inv_one, axis=0)
    gains = jnp.stack([gain_one_part, gain_two_part])
    gains = tie("gains", gains, attn_parts, attn_recv, attn_recv_a, up_recv_z, kv_recv)
    gains = all_sum(gains, ("core", "x", "y", "z"))
    grad_normed = normed_part[:local] + swap(normed_part[local:].astype(BF16)).astype(F32)
    input_grad = (
        grad_resid + rms_back(grad_normed, inputs[:local], inv_one[:local], gain_one)
    ).astype(BF16)[None]
    mlp_sent = tie("mlp", mlp_sent, gate_parts, grad_attended, attn_parts)
    result = (resid[:local] + mlp_own + swap(mlp_sent).astype(F32)).astype(BF16)[None]
    kv_sum = kv_z.astype(F32)
    for part in tie("kv_sum", kv_recv, attn_parts, attn_recv, attn_recv_a):
        kv_sum = kv_sum + part.astype(F32)
    kv_sum = tie("kv_spread", kv_sum.astype(BF16), attn_parts, attn_recv, attn_recv_a)
    kv_a, kv_b = spread_own(kv_sum)
    kv_all = merge_blocks(spread_rest(kv_sum, kv_a, kv_b), fixed=True)
    kv_pair = in_order(core, kv_all[None], swap(kv_all)[None], 0).astype(F32)
    kv_pair = kv_pair.reshape((2,) + kv_grads.shape).transpose(1, 0, 3, 2, 4)
    kv_pair = kv_pair.reshape(2, KV_GROUPS, LATENT, query_width)

    def owned(totals):
        joined = jnp.concatenate(totals, axis=1).astype(BF16)
        received = swap(half(joined, other, 0))
        mine = half(joined, core, 0)
        results, start = [], 0
        for total in totals:
            width = total.shape[1]
            results.append(
                in_order(core, mine[:, start : start + width], received[:, start : start + width], 1)
                .astype(F32)
            )
            start += width
        return results

    gate_recv_z = tie("gate_last", gate_recv_z, attn_recv, attn_recv_a)
    up_recv_z = tie("up_last", up_recv_z, attn_recv, attn_recv_a)
    owned_gate, owned_up = owned([add_z(gate_own, gate_recv_z), add_z(up_own, up_recv_z)])
    owned_down = own_down(down_own, tie("down_last", down_recv_z, attn_recv, lat_recv, attn_recv_a))
    attn_total = add_z(attn_own, attn_recv_z)
    first = query_width + latent_width
    owned_query, owned_latent, owned_out = owned(
        [attn_total[:, :query_width], attn_total[:, query_width:first], attn_total[:, first:]]
    )
    return (
        result,
        input_grad,
        gains[0],
        owned_query,
        owned_latent,
        kv_pair[0],
        kv_pair[1],
        owned_out.T,
        gains[1],
        owned_gate,
        owned_up,
        owned_down,
    )


def solution(mesh):
    nz = mesh.shape["seq"]
    chips = mesh.shape["batch"] // 2
    nx = math.isqrt(chips)
    while chips % nx:
        nx -= 1
    fine = Mesh(mesh.devices.reshape(nz, chips // nx, nx, 2), ("z", "y", "x", "core"))
    batch = ("y", "x", "core")
    every = ("z",) + batch
    by_rows = P(every, None)
    in_specs = (
        P(batch, "z", None),
        P(batch, "z", None),
        P(batch),
        P(),
        P(),
        by_rows,
        by_rows,
        P(),
        P(),
        P(None, every),
        P(),
        by_rows,
        by_rows,
        by_rows,
    )
    out_specs = (
        P(batch, "z", None),
        P(batch, "z", None),
        P(),
        by_rows,
        by_rows,
        P(),
        P(),
        P(None, every),
        P(),
        by_rows,
        by_rows,
        by_rows,
    )
    return jax.shard_map(
        on_device, mesh=fine, in_specs=in_specs, out_specs=out_specs, check_vma=False
    )
```

```python
import math

import jax
import jax.numpy as jnp
from jax import lax
from jax.experimental import pallas as pl
from jax.experimental.pallas import tpu as pltpu
from jax.sharding import Mesh
from jax.sharding import PartitionSpec as P

HEADS = 16
HEAD_DIM = 64
LATENT = 256
KV_GROUPS = 2
GROUPS = 4
EPSILON = 1e-06
BF16 = jnp.bfloat16
F32 = jnp.float32
ROWS = (((0,), (0,)), ((), ()))
OPT = {"attn_z": 13, "back_0": 16, "back_1": 80, "c_attend": 4, "c_back": 3, "c_fb": 3, "c_ff": 3, "c_merge": 4, "c_mix": 4, "c_nb": 2, "c_rb": 4, "c_split": 4, "down_last": 2, "down_plane": 3, "down_z": 2, "ff_back_z": 24, "ff_late": 2, "ff_plane": 8, "ff_z": 2, "gains": 2, "gate_row": 1, "kv": 3, "kv_spread": 4, "kv_sum": 3, "kv_z": 3, "lat_back": 28, "normed_last": 1, "normed_part": 1, "normed_query": 1, "query_back": 6, "up_b": 1, "up_last": 1}
COLS = (((1,), (1,)), ((), ()))
PLAIN = (((1,), (0,)), ((), ()))


def dot(a, b, dims=PLAIN):
    return lax.dot_general(a, b, dims, preferred_element_type=F32)


PLANE = ("y", "x", "core")


def shift(values, axis, step):
    size = lax.axis_size(axis)
    return lax.ppermute(values, axis, [(i, (i + step) % size) for i in range(size)])


def leg(values, first, step):
    size = lax.axis_size("x")
    pairs = []
    for y in range(size):
        for x in range(size):
            for core in range(2):
                if (core == 0) == first:
                    target = (y, (x + step) % size, core)
                else:
                    target = ((y + step) % size, x, core)
                pairs.append(
                    ((y * size + x) * 2 + core, (target[0] * size + target[1]) * 2 + target[2])
                )
    return lax.ppermute(values, PLANE, pairs)


def swap(values):
    return shift(values, "core", 1)


def spread_z(shard):
    return [shard] + [shift(shard, "z", k) for k in range(1, lax.axis_size("z"))]


def spread_ring(shard):
    nz = lax.axis_size("z")
    pairs = [(z * 2 + c, (z + 1 - 2 * c) % nz * 2 + c) for z in range(nz) for c in range(2)]
    blocks = [shard]
    for _ in range(nz - 1):
        blocks.append(lax.ppermute(blocks[-1], ("z", "core"), pairs))
    return blocks


def spread_own(stack, late=None):
    size = lax.axis_size("x")
    late = stack if late is None else late
    return (
        [leg(stack, True, a) for a in range(1, size)],
        [leg(late, False, b) for b in range(1, size)],
    )


def spread_rest(stack, on_a, on_b):
    size = lax.axis_size("x")
    return [[stack] + on_a] + [
        [on_b[b - 1]] + [leg(block, False, b) for block in on_a] for b in range(1, size)
    ]


def after(value, *others):
    return lax.optimization_barrier((value,) + others)[0]


def tie(name, value, *others):
    mask = OPT.get(name, 0)
    chosen = [other for i, other in enumerate(others) if mask >> i & 1]
    return after(value, *chosen) if chosen else value


def cost(name, flops):
    return pl.CostEstimate(
        flops=int(flops * OPT.get(name, 0) / 4), bytes_accessed=4096, transcendentals=0
    )


def send_b(parts):
    return [leg(parts[b], False, b) for b in range(1, len(parts))]


def add_b(parts, received):
    row = parts[0]
    for part in received:
        row = add(row, part)
    return row


def send_a(row):
    return [leg(row[a], True, a) for a in range(1, row.shape[0])]


def add_a(row, received):
    own = row[0]
    for part in received:
        own = add(own, part)
    return own


RING = bool(OPT.get("ring_back", 0))


def ring(values):
    nz = lax.axis_size("z")
    pairs = [(z * 2 + c, (z + 1 - 2 * c) % nz * 2 + c) for z in range(nz) for c in range(2)]
    return lax.ppermute(values, ("z", "core"), pairs)


def back_away(k):
    return k * (2 * lax.axis_index("core") - 1) if RING else k


def send_z(own):
    if not RING:
        return [shift(own[k], "z", k) for k in range(1, own.shape[0])]
    part = own[1]
    for k in range(2, own.shape[0]):
        part = add(own[k], ring(part))
    return [ring(part)]


def add_z(own, received):
    total = own[0].astype(F32)
    for part in received:
        total = total + part.astype(F32)
    return total


def add(left, right):
    return (left.astype(F32) + right.astype(F32)).astype(BF16)


def to_half(values, step):
    nz = lax.axis_size("z")
    pairs = []
    for z in range(nz):
        keeper = z // (nz // 2)
        source = z * 2 + (keeper if step else 1 - keeper)
        pairs.append((source, (z + step) % nz * 2 + keeper))
    return lax.ppermute(values, ("z", "core"), pairs)


def spread_down_z(chip):
    nz, z, core = lax.axis_size("z"), lax.axis_index("z"), lax.axis_index("core")
    return [chip] + [to_half(chip, k) for k in range(1, nz)]


def down_stack(received):
    nz, z, core = lax.axis_size("z"), lax.axis_index("z"), lax.axis_index("core")
    received = jnp.stack(received)
    parts = []
    for j in range(nz // 2):
        step = lax.rem(z + nz - core * (nz // 2) - j, nz)
        parts.append(lax.dynamic_slice_in_dim(received, step, 1, 0))
    return jnp.concatenate(parts, axis=0)


def down_block(own, chip_z):
    count = own.shape[0]
    index = jnp.clip(chip_z - lax.axis_index("core") * count, 0, count - 1)
    return lax.dynamic_index_in_dim(own, index, 0, keepdims=False)


def send_down_z(own):
    nz, z, count = lax.axis_size("z"), lax.axis_index("z"), own.shape[0]
    received = []
    for k in range(1, nz):
        pairs = [((d + k) % nz * 2 + d // count, d * 2 + d // count) for d in range(nz)]
        part = down_block(own, lax.rem(z + nz - k, nz))
        received.append(lax.ppermute(part, ("z", "core"), pairs))
    return received


def own_down(own, received):
    nz, z, core = lax.axis_size("z"), lax.axis_index("z"), lax.axis_index("core")
    count = nz // 2
    total = down_block(own, z).astype(F32)
    for part in received:
        total = total + part.astype(F32)
    pairs = [(d * 2 + d // count, d * 2 + 1 - d // count) for d in range(nz)]
    sent = lax.ppermute(half(total, 1 - core, 0).astype(BF16), ("z", "core"), pairs)
    return jnp.where(core == z // count, half(total, core, 0), sent.astype(F32))


def place(size, nz, k, b, a):
    core = lax.axis_index("core")
    z = lax.rem(lax.axis_index("z") + nz + k, nz)
    y = lax.rem(lax.axis_index("y") + size + b + core * (a - b), size)
    x = lax.rem(lax.axis_index("x") + size + a + core * (b - a), size)
    return z, y, x


def merge_blocks(blocks, fixed=False, ring=False):
    size = len(blocks)
    nz, rows, columns = blocks[0][0].shape
    parts = [block for row in blocks for block in row]

    def kernel(*refs):
        out, sems = refs[-2], refs[-1]
        copies = []
        for b in range(size):
            for a in range(size):
                for k in range(nz):
                    away = k * (2 * lax.axis_index("core") - 1) if ring else -k
                    z, y, x = place(size, nz, away, -b, -a)
                    n = b * size + a
                    copies.append(
                        pltpu.make_async_copy(
                            refs[n].at[k], out.at[k if fixed else z, y, x], sems.at[n * nz + k]
                        )
                    )
        for copy in copies:
            copy.start()
        for copy in copies:
            copy.wait()

    out = pl.pallas_call(
        kernel,
        out_shape=jax.ShapeDtypeStruct((nz, size, size, rows, columns), parts[0].dtype),
        in_specs=[pl.BlockSpec(memory_space=pl.ANY)] * len(parts),
        out_specs=pl.BlockSpec(memory_space=pltpu.VMEM),
        scratch_shapes=[pltpu.SemaphoreType.DMA((nz * size * size,))],
        compiler_params=pltpu.CompilerParams(vmem_limit_bytes=48 * 2**20),
        cost_estimate=cost("c_merge", 3e9),
        name="merge",
    )(*parts)
    return out.reshape(nz * size * size * rows, columns)


def split_blocks(full, nz, fixed=False):
    size = lax.axis_size("x")
    rows = full.shape[0] // (nz * size * size)
    columns = full.shape[1]

    def kernel(*refs):
        source, outs, sems = refs[0], refs[1:-1], refs[-1]
        copies = []
        for b in range(size):
            for a in range(size):
                for k in range(nz):
                    z, y, x = place(size, nz, back_away(k), b, a)
                    copies.append(
                        pltpu.make_async_copy(
                            source.at[k if fixed else z, y, x],
                            outs[b].at[a, k],
                            sems.at[(b * size + a) * nz + k],
                        )
                    )
        for copy in copies:
            copy.start()
        for copy in copies:
            copy.wait()

    return pl.pallas_call(
        kernel,
        out_shape=[jax.ShapeDtypeStruct((size, nz, rows, columns), full.dtype)] * size,
        in_specs=[pl.BlockSpec(memory_space=pltpu.VMEM)],
        out_specs=[pl.BlockSpec(memory_space=pl.ANY)] * size,
        scratch_shapes=[pltpu.SemaphoreType.DMA((nz * size * size,))],
        compiler_params=pltpu.CompilerParams(vmem_limit_bytes=48 * 2**20),
        cost_estimate=cost("c_split", 3e9),
        name="split",
    )(full.reshape(nz, size, size, rows, columns))


def all_sum(values, axes):
    for axis in axes:
        size = lax.axis_size(axis)
        total = values
        for k in range(1, size):
            total = total + shift(values, axis, k)
        values = total
    return values


def head_halves(pair):
    lane = lax.broadcasted_iota(jnp.int32, pair.shape, 1)
    zero = jnp.zeros_like(pair)
    return jnp.concatenate(
        [jnp.where(lane < HEAD_DIM, pair, zero), jnp.where(lane >= HEAD_DIM, pair, zero)], axis=0
    )


def join_halves(halves):
    rows = halves.shape[0] // 2
    lane = lax.broadcasted_iota(jnp.int32, (rows, halves.shape[1]), 1)
    return jnp.where(lane < HEAD_DIM, halves[:rows], halves[rows:])


def attend_kernel(nz, q_ref, *refs):
    lats, (wk_ref, wv_ref, att_ref, key_ref, value_ref, prob_ref) = refs[:nz], refs[nz:]
    local = q_ref.shape[1]
    z = lax.axis_index("z")
    q2 = head_halves(q_ref[0] * BF16(HEAD_DIM**-0.5))
    wk, wv = wk_ref[...], wv_ref[...]
    scores = []
    for k in range(nz):
        lat = lats[k][0]
        key = dot(lat, wk).astype(BF16)
        value = dot(lat, wv).astype(BF16)
        key_ref[0, k * local : (k + 1) * local] = key
        value_ref[0, k * local : (k + 1) * local] = value
        block = dot(q2, key, COLS)
        if k == 0:
            row = lax.rem(lax.broadcasted_iota(jnp.int32, block.shape, 0), local)
            column = lax.broadcasted_iota(jnp.int32, block.shape, 1)
            block = jnp.where(column <= row, block, -1e30)
        else:
            block = block + jnp.where(z >= k, 0.0, -1e30)
        scores.append(block)
    top = scores[0]
    for block in scores[1:]:
        top = jnp.maximum(top, block)
    top = jnp.max(top, axis=1, keepdims=True)
    exps = [jnp.exp(block - top) for block in scores]
    total = exps[0]
    for block in exps[1:]:
        total = total + block
    inverse = 1.0 / jnp.sum(total, axis=1, keepdims=True)
    mixed = jnp.zeros((2 * local, q_ref.shape[2]), F32)
    for k in range(nz):
        prob = (exps[k] * inverse).astype(BF16)
        prob_ref[0, 0, k] = prob
        mixed = mixed + dot(prob, value_ref[0, k * local : (k + 1) * local])
    att_ref[0] = join_halves(mixed).astype(BF16)


def attend(queries, lats, key_up, value_up):
    seqs, local, width = queries.shape
    nz = len(lats)
    pairs = width // 128
    query_spec = pl.BlockSpec((1, local, 128), lambda s, h: (s, 0, h))
    full_spec = pl.BlockSpec((1, nz * local, 128), lambda s, h: (s, 0, h))
    lat_spec = pl.BlockSpec((1, local, LATENT), lambda s, h: (s, 0, 0))
    up_spec = pl.BlockSpec((LATENT, 128), lambda s, h: (0, h))
    full = jax.ShapeDtypeStruct((seqs, nz * local, width), BF16)
    return pl.pallas_call(
        lambda *refs: attend_kernel(nz, *refs),
        grid=(seqs, pairs),
        in_specs=[query_spec] + [lat_spec] * nz + [up_spec] * 2,
        out_specs=[
            query_spec,
            full_spec,
            full_spec,
            pl.BlockSpec((1, 1, nz, 2 * local, local), lambda s, h: (s, h, 0, 0, 0)),
        ],
        out_shape=[
            jax.ShapeDtypeStruct(queries.shape, BF16),
            full,
            full,
            jax.ShapeDtypeStruct((seqs, pairs, nz, 2 * local, local), BF16),
        ],
        compiler_params=pltpu.CompilerParams(vmem_limit_bytes=48 * 2**20),
        cost_estimate=cost("c_attend", 16e9),
        name="attend",
    )(queries, *lats, key_up, value_up)


def attend_back_kernel(nz, pairs, first, q_ref, g_ref, att_ref, key_ref, value_ref, prob_ref, *refs):
    lats, (wk_ref, wv_ref, old_ref), rest = refs[:nz], refs[nz : nz + 3], refs[nz + 3 :]
    dq_ref, dlats, (up_ref, lat_acc) = rest[0], rest[1 : nz + 1], rest[nz + 1 :]
    pair = pl.program_id(0)
    local = q_ref.shape[1]
    scale = HEAD_DIM**-0.5
    grad = g_ref[0].astype(F32)
    query = head_halves(q_ref[0].astype(F32) * scale)
    g2 = head_halves(grad)
    inner = jnp.sum(head_halves(grad * att_ref[0].astype(F32)), axis=1, keepdims=True)
    query_t, g2_t = query.T.astype(BF16), g2.T.astype(BF16)
    g2 = g2.astype(BF16)
    @pl.when(pair == 0)
    def _():
        lat_acc[...] = jnp.zeros_like(lat_acc)

    dq = jnp.zeros((2 * local, 128), F32)
    up_key = jnp.zeros((128, LATENT), F32)
    up_value = jnp.zeros((128, LATENT), F32)
    for k in range(nz):
        rows = slice(k * local, (k + 1) * local)
        prob = prob_ref[0, 0, k]
        key, value = key_ref[0, rows], value_ref[0, rows]
        grad_prob = dot(g2, value, COLS)
        grad_score = (prob.astype(F32) * (grad_prob - inner)).astype(BF16)
        dq = dq + dot(grad_score, key)
        grad_key = dot(query_t, grad_score).astype(BF16)
        grad_value = dot(g2_t, prob).astype(BF16)
        term = dot(wk_ref[...], grad_key) + dot(wv_ref[...], grad_value)

        lat_acc[:, rows] += term
        lat = lats[k][0]
        up_key = up_key + dot(grad_key, lat)
        up_value = up_value + dot(grad_value, lat)
    dq_ref[0] = (join_halves(dq) * scale).astype(BF16)
    up_ref[0, 0] = up_key.T if first else up_key.T + old_ref[0, 0]
    up_ref[1, 0] = up_value.T if first else up_value.T + old_ref[1, 0]

    @pl.when(pair == pairs - 1)
    def _():
        for k in range(nz):
            dlats[k][0] = lat_acc[:, k * local : (k + 1) * local].T.astype(BF16)


def attend_back(seq, queries, grad_att, attended, keys, values, probs, lats, key_up, value_up, old):
    _, local, width = queries.shape
    nz = len(lats)
    pairs = width // 128
    query_spec = pl.BlockSpec((1, local, 128), lambda h: (seq, 0, h))
    full_spec = pl.BlockSpec((1, nz * local, 128), lambda h: (seq, 0, h))
    lat_spec = pl.BlockSpec((1, local, LATENT), lambda h: (seq, 0, 0))
    up_spec = pl.BlockSpec((LATENT, 128), lambda h: (0, h))
    prob_spec = pl.BlockSpec((1, 1, nz, 2 * local, local), lambda h: (seq, h, 0, 0, 0))
    grad_spec = pl.BlockSpec((2, 1, LATENT, 128), lambda h: (0, h, 0, 0))
    outs = pl.pallas_call(
        lambda *refs: attend_back_kernel(nz, pairs, old is None, *refs),
        grid=(pairs,),
        in_specs=[query_spec] * 3
        + [full_spec] * 2
        + [prob_spec]
        + [lat_spec] * nz
        + [up_spec] * 2
        + [pl.BlockSpec(memory_space=pl.ANY) if old is None else grad_spec],
        out_specs=[pl.BlockSpec((1, local, 128), lambda h: (0, 0, h))]
        + [pl.BlockSpec((1, local, LATENT), lambda h: (0, 0, 0))] * nz
        + [grad_spec],
        out_shape=[jax.ShapeDtypeStruct((1, local, width), BF16)]
        + [jax.ShapeDtypeStruct((1, local, LATENT), BF16)] * nz
        + [jax.ShapeDtypeStruct((2, pairs, LATENT, 128), F32)],
        scratch_shapes=[pltpu.VMEM((LATENT, nz * local), F32)],
        compiler_params=pltpu.CompilerParams(vmem_limit_bytes=48 * 2**20),
        cost_estimate=cost("c_back", 17e9),
        name="attend_back",
    )(queries, grad_att, attended, keys, values, probs, *lats, key_up, value_up,
      key_up if old is None else old)
    return outs[0], outs[1 : nz + 1], outs[nz + 1]


VMEM = pl.BlockSpec(memory_space=pltpu.VMEM)
ANY = pl.BlockSpec(memory_space=pl.ANY)
PARAMS = pltpu.CompilerParams(vmem_limit_bytes=56 * 2**20)


def chunks(width):
    return [slice(start, min(start + 256, width)) for start in range(0, width, 256)]


def row_blocks(count, body):
    @pl.loop(0, count, step=64)
    def _(start):
        body(pl.ds(pl.multiple_of(start, 64), 64))


def block_copies(size, nz, sems, make):
    copies = []
    for b in range(size):
        for a in range(size):
            for k in range(nz):
                copies.append(make(b, a, k, sems.at[(b * size + a) * nz + k]))
    for copy in copies:
        copy.start()
    return copies


def mix_heads(attended, attn_w, first):
    rows, width = attended.shape
    depth = attn_w.shape[0]
    local = rows // 2

    def kernel(att_ref, w_ref, sent_ref, out_w, sem):
        copy = pltpu.make_async_copy(w_ref.at[:, pl.ds(first, width)], out_w, sem)
        copy.start()
        copy.wait()
        sent_ref[:local] = dot(att_ref[local:], out_w[...], COLS).astype(BF16)
        sent_ref[local:] = dot(att_ref[:local], out_w[...], COLS).astype(BF16)

    return pl.pallas_call(
        kernel,
        in_specs=[VMEM, ANY],
        out_specs=VMEM,
        out_shape=jax.ShapeDtypeStruct((rows, depth), BF16),
        scratch_shapes=[pltpu.VMEM((depth, width), BF16), pltpu.SemaphoreType.DMA],
        compiler_params=pltpu.CompilerParams(vmem_limit_bytes=16 * 2**20),
        cost_estimate=cost("c_mix", 2e9),
        name="mix_heads",
    )(attended, attn_w)


def feed_forward(tokens, attended, attn_w, first, mixed, gain, grad_low, blocks):
    size = len(blocks)
    nz, block_rows, wide = blocks[0][0].shape
    rows, heads_width = attended.shape
    depth = tokens.shape[1]
    width = wide // 2
    half_z = nz // 2
    down_rows = width // (half_z * size * size)
    direct = block_rows % 16 == 0 and down_rows % 16 == 0
    flat = [block for row in blocks for block in row]
    if not direct:
        flat = [merge_blocks(blocks)]
    shapes = [
        ((rows, depth), F32),
        ((rows, depth), BF16),
        ((depth, wide), BF16),
        ((rows, width), BF16),
        ((rows, width), BF16),
        ((rows, width), BF16),
    ]

    def kernel(x_ref, att_ref, mix_ref, gain_ref, go_ref, attn_ref, *refs):
        sources, refs = refs[: len(flat)], refs[len(flat) :]
        leaving, outs = refs[:6], refs[6 : 6 + (size if direct else 1)]
        held, (out_w, grad_ref, sem, held_sems, in_sems, out_sems) = refs[-12:-6], refs[-6:]
        resid_ref, norm_ref, w_ref, gate_ref, up_ref, hid_ref = held

        def fetch(b, a, k, sem):
            z, y, x = place(size, nz, -k, -b, -a)
            start = ((z * size + y) * size + x) * block_rows
            target = w_ref.at[pl.ds(pl.multiple_of(start, 16), block_rows)]
            return pltpu.make_async_copy(sources[b * size + a].at[k], target, sem)

        first_copy = pltpu.make_async_copy(attn_ref.at[:, pl.ds(first, heads_width)], out_w, sem)
        first_copy.start()
        if direct:
            copies = block_copies(size, nz, in_sems, fetch)
        else:
            copies = [pltpu.make_async_copy(sources[0], w_ref, in_sems.at[0])]
            copies[0].start()
        out_copies = [
            pltpu.make_async_copy(held[i], leaving[i], held_sems.at[i]) for i in range(6)
        ]
        first_copy.wait()
        resid_ref[...] = dot(att_ref[...], out_w[...], COLS)

        def norm(at):
            resid = x_ref[at].astype(F32) + resid_ref[at] + mix_ref[at].astype(F32)
            resid_ref[at] = resid
            norm_ref[at] = (resid * inverse_rms(resid) * gain_ref[...]).astype(BF16)

        row_blocks(rows, norm)
        out_copies[0].start()
        out_copies[1].start()
        for copy in copies:
            copy.wait()
        out_copies[2].start()
        normed = norm_ref[...]
        low = go_ref[...]
        for at in chunks(width):
            gate = dot(normed, w_ref[:, at])
            up = dot(normed, w_ref[:, width + at.start : width + at.stop])
            gate_ref[:, at] = gate.astype(BF16)
            up_ref[:, at] = up.astype(BF16)
            hid_ref[:, at] = (gate * jax.nn.sigmoid(gate) * up).astype(BF16)
        for copy in out_copies[3:]:
            copy.start()
        for at in chunks(width):
            grad_ref[at] = dot(hid_ref[:, at], low, ROWS).astype(BF16)

        def leave(b, a, k, sem):
            _, y, x = place(size, nz, 0, b, a)
            start = ((k * size + y) * size + x) * down_rows
            source = grad_ref.at[pl.ds(pl.multiple_of(start, 16), down_rows)]
            return pltpu.make_async_copy(source, outs[b].at[a, k], sem)

        if direct:
            copies = block_copies(size, half_z, out_sems, leave)
        else:
            copies = [pltpu.make_async_copy(grad_ref, outs[0], out_sems.at[0])]
            copies[0].start()
        for copy in copies + out_copies:
            copy.wait()

    outs = pl.pallas_call(
        kernel,
        in_specs=[VMEM] * 5 + [ANY] * (1 + len(flat)),
        out_specs=[ANY] * (6 + (size if direct else 1)),
        out_shape=[jax.ShapeDtypeStruct(*shape) for shape in shapes]
        + (
            [jax.ShapeDtypeStruct((size, half_z, down_rows, depth), BF16)] * size
            if direct
            else [jax.ShapeDtypeStruct((width, depth), BF16)]
        ),
        scratch_shapes=[pltpu.VMEM(*shape) for shape in shapes]
        + [
            pltpu.VMEM((depth, heads_width), BF16),
            pltpu.VMEM((width, depth), BF16),
            pltpu.SemaphoreType.DMA,
            pltpu.SemaphoreType.DMA((6,)),
            pltpu.SemaphoreType.DMA((nz * size * size,)),
            pltpu.SemaphoreType.DMA((half_z * size * size,)),
        ],
        compiler_params=PARAMS,
        cost_estimate=cost("c_ff", 14e9),
        name="feed_forward",
    )(tokens, attended, mixed, gain, grad_low, attn_w, *flat)
    parts = list(outs[6:]) if direct else split_blocks(outs[6], half_z, True)
    return (*outs[:6], list(parts))


def feed_back(gate, up, hidden, normed, grad_low, blocks):
    size = len(blocks)
    half_z, block_rows, depth = blocks[0][0].shape
    nz = half_z * 2
    rows, width = gate.shape
    wide = 2 * width
    local = rows // 2
    grad_rows = depth // (nz * size * size)
    direct = block_rows % 16 == 0 and grad_rows % 16 == 0
    flat = [block for row in blocks for block in row]
    if not direct:
        flat = [merge_blocks(blocks, True)]
    parts = chunks(width)

    def kernel(norm_ref, go_ref, gate_in, up_in, hid_in, *refs):
        sources, refs = refs[: len(flat)], refs[len(flat) :]
        grad_out, own_ref, sent_ref = refs[:3]
        outs, refs = refs[3:-9], refs[-9:]
        w_ref, dw_ref, gate_ref, up_ref, hid_ref, grad_ref, sems, in_sems, out_sems = refs

        def fetch(b, a, k, sem):
            _, y, x = place(size, nz, 0, -b, -a)
            start = ((k * size + y) * size + x) * block_rows
            target = w_ref.at[pl.ds(pl.multiple_of(start, 16), block_rows)]
            return pltpu.make_async_copy(sources[b * size + a].at[k], target, sem)

        if direct:
            copies = block_copies(size, half_z, in_sems, fetch)
        else:
            copies = [pltpu.make_async_copy(sources[0], w_ref, in_sems.at[0])]
            copies[0].start()
        arriving = []
        for i, at in enumerate(parts):
            span = pl.ds(at.start, at.stop - at.start)
            arriving.append(
                [
                    pltpu.make_async_copy(source.at[:, span], target.at[:, span], sems.at[3 * i + j])
                    for j, (source, target) in enumerate(
                        ((gate_in, gate_ref), (up_in, up_ref), (hid_in, hid_ref))
                    )
                ]
            )
            for copy in arriving[-1]:
                copy.start()
        normed = norm_ref[...]
        for copy in copies:
            copy.wait()
        low = go_ref[...]
        for i, at in enumerate(parts):
            for copy in arriving[i]:
                copy.wait()
            grad_hidden = dot(low, w_ref[at], COLS)
            gate = gate_ref[:, at].astype(F32)
            sigma = jax.nn.sigmoid(gate)
            grad_gate = grad_hidden * up_ref[:, at].astype(F32) * sigma * (1.0 + gate * (1.0 - sigma))
            grad_up = grad_hidden * (gate * sigma)
            other = slice(width + at.start, width + at.stop)
            grad_ref[:, at] = grad_gate.astype(BF16)
            grad_ref[:, other] = grad_up.astype(BF16)
            dw_ref[:, at] = dot(normed, grad_ref[:, at], ROWS).astype(BF16)
            dw_ref[:, other] = dot(normed, grad_ref[:, other], ROWS).astype(BF16)

        def leave(part):
            def make(b, a, k, sem):
                z, y, x = place(size, nz, back_away(k), b, a)
                start = ((z * size + y) * size + x) * grad_rows
                rows_at = pl.ds(pl.multiple_of(start, 16), grad_rows)
                source = dw_ref.at[rows_at, pl.ds(part * width, width)]
                return pltpu.make_async_copy(source, outs[part * size + b].at[a, k], sem)

            return make

        if direct:
            copies = []
            for part in range(2):
                copies += block_copies(size, nz, out_sems.at[part], leave(part))
        else:
            copies = []
            for part in range(2):
                source = dw_ref.at[:, pl.ds(part * width, width)]
                copies.append(pltpu.make_async_copy(source, outs[part], out_sems.at[part, 0]))
                copies[-1].start()
        last = pltpu.make_async_copy(grad_ref, grad_out, sems.at[3 * len(parts)])
        last.start()
        own_ref[...] = dot(hid_ref[:local], w_ref[...])
        sent_ref[...] = dot(hid_ref[local:], w_ref[...]).astype(BF16)
        for copy in copies + [last]:
            copy.wait()

    outs = pl.pallas_call(
        kernel,
        in_specs=[VMEM] * 2 + [ANY] * (3 + len(flat)),
        out_specs=[ANY] + [VMEM] * 2 + [ANY] * (2 * size if direct else 2),
        out_shape=[
            jax.ShapeDtypeStruct((rows, wide), BF16),
            jax.ShapeDtypeStruct((local, depth), F32),
            jax.ShapeDtypeStruct((local, depth), BF16),
        ]
        + (
            [jax.ShapeDtypeStruct((size, nz, grad_rows, width), BF16)] * (2 * size)
            if direct
            else [jax.ShapeDtypeStruct((depth, width), BF16)] * 2
        ),
        scratch_shapes=[
            pltpu.VMEM((width, depth), BF16),
            pltpu.VMEM((depth, wide), BF16),
            pltpu.VMEM((rows, width), BF16),
            pltpu.VMEM((rows, width), BF16),
            pltpu.VMEM((rows, width), BF16),
            pltpu.VMEM((rows, wide), BF16),
            pltpu.SemaphoreType.DMA((3 * len(parts) + 1,)),
            pltpu.SemaphoreType.DMA((half_z * size * size,)),
            pltpu.SemaphoreType.DMA((2, nz * size * size)),
        ],
        compiler_params=PARAMS,
        cost_estimate=cost("c_fb", 18e9),
        name="feed_back",
    )(normed, grad_low, gate, up, hidden, *flat)
    if direct:
        parts = [list(outs[3 : 3 + size]), list(outs[3 + size :])]
    else:
        parts = [list(split_blocks(part, nz)) for part in outs[3:]]
    return outs[0], outs[1], outs[2], *parts


def norm_back(grad_ff, ff_w):
    rows, wide = grad_ff.shape
    depth = ff_w.shape[0]
    local = rows // 2

    def kernel(grad_ref, w_ref, part_ref, sent_ref):
        for at in chunks(depth):
            part = dot(grad_ref[...], w_ref[at], COLS)
            part_ref[:, at] = part
            sent_ref[:local, at] = part[local:].astype(BF16)
            sent_ref[local:, at] = part[:local].astype(BF16)

    return pl.pallas_call(
        kernel,
        in_specs=[VMEM] * 2,
        out_specs=[VMEM] * 2,
        out_shape=[
            jax.ShapeDtypeStruct((rows, depth), F32),
            jax.ShapeDtypeStruct((rows, depth), BF16),
        ],
        compiler_params=pltpu.CompilerParams(vmem_limit_bytes=32 * 2**20),
        cost_estimate=cost("c_nb", 6e9),
        name="norm_back",
    )(grad_ff, ff_w)


def resid_back(normed_part, received, resid, cotangents, factors, gain, attended, attn_w, first):
    rows, depth = resid.shape
    width = attended.shape[1]
    local = rows // 2

    def kernel(part_ref, recv_ref, resid_ref, cot_ref, gain_ref, att_ref, fac_ref, w_ref, *refs):
        grad_ref, datt_ref, dw_ref, dg_ref, low_ref, sum_ref, out_w, sem = refs
        copy = pltpu.make_async_copy(w_ref.at[:, pl.ds(first, width)], out_w, sem)
        copy.start()
        sum_ref[...] = jnp.zeros_like(sum_ref)

        def norm(at):
            resid = resid_ref[at]
            part = part_ref[at]
            inverse = inverse_rms(resid)
            scaled = resid * inverse
            gains = part * scaled
            total = gains[:8]
            for row in range(8, 64, 8):
                total = total + gains[row : row + 8]
            sum_ref[...] += total
            weighted = (part + recv_ref[at].astype(F32)) * gain_ref[...]
            mean = jnp.mean(weighted * scaled, axis=-1, keepdims=True)
            factor = jnp.where(at.start < local, fac_ref[0], fac_ref[1])
            grad = cot_ref[at].astype(F32) * factor + inverse * (weighted - scaled * mean)
            low_ref[at] = grad.astype(BF16)

            @pl.when(at.start < local)
            def _():
                grad_ref[at] = grad

        row_blocks(rows, norm)
        dg_ref[...] = jnp.sum(sum_ref[...], axis=0, keepdims=True)
        copy.wait()
        low = low_ref[...]
        datt_ref[...] = dot(low, out_w[...]).astype(BF16)
        dw_ref[...] = dot(low, att_ref[...], ROWS).astype(BF16)

    return pl.pallas_call(
        kernel,
        in_specs=[VMEM] * 6 + [pl.BlockSpec(memory_space=pltpu.SMEM), ANY],
        out_specs=[VMEM] * 4,
        out_shape=[
            jax.ShapeDtypeStruct((local, depth), F32),
            jax.ShapeDtypeStruct((rows, width), BF16),
            jax.ShapeDtypeStruct((depth, width), BF16),
            jax.ShapeDtypeStruct((1, depth), F32),
        ],
        scratch_shapes=[
            pltpu.VMEM((rows, depth), BF16),
            pltpu.VMEM((8, depth), F32),
            pltpu.VMEM((depth, width), BF16),
            pltpu.SemaphoreType.DMA,
        ],
        compiler_params=pltpu.CompilerParams(vmem_limit_bytes=32 * 2**20),
        cost_estimate=cost("c_rb", 4e9),
        name="resid_back",
    )(normed_part, received, resid, cotangents, gain, attended, factors, attn_w)


def half(values, which, axis=1):
    size = values.shape[axis] // 2
    return lax.dynamic_slice_in_dim(values, which * size, size, axis)


def in_order(core, own, other, axis):
    return jnp.where(
        core == 0,
        jnp.concatenate([own, other], axis=axis),
        jnp.concatenate([other, own], axis=axis),
    )


def rms_back(grad_normed, inputs, inv_rms, gain):
    weighted = grad_normed * gain
    return inv_rms * weighted - inputs * inv_rms**3 * jnp.mean(
        weighted * inputs, axis=-1, keepdims=True
    )


def inverse_rms(values):
    return lax.rsqrt(jnp.mean(values * values, axis=-1, keepdims=True) + EPSILON)


def on_device(
    tokens,
    cotangent,
    group_ids,
    loss_weight,
    gain_attn,
    w_query,
    w_latent,
    w_key_up,
    w_value_up,
    w_out,
    gain_mlp,
    w_gate,
    w_up,
    w_down,
):
    nz, ny, nx = lax.axis_size("z"), lax.axis_size("y"), lax.axis_size("x")
    core = lax.axis_index("core")
    other = 1 - core
    local, depth = tokens.shape[1:]
    latent_width = w_latent.shape[1] // 2
    hidden_width = w_gate.shape[1] // 2
    query_width = w_query.shape[1] // 2
    gain_one = gain_attn.astype(F32)
    gain_two = gain_mlp.astype(F32)

    out_t = w_out.T
    row_parts = [w_query, w_latent, out_t, w_gate, w_up]
    mine = [half(part, core) for part in row_parts]
    theirs = [half(part, other) for part in row_parts]
    attn_recv = swap(jnp.concatenate(theirs[:3], axis=1))
    ff_recv = swap(jnp.concatenate(theirs[3:], axis=1))
    down_recv = to_half(w_down, 0)
    both = swap(jnp.concatenate([tokens, cotangent], axis=0))
    onehot = (group_ids[:, None] == jnp.arange(GROUPS, dtype=jnp.int32)[None, :]).astype(F32)
    onehot_other = swap(onehot)
    attn_shard = in_order(core, jnp.concatenate(mine[:3], axis=1), attn_recv, 0)
    ff_shard = in_order(core, jnp.concatenate(mine[3:], axis=1), ff_recv, 0)
    down_chip = in_order(core, w_down, down_recv, 0)

    counts = jnp.sum(onehot, axis=0) + jnp.sum(onehot_other, axis=0)
    counts = all_sum(counts, ("x", "y"))
    attn_shard = tie("attn_z", attn_shard, both, ff_shard, down_chip, onehot_other)
    attn_z = spread_z(attn_shard)
    attn_stack = tie("attn_plane", jnp.stack(attn_z), counts, ff_shard, down_chip)
    attn_a, attn_b = spread_own(attn_stack)
    attn_blocks = spread_rest(attn_stack, attn_a, attn_b)
    ff_shard = tie("ff_z", ff_shard, attn_z, counts)
    ff_z = spread_z(ff_shard)

    tokens_both = jnp.concatenate([tokens[0], both[0]], axis=0)
    inputs = tokens_both.astype(F32)
    inv_one = inverse_rms(inputs)
    normed_one = (inputs * inv_one * gain_one).astype(BF16)
    total_seqs = ny * nx * 2 * group_ids.shape[0]

    def factor(row):
        return jnp.sum(row * loss_weight) * (total_seqs / GROUPS) / jnp.sum(row * counts)

    factors = jnp.stack([factor(onehot[0]), factor(onehot_other[0])])
    cotangents = jnp.concatenate([cotangent[0], both[1]], axis=0)
    grad_out_low = (
        cotangents.astype(F32) * jnp.repeat(factors, local)[:, None]
    ).astype(BF16)

    attn_w = merge_blocks(attn_blocks)
    query_w = attn_w[:, :query_width]
    latent_w = attn_w[:, query_width : query_width + latent_width]
    latent = dot(normed_one, latent_w).astype(BF16).reshape(2, local, latent_width)
    latent = tie("lat", latent, ff_z)
    key_up = lax.dynamic_index_in_dim(w_key_up, core, 0, keepdims=False)
    value_up = lax.dynamic_index_in_dim(w_value_up, core, 0, keepdims=False)
    lats = [latent]
    for _ in range(1, nz):
        lats.append(lax.ppermute(lats[-1], "z", [(i, i + 1) for i in range(nz - 1)]))
    ff_z = tie("ff_plane", ff_z, attn_a, attn_b, attn_blocks[-1][-1], latent, lats[1:])
    ff_stack = jnp.stack(ff_z)
    ff_a, ff_b = spread_own(ff_stack, tie("ff_late", ff_stack, lats[1:], attn_blocks[-1][-1]))
    ff_blocks = spread_rest(
        ff_stack, [tie("ff_rest", part, lats, attn_blocks[-1][-1]) for part in ff_a], ff_b
    )
    ff_last = ff_blocks[-1][-1]
    down_z = spread_down_z(tie("down_z", down_chip, ff_z, lats, (ff_a, ff_b), ff_last))
    down_own = tie("down_plane", down_stack(down_z), (ff_a, ff_b), ff_last)
    down_a, down_b = spread_own(down_own)
    queries = dot(normed_one, query_w).astype(BF16).reshape(2, local, query_width)
    queries = tie("attend", queries, (ff_a, ff_b), down_z, ff_last, ff_a)
    attended, keys, values, probs = attend(queries, lats, key_up, value_up)
    attended_flat = tie("post", attended, (ff_a, ff_b), ff_last, down_z, (down_a, down_b), ff_a)
    attended_flat = attended_flat.reshape(2 * local, query_width)
    first = query_width + latent_width
    mixed = swap(mix_heads(attended_flat, attn_w, first))

    mixed = tie("gate", mixed, down_z, (down_a, down_b), (ff_a, ff_b), ff_last)
    resid, normed_two, ff_w, gate, up_value, hidden, down_parts = feed_forward(
        tokens_both, attended_flat, attn_w, first, mixed, gain_two[None], grad_out_low, ff_blocks
    )
    down_blocks = spread_rest(down_own, tie("down_rest", down_a, hidden), down_b)
    down_last = down_blocks[-1][-1]
    hidden = tie("hidden", hidden, (down_a, down_b), down_last)
    down_recv = send_b(down_parts)
    gate = tie("down_w", gate, down_parts, down_last)
    grad_ff, mlp_own, mlp_sent, gate_parts, up_parts = feed_back(
        gate, up_value, hidden, normed_two, grad_out_low, down_blocks
    )
    gate_recv = send_b(tie("gate_b", gate_parts, down_recv))
    up_parts = tie("up_b", up_parts, gate_recv, down_recv)
    up_recv = send_b(up_parts)
    down_row = add_b(down_parts, down_recv)
    down_recv_a = send_a(down_row)
    normed_part, sent = norm_back(tie("normed_part", grad_ff, gate_parts, down_recv), ff_w)
    received = swap(sent)
    grad_resid, grad_attended, out_rows, gain_two_part = resid_back(
        normed_part,
        received,
        resid,
        cotangents,
        factors,
        gain_two[None],
        attended_flat,
        attn_w,
        first,
    )
    gain_two_part = gain_two_part[0]

    grad_attended = grad_attended.reshape(2, local, query_width)
    down_own = add_a(tie("down_a", down_row, grad_attended), down_recv_a)
    down_recv_z = send_down_z(tie("down_back_z", down_own, grad_attended))
    gate_row = add_b(tie("gate_row", gate_parts, grad_attended), gate_recv)
    gate_recv_a = send_a(gate_row)
    gate_own = add_a(gate_row, gate_recv_a)
    grad_attended = tie(
        "back_0",
        grad_attended,
        down_recv,
        gate_recv,
        down_recv_a,
        out_rows,
        down_row,
        down_own,
        up_recv,
        gate_row,
        gate_own,
    )
    query_0, lat_0, up_0 = attend_back(
        0, queries, grad_attended, attended, keys, values, probs, lats, key_up, value_up, None
    )
    up_row = add_b(up_parts, up_recv)
    up_recv_a = send_a(up_row)
    up_own = add_a(up_row, up_recv_a)
    grad_attended = tie(
        "back_1",
        grad_attended,
        query_0,
        down_recv_a,
        up_recv,
        down_recv_z,
        up_row,
        down_own,
        gate_own,
        up_own,
    )
    query_1, lat_1, kv_grads = attend_back(
        1, queries, grad_attended, attended, keys, values, probs, lats, key_up, value_up, up_0
    )
    gate_recv_z = send_z(tie("gate_z", gate_own, grad_attended))
    lat_1 = tie("lat_back", list(lat_1), gate_own, up_row, up_recv_a, down_recv_z, gate_recv_z)
    lat_sum = jnp.concatenate([lat_0[0], lat_1[0]], axis=0).astype(F32)
    lat_recv = []
    for k in range(1, nz):
        sent = jnp.concatenate([lat_0[k], lat_1[k]], axis=0)
        lat_recv.append(lax.ppermute(sent, "z", [(i, i - k) for i in range(k, nz)]))
    kv_flat = kv_grads.reshape(depth, -1).astype(BF16)
    kv_parts = split_blocks(tie("kv", kv_flat, up_recv, lat_1), nz, True)
    kv_row = add_b(kv_parts, send_b(kv_parts))
    kv_row = tie("kv_a", kv_row, lat_recv)
    kv_own = add_a(kv_row, send_a(kv_row))
    grad_queries = jnp.concatenate([query_0[0], query_1[0]], axis=0)
    kv_z = tie("kv_z", kv_own, lat_recv, gate_recv_z)
    kv_recv = spread_ring(kv_z)[1:] if OPT.get("ring_kv", 0) else spread_z(kv_z)[1:]
    query_rows = dot(normed_one, tie("query_back", grad_queries, up_recv_a, lat_1, up_own), ROWS)
    normed_query = dot(tie("normed_query", grad_queries, lat_1), query_w, COLS)
    for part in lat_recv:
        lat_sum = lat_sum + part.astype(F32)
    grad_latent = tie("grad_latent", lat_sum.astype(BF16), query_rows, normed_query, kv_row, kv_own)
    grad_latent = grad_latent.reshape(2 * local, latent_width)
    last_rows = dot(normed_one, grad_latent, ROWS)
    attn_rows = [query_rows.astype(BF16), last_rows.astype(BF16), out_rows]
    attn_parts = list(split_blocks(jnp.concatenate(attn_rows, axis=1), nz))
    attn_recv = send_b(tie("attn_back", attn_parts, kv_row, kv_own))
    attn_row = add_b(attn_parts, attn_recv)
    attn_recv_a = send_a(attn_row)
    attn_own = add_a(attn_row, attn_recv_a)
    up_recv_z = send_z(
        tie("ff_back_z", up_own, lat_recv, gate_recv_z, kv_row, attn_recv, attn_recv_a, kv_recv)
    )
    attn_recv_z = send_z(tie("attn_back_z", attn_own, up_recv_z, kv_recv))
    normed_part = normed_query + dot(tie("normed_last", grad_latent, attn_parts), latent_w, COLS)
    gain_one_part = jnp.sum(normed_part * inputs * inv_one, axis=0)
    gains = jnp.stack([gain_one_part, gain_two_part])
    gains = tie("gains", gains, attn_parts, attn_recv, attn_recv_a, up_recv_z, kv_recv)
    gains = all_sum(gains, ("core", "x", "y", "z"))
    grad_normed = normed_part[:local] + swap(normed_part[local:].astype(BF16)).astype(F32)
    input_grad = (
        grad_resid + rms_back(grad_normed, inputs[:local], inv_one[:local], gain_one)
    ).astype(BF16)[None]
    mlp_sent = tie("mlp", mlp_sent, gate_parts, grad_attended, attn_parts)
    result = (resid[:local] + mlp_own + swap(mlp_sent).astype(F32)).astype(BF16)[None]
    kv_sum = kv_z.astype(F32)
    for part in tie("kv_sum", kv_recv, attn_parts, attn_recv, attn_recv_a):
        kv_sum = kv_sum + part.astype(F32)
    kv_sum = tie("kv_spread", kv_sum.astype(BF16), attn_parts, attn_recv, attn_recv_a)
    kv_a, kv_b = spread_own(kv_sum)
    kv_all = merge_blocks(spread_rest(kv_sum, kv_a, kv_b), fixed=True)
    kv_pair = in_order(core, kv_all[None], swap(kv_all)[None], 0).astype(F32)
    kv_pair = kv_pair.reshape((2,) + kv_grads.shape).transpose(1, 0, 3, 2, 4)
    kv_pair = kv_pair.reshape(2, KV_GROUPS, LATENT, query_width)

    def owned(totals):
        joined = jnp.concatenate(totals, axis=1).astype(BF16)
        received = swap(half(joined, other, 0))
        mine = half(joined, core, 0)
        results, start = [], 0
        for total in totals:
            width = total.shape[1]
            results.append(
                in_order(core, mine[:, start : start + width], received[:, start : start + width], 1)
                .astype(F32)
            )
            start += width
        return results

    gate_recv_z = tie("gate_last", gate_recv_z, attn_recv, attn_recv_a)
    up_recv_z = tie("up_last", up_recv_z, attn_recv, attn_recv_a)
    owned_gate, owned_up = owned([add_z(gate_own, gate_recv_z), add_z(up_own, up_recv_z)])
    owned_down = own_down(down_own, tie("down_last", down_recv_z, attn_recv, lat_recv, attn_recv_a))
    attn_total = add_z(attn_own, attn_recv_z)
    first = query_width + latent_width
    owned_query, owned_latent, owned_out = owned(
        [attn_total[:, :query_width], attn_total[:, query_width:first], attn_total[:, first:]]
    )
    return (
        result,
        input_grad,
        gains[0],
        owned_query,
        owned_latent,
        kv_pair[0],
        kv_pair[1],
        owned_out.T,
        gains[1],
        owned_gate,
        owned_up,
        owned_down,
    )


def solution(mesh):
    nz = mesh.shape["seq"]
    chips = mesh.shape["batch"] // 2
    nx = math.isqrt(chips)
    while chips % nx:
        nx -= 1
    fine = Mesh(mesh.devices.reshape(nz, chips // nx, nx, 2), ("z", "y", "x", "core"))
    batch = ("y", "x", "core")
    every = ("z",) + batch
    by_rows = P(every, None)
    in_specs = (
        P(batch, "z", None),
        P(batch, "z", None),
        P(batch),
        P(),
        P(),
        by_rows,
        by_rows,
        P(),
        P(),
        P(None, every),
        P(),
        by_rows,
        by_rows,
        by_rows,
    )
    out_specs = (
        P(batch, "z", None),
        P(batch, "z", None),
        P(),
        by_rows,
        by_rows,
        P(),
        P(),
        P(None, every),
        P(),
        by_rows,
        by_rows,
        by_rows,
    )
    return jax.shard_map(
        on_device, mesh=fine, in_specs=in_specs, out_specs=out_specs, check_vma=False
    )
```
